256 devices in a mesh: dp: 16 (over x_lo, z), mp: 16 (over x_hi, y, core).
Axes of the slice: x: 4 (x_hi: 2, x_lo: 2; x = x_hi * 2 + x_lo), y: 4, z: 8, core: 2. Of those that a mesh axis runs over, the one named last changes fastest.
Arguments:
- tokens: bfloat16 [6144, 1536], P('dp', 'mp'), may hold values from -6 to 6
- ln_gain: float32 [1536], replicated, may hold values from 0.25 to 1.75
- w_in: bfloat16 [1536, 6144], P(None, 'mp'), may hold values from -0.15625 to 0.15625
- w_out: bfloat16 [6144, 1536], P('mp'), may hold values from -0.078125 to 0.078125
- adapt_in: bfloat16 [3, 1536, 1536], P(None, None, 'mp'), may hold values from -0.15625 to 0.15625
- out_dino: bfloat16 [1536, 1536], P('mp'), may hold values from -0.3125 to 0.3125
- out_siglip: bfloat16 [1536, 1152], P('mp'), may hold values from -0.3125 to 0.3125
- out_sam: bfloat16 [1536, 1280], P('mp'), may hold values from -0.3125 to 0.3125
- teach_dino: bfloat16 [512, 1536], P('dp'), may hold values from -6 to 6
- teach_siglip: bfloat16 [512, 1152], P('dp'), may hold values from -6 to 6
- teach_sam: bfloat16 [512, 1280], P('dp'), may hold values from -6 to 6
- src_dev: int32 [6144, 1], P(('dp', 'mp')), may hold values from 0 to 15; in each aligned block of 24 rows (0 to 23, 24 to 47, ...) at most 3 rows name the same one
- src_row: int32 [6144, 3], P(('dp', 'mp')), may hold values from 0 to 31
Outputs:
- grad_tokens: float32 [6144, 1536], P('dp', 'mp')
- grad_w_in: float32 [1536, 6144], P('dp', 'mp')
- grad_w_out: float32 [6144, 1536], P('mp', 'dp')
- grad_adapt_in: float32 [3, 1536, 1536], P(None, 'dp', 'mp')
- grad_out_dino: float32 [1536, 1536], P('mp', 'dp')
- grad_out_siglip: float32 [1536, 1152], P('mp', 'dp')
- grad_out_sam: float32 [1536, 1280], P('mp', 'dp')
The draws below stay inside these ranges and needn't reach their ends.
Inputs may be any that keep to these rules, and one draw needn't show every extreme that they name: `src_dev`: in each aligned block of 24 rows (the rows of one device) at most 3 rows name one teacher group; some block reaches 3.
All inputs are finite; a program needn't handle non-finite values.
Results may differ from the reference program's by a relative error of at most 0.02.
Values may be sent and summed in bfloat16 or wider, within the bound.
No kernel may reach another device: no remote copies, remote signals or barrier semaphores. Data moves between devices by JAX's collectives and lax.ppermute only.
A program may use at most 64 MiB of HBM per device.

```python
import math
import jax
import jax.numpy as jnp
import numpy as np
from jax import lax

D = 1536
FF = 6144
HID = 1536
C_DINO = 1536
C_SIGLIP = 1152
C_SAM = 1280
TROW_DEV = 32
TOKENS = 6144
ROWS_DEV = 24
CAP = 3
N_DP = 16


def plant(drawn, rng, low, top_value):
    longest = drawn.shape.index(max(drawn.shape))
    spots = []
    for shift in (0, 1):
        where = [jax.random.randint(jax.random.fold_in(rng, axis), (), 0, length) for axis, length in enumerate(drawn.shape)]
        where[longest] = (where[longest] + shift) % drawn.shape[longest]
        spots.append(tuple(where))
    return drawn.at[spots[0]].set(low).at[spots[1]].set(top_value)


def spiked(array, key, source, target, parts, factor):
    def block_of(position):
        return (jnp.arange(array.shape[position]) // (array.shape[position] // parts)).reshape((-1,) + (1,) * (array.ndim - 1 - position))

    first = jax.random.permutation(key, parts)[block_of(target)]
    far = (block_of(target) + parts // 2) % parts
    return jnp.where((block_of(source) == first) | (block_of(source) == far), factor * array, array)


def block_levels(rng, dims, cuts, low, high):
    def one(position, blocks):
        heights = jax.random.uniform(jax.random.fold_in(jax.random.fold_in(rng, 6), position), (blocks,), jnp.float32, low / len(cuts), high / len(cuts))
        return jnp.repeat(jnp.exp(heights), dims[position] // blocks).reshape((-1,) + (1,) * (len(dims) - position - 1))

    level = one(*cuts[0])
    for cut in cuts[1:]:
        level = level * one(*cut)
    return level


def deal_out(stream_key, own, number, rows, amount, top, bound, lean):
    sequence = jax.random.permutation(stream_key, amount)
    crowded, ordinary = portions_of(amount, rows * top, bound, lean, True), portions_of(amount, rows * top, bound, lean, False)
    places = jnp.arange(amount)

    def named(sizes, turn):
        used = int((sizes > 0).sum())
        fixed = max(1, used // 4)
        passed = fixed + (places - fixed + turn * (used - fixed)) % max(1, amount - fixed)
        return jnp.zeros((amount,), jnp.int32).at[sequence[jnp.where(places < fixed, places, passed)]].set(jnp.asarray(sizes, jnp.int32))

    sizes = jnp.where(number % 4 == 0, named(crowded, number // 4), named(ordinary, number - number // 4 - 1))
    mixed = jax.random.permutation(jax.random.fold_in(own, 3), amount)
    giver, sink = mixed[0:amount // 2 * 2:2], mixed[1:amount // 2 * 2:2]
    room = jnp.minimum(sizes[giver] - 1, bound - sizes[sink]) // 2
    room = jnp.where((giver == sequence[0]) | (sink == sequence[0]) | (sizes[sink] == 0), 0, jnp.maximum(room, 0))
    passed = jax.random.randint(jax.random.fold_in(own, 4), (amount // 2,), 0, 1 << 20) % (room + 1)
    sizes = sizes.at[giver].add(-passed).at[sink].add(passed)
    items = jnp.searchsorted(jnp.cumsum(sizes), jnp.arange(rows * top), side="right").astype(jnp.int32)
    table = items.reshape(top, rows).T
    table = table[jax.random.permutation(jax.random.fold_in(own, 1), rows)]
    turn = jax.random.randint(jax.random.fold_in(own, 2), (rows, 1), 0, top)
    return jnp.take_along_axis(table, (jnp.arange(top)[None, :] + turn) % top, axis=1)


def portions_of(count, total, most, slope, full):
    loads = [(1 << 20) // math.isqrt(grade ** slope) + 1 for grade in range(1, count + 1)]
    largest = most if full else min(most, max(-(-total // count), total * loads[0] // sum(loads)))
    least = 1 if total - largest >= count - 1 else 0
    given, spare = [largest] + [least] * (count - 1), total - largest - least * (count - 1)
    while spare > 0:
        movable = [i for i in range(1, count) if given[i] < largest] or [i for i in range(1, count) if given[i] < most]
        pool, remaining = sum([loads[i] for i in movable]), spare
        for i in movable:
            addition = min(most - given[i], max(1, remaining * loads[i] // pool), spare)
            given[i] = given[i] + addition
            spare = spare - addition
    return np.array(given)


def noise(own_key, extent, scale, most, split=(), kind=jnp.bfloat16):
    drawn = jax.random.normal(own_key, extent, jnp.float32) * scale
    if len(split) > 0:
        drawn = block_levels(own_key, extent, split, -0.22, 0.18) * drawn
    return jnp.clip(drawn, min=-most, max=most).astype(kind)


def noise_with(stream_key, shape, deviation, most, cuts, heavy, held_as=jnp.bfloat16):
    array = deviation * jax.random.normal(stream_key, shape, jnp.float32)
    if cuts:
        array = array * block_levels(stream_key, shape, cuts, -0.22, 0.18)
    return jnp.clip(spiked(array, jax.random.fold_in(stream_key, 3), *heavy), -most, most).astype(held_as)


def setup_inputs(seed: int = 0) -> dict:
    arg_keys = jax.random.split(jax.random.key(seed), 14)
    tokens = noise_with(arg_keys[0], (TOKENS, D), 1.0, 6.0, ((0, 16), (1, 16)), (0, 1, 16, 2.0))
    ln_gain = jnp.clip(1.0 + 0.15 * jax.random.normal(arg_keys[1], (D,), jnp.float32), 0.25, 1.75)
    w_in = noise(arg_keys[2], (D, FF), D ** -0.5, 0.15625, ((1, 16),))
    w_out = noise(arg_keys[3], (FF, D), FF ** -0.5, 0.078125, ((0, 16),))
    adapt_in = noise(arg_keys[4], (3, D, HID), D ** -0.5, 0.15625, ((2, 16),))
    out_dino = noise(arg_keys[5], (HID, C_DINO), (HID // 4) ** -0.5, 0.3125, ((0, 16),))
    out_siglip = noise(arg_keys[6], (HID, C_SIGLIP), (HID // 4) ** -0.5, 0.3125, ((0, 16),))
    out_sam = noise(arg_keys[7], (HID, C_SAM), (HID // 4) ** -0.5, 0.3125, ((0, 16),))
    teach_dino = noise(arg_keys[8], (N_DP * TROW_DEV, C_DINO), 1.0, 6.0, ((0, 16),))
    teach_siglip = noise(arg_keys[9], (N_DP * TROW_DEV, C_SIGLIP), 1.0, 6.0, ((0, 16),))
    teach_sam = noise(arg_keys[10], (N_DP * TROW_DEV, C_SAM), 1.0, 6.0, ((0, 16),))
    src_dev_keys = jax.random.split(jax.random.fold_in(arg_keys[11], 1), TOKENS // ROWS_DEV)
    src_dev_turns = jax.random.permutation(jax.random.fold_in(arg_keys[11], 3), TOKENS // ROWS_DEV)
    src_dev = jax.vmap(lambda own, number: deal_out(jax.random.fold_in(arg_keys[11], 2), own, number, ROWS_DEV, N_DP, 1, CAP, 2))(src_dev_keys, src_dev_turns).reshape((TOKENS, 1))
    src_row = plant(jax.random.randint(arg_keys[12], (TOKENS, 3), 0, TROW_DEV), jax.random.fold_in(arg_keys[12], 1), 0, TROW_DEV - 1).astype(jnp.int32)
    return {"tokens": tokens, "ln_gain": ln_gain, "w_in": w_in, "w_out": w_out, "adapt_in": adapt_in, "out_dino": out_dino, "out_siglip": out_siglip, "out_sam": out_sam, "teach_dino": teach_dino, "teach_siglip": teach_siglip, "teach_sam": teach_sam, "src_dev": src_dev, "src_row": src_row}


def gelu(value):
    return 0.5 * value * (1.0 + jax.scipy.special.erf(value * 0.7071067811865476))

def gelu_slope(value):
    return 0.5 * (1.0 + jax.scipy.special.erf(value * 0.7071067811865476)) + value * jnp.exp(-0.5 * value * value) * 0.3989422804014327

def reference(tokens, ln_gain, w_in, w_out, adapt_in, out_dino, out_siglip, out_sam, teach_dino, teach_siglip, teach_sam, src_dev, src_row):
    scale = 1.0 / math.sqrt(TOKENS)
    x_float = tokens.astype(jnp.float32)
    row_mean = lax.optimization_barrier(jnp.mean(x_float, axis=1, keepdims=True))
    centred = x_float - row_mean
    inv_std = 1.0 / jnp.sqrt(lax.optimization_barrier(jnp.mean(centred * centred, axis=1, keepdims=True)) + 1e-06)
    normed = centred * inv_std
    z_rows = (normed * ln_gain).astype(jnp.bfloat16)
    pre_mlp = jnp.dot(z_rows, w_in, preferred_element_type=jnp.float32)
    act = gelu(pre_mlp).astype(jnp.bfloat16)
    hstate = (x_float + jnp.dot(act, w_out, preferred_element_type=jnp.float32)).astype(jnp.bfloat16)
    heads = (out_dino, out_siglip, out_sam)
    teachers = (teach_dino, teach_siglip, teach_sam)
    dstate = jnp.zeros(x_float.shape, jnp.float32)
    grads_out = []
    grads_in = []
    for which in range(3):
        pre_k = jnp.dot(hstate, adapt_in[which], preferred_element_type=jnp.float32)
        q_rows = gelu(pre_k).astype(jnp.bfloat16)
        pred = jnp.dot(q_rows, heads[which], preferred_element_type=jnp.float32)
        glob = (src_dev[:, 0] * TROW_DEV + src_row[:, which]).astype(jnp.int32)
        target = teachers[which][glob].astype(jnp.float32)
        error = (pred - target).astype(jnp.bfloat16)
        grads_out.append(jnp.dot(q_rows.T, error, preferred_element_type=jnp.float32) * scale)
        back = (jnp.dot(error, heads[which].T, preferred_element_type=jnp.float32) * gelu_slope(pre_k)).astype(jnp.bfloat16)
        grads_in.append(jnp.dot(hstate.T, back, preferred_element_type=jnp.float32) * scale)
        dstate = dstate + jnp.dot(back, adapt_in[which].T, preferred_element_type=jnp.float32)
    dstate_b = dstate.astype(jnp.bfloat16)
    grad_w_out = jnp.dot(act.T, dstate_b, preferred_element_type=jnp.float32) * scale
    dpre = (jnp.dot(dstate_b, w_out.T, preferred_element_type=jnp.float32) * gelu_slope(pre_mlp)).astype(jnp.bfloat16)
    grad_w_in = jnp.dot(z_rows.T, dpre, preferred_element_type=jnp.float32) * scale
    dnorm = jnp.dot(dpre, w_in.T, preferred_element_type=jnp.float32) * ln_gain
    first = lax.optimization_barrier(jnp.mean(dnorm, axis=1, keepdims=True))
    second = lax.optimization_barrier(jnp.mean(dnorm * normed, axis=1, keepdims=True))
    grad_tokens = dstate + inv_std * (dnorm - first - normed * second)
    return (grad_tokens, grad_w_in, grad_w_out, jnp.stack(grads_in), grads_out[0], grads_out[1], grads_out[2])
```

```python
import math

import jax
import jax.numpy as jnp
from jax import lax
from jax.sharding import PartitionSpec as P

F32 = jnp.float32
BF16 = jnp.bfloat16

CORE = [(i, i ^ 1) for i in range(16)]
FAR = [(i, i ^ 8) for i in range(16)]
AROUND_Y = [[(i, (i & 9) | ((((i >> 1 & 3) + k) & 3) << 1)) for i in range(16)] for k in range(4)]
AROUND_Z = [[(i, (i & 8) | ((i + k) & 7)) for i in range(16)] for k in range(8)]


def gelu(value):
    return 0.5 * value * (1.0 + jax.scipy.special.erf(value * 0.7071067811865476))


def gelu_slope(value):
    return (
        0.5 * (1.0 + jax.scipy.special.erf(value * 0.7071067811865476))
        + value * jnp.exp(-0.5 * value * value) * 0.3989422804014327
    )


def dot(left, right, over_left, over_right):
    return lax.dot_general(
        left, right, (((over_left,), (over_right,)), ((), ())), preferred_element_type=F32
    )


def pick(array, index, axis):
    return lax.dynamic_index_in_dim(array, index, axis, keepdims=False)


def put(buffer, piece, *at):
    return lax.dynamic_update_slice(buffer, piece, at + (0,) * (buffer.ndim - len(at)))


def mp_place():
    index = lax.axis_index("mp")
    return index >> 3, (index >> 1) & 3, index & 1


def gather_mp(block):
    x_hi, y, core = mp_place()
    other = lax.ppermute(block, "mp", FAR)
    pair = jnp.zeros((2, *block.shape), block.dtype)
    pair = put(put(pair, block[None], x_hi), other[None], 1 - x_hi)
    held = put(jnp.zeros((2, 4, *block.shape), block.dtype), pair[:, None], 0, y)
    for k in (1, 3, 2):
        held = put(held, lax.ppermute(pair, "mp", AROUND_Y[k])[:, None], 0, (y - k) & 3)
    other = lax.ppermute(held, "mp", CORE)
    full = jnp.zeros((2, 4, 2, *block.shape), block.dtype)
    full = put(put(full, held[:, :, None], 0, 0, core), other[:, :, None], 0, 0, 1 - core)
    return full.reshape(16, *block.shape)


def scatter_mp(blocks):
    x_hi, y, core = mp_place()
    blocks = blocks.reshape(2, 4, 2, *blocks.shape[1:])
    other = lax.ppermute(pick(blocks, 1 - core, 2), "mp", CORE)
    held = (pick(blocks, core, 2).astype(F32) + other.astype(F32)).astype(BF16)
    arrived = [lax.ppermute(pick(held, (y + k) & 3, 1), "mp", AROUND_Y[k]) for k in (1, 3, 2)]
    total = pick(held, y, 1).astype(F32)
    for piece in arrived:
        total = total + piece.astype(F32)
    other = lax.ppermute(pick(total.astype(BF16), 1 - x_hi, 0), "mp", FAR)
    return pick(total, x_hi, 0) + other.astype(F32)


def scatter_dp(blocks):
    index = lax.axis_index("dp")
    x_lo, z = index >> 3, index & 7
    blocks = blocks.reshape(2, 8, *blocks.shape[1:])
    other = lax.ppermute(pick(blocks, 1 - x_lo, 0), "dp", FAR)
    held = (pick(blocks, x_lo, 0).astype(F32) + other.astype(F32)).astype(BF16)
    arrived = [
        lax.ppermute(pick(held, (z + k) & 7, 0), "dp", AROUND_Z[k]) for k in (4, 3, 5, 2, 6, 1, 7)
    ]
    total = pick(held, z, 0).astype(F32)
    for piece in arrived:
        total = total + piece.astype(F32)
    return total


def body(
    tokens,
    ln_gain,
    w_in,
    w_out,
    adapt_in,
    out_dino,
    out_siglip,
    out_sam,
    teach_dino,
    teach_siglip,
    teach_sam,
    src_dev,
    src_row,
):
    heads = (out_dino, out_siglip, out_sam)
    widths = [head.shape[1] for head in heads]
    n_rows, width_dev = tokens.shape
    n_mp = lax.axis_size("mp")
    n_dp = lax.axis_size("dp")
    width = width_dev * n_mp
    hid = adapt_in.shape[2]
    share = n_rows // n_mp
    scale = 1.0 / math.sqrt(n_rows * n_dp)
    mp_index = lax.axis_index("mp")

    with jax.named_scope("targets"):
        teach = jnp.concatenate([teach_dino, teach_siglip, teach_sam], axis=1)
        pool = lax.all_gather(teach, "dp", axis=0, tiled=True)
        spots = src_dev * teach_dino.shape[0] + src_row
        places = jnp.arange(pool.shape[0], dtype=jnp.int32)
        columns = []
        offset = 0
        for which in range(3):
            chosen = (spots[:, which : which + 1] == places[None, :]).astype(BF16)
            columns.append(dot(chosen, pool[:, offset : offset + widths[which]], 1, 0))
            offset = offset + widths[which]
        target = jnp.concatenate(columns, axis=1)

    with jax.named_scope("norm"):
        own = tokens.T
        x = gather_mp(own).reshape(width, n_rows).astype(F32)
        row_mean = jnp.mean(x, axis=0, keepdims=True)
        centred = x - row_mean
        inv_std = 1.0 / jnp.sqrt(jnp.mean(centred * centred, axis=0, keepdims=True) + 1e-06)
        normed = centred * inv_std
        z = (normed * ln_gain[:, None]).astype(BF16)

    with jax.named_scope("block"):
        pre_mlp = dot(z, w_in, 0, 0)
        act = gelu(pre_mlp).astype(BF16)
        branch = dot(w_out, act, 0, 1).astype(BF16)
        state = scatter_mp(branch.reshape(n_mp, width_dev, n_rows)) + own.astype(F32)
        hstate = gather_mp(state.astype(BF16)).reshape(width, n_rows)

    with jax.named_scope("adaptors"):
        adapt = jnp.concatenate([adapt_in[0], adapt_in[1], adapt_in[2]], axis=1)
        pre_adapt = dot(adapt, hstate, 0, 0)
        q = gelu(pre_adapt).astype(BF16)
        pred = jnp.concatenate(
            [dot(q[k * hid : (k + 1) * hid], heads[k], 0, 0).astype(BF16) for k in range(3)], axis=1
        )
        error = (scatter_mp(pred.reshape(n_mp, share, sum(widths))) - target).astype(BF16)
        error = gather_mp(error).reshape(n_rows, sum(widths))

    with jax.named_scope("adaptors_back"):
        parts = []
        grads = []
        offset = 0
        for k in range(3):
            cols = error[:, offset : offset + widths[k]]
            parts.append(dot(heads[k], cols, 1, 1))
            grads.append((dot(cols, q[k * hid : (k + 1) * hid], 0, 1) * scale).astype(BF16))
            offset = offset + widths[k]
        back = (jnp.concatenate(parts, axis=0) * gelu_slope(pre_adapt)).astype(BF16)
        dstate = dot(adapt, back, 1, 0).astype(BF16)
        dstate_own = scatter_mp(dstate.reshape(n_mp, width_dev, n_rows))
        dstate_b = gather_mp(dstate_own.astype(BF16)).reshape(width, n_rows)

    with jax.named_scope("adaptor_grads"):
        grad_adapt = (dot(hstate, back, 1, 1) * scale).astype(BF16)
        first_rows = jnp.concatenate([grad_adapt, grads[0]], axis=1).reshape(n_dp, width // n_dp, 4 * hid)
        short = [w // n_dp for w in widths]
        tall = max(short[1], short[2])
        rest = [
            jnp.pad(
                grads[k].reshape(n_dp, short[k], hid), ((0, 0), (0, tall - short[k]), (0, 0))
            )
            for k in (1, 2)
        ]
        rest = jnp.pad(jnp.concatenate(rest, axis=2), ((0, 0), (0, 0), (0, 2 * hid)))
        pack = jnp.concatenate([first_rows, rest], axis=1)
        pack = lax.psum_scatter(
            pack.reshape(-1, 4 * hid), "dp", scatter_dimension=0, tiled=True
        ).astype(F32)

    with jax.named_scope("block_back"):
        dpre = (dot(dstate_b, w_out, 0, 1) * gelu_slope(pre_mlp)).astype(BF16)
        dnorm = dot(w_in, dpre, 1, 1)
        lifted = dnorm * ln_gain[:, None]
        means = []
        for part in (
            jnp.mean(lifted, axis=0, keepdims=True),
            jnp.mean(lifted * normed, axis=0, keepdims=True),
        ):
            high = part.astype(BF16)
            means = means + [high, (part - high.astype(F32)).astype(BF16)]
        means = jnp.concatenate(means + [jnp.zeros((4, n_rows), BF16)], axis=0)
        sent = jnp.concatenate(
            [
                dnorm.astype(BF16).reshape(n_mp, width_dev, n_rows),
                jnp.broadcast_to(means[None], (n_mp, 8, n_rows)),
            ],
            axis=1,
        )
        summed = scatter_mp(sent)
        gain_own = lax.dynamic_slice_in_dim(ln_gain, mp_index * width_dev, width_dev, 0)
        normed_own = (own.astype(F32) - row_mean) * inv_std
        dnorm_own = summed[:width_dev] * gain_own[:, None]
        first = summed[width_dev : width_dev + 1] + summed[width_dev + 1 : width_dev + 2]
        second = summed[width_dev + 2 : width_dev + 3] + summed[width_dev + 3 : width_dev + 4]
        grad_tokens = dstate_own + inv_std * (dnorm_own - first - normed_own * second)

    with jax.named_scope("block_grads"):
        grad_w_out = (dot(dstate_b, act, 1, 0) * scale).astype(BF16)
        grad_w_out = scatter_dp(grad_w_out.reshape(n_dp, width // n_dp, -1))
        grad_w_in = (dot(z, dpre, 1, 0) * scale).astype(BF16)
        grad_w_in = scatter_dp(grad_w_in.reshape(n_dp, width // n_dp, -1))

    lead = width // n_dp
    return (
        grad_tokens.T,
        grad_w_in,
        grad_w_out.T,
        jnp.stack([pack[:lead, k * hid : (k + 1) * hid] for k in range(3)]),
        pack[:lead, 3 * hid :].T,
        pack[lead : lead + short[1], :hid].T,
        pack[lead : lead + short[2], hid : 2 * hid].T,
    )


def solution(mesh):
    placed = (
        P("dp", "mp"),
        P(),
        P(None, "mp"),
        P("mp", None),
        P(None, None, "mp"),
        P("mp", None),
        P("mp", None),
        P("mp", None),
        P("dp", None),
        P("dp", None),
        P("dp", None),
        P(("dp", "mp"), None),
        P(("dp", "mp"), None),
    )
    return jax.shard_map(
        body,
        mesh=mesh,
        in_specs=placed,
        out_specs=(
            P("dp", "mp"),
            P("dp", "mp"),
            P("mp", "dp"),
            P(None, "dp", "mp"),
            P("mp", "dp"),
            P("mp", "dp"),
            P("mp", "dp"),
        ),
        check_vma=False,
    )
```

```python
import functools
import math

import jax
import jax.numpy as jnp
from jax import lax
from jax.experimental import pallas as pl
from jax.experimental.pallas import tpu as pltpu
from jax.sharding import PartitionSpec as P

F32 = jnp.float32
BF16 = jnp.bfloat16
VMEM_LIMIT = 28 * 1024 * 1024

CORE = [(i, i ^ 1) for i in range(16)]
FAR = [(i, i ^ 8) for i in range(16)]
AROUND_Y = [[(i, (i & 9) | ((((i >> 1 & 3) + k) & 3) << 1)) for i in range(16)] for k in range(4)]
AROUND_Z = [[(i, (i & 8) | ((i + k) & 7)) for i in range(16)] for k in range(8)]
TWICE_Z = [[(i, i ^ k) for i in range(16)] for k in (1, 2, 4, 8)]

BLOCK = 96
TEACH = 256
EXTRA = 8
SUMS = 16
LOW = 48


def gelu(value):
    return 0.5 * value * (1.0 + lax.erf(value * 0.7071067811865476))


def gelu_slope(value):
    return (
        0.5 * (1.0 + lax.erf(value * 0.7071067811865476))
        + value * jnp.exp(-0.5 * value * value) * 0.3989422804014327
    )


def dot(left, right, over_left=1, over_right=0):
    return lax.dot_general(
        left, right, (((over_left,), (over_right,)), ((), ())), preferred_element_type=F32
    )


def pick(array, index, axis):
    return lax.dynamic_index_in_dim(array, index, axis, keepdims=False)


def put(buffer, piece, *at):
    return lax.dynamic_update_slice(buffer, piece, at + (0,) * (buffer.ndim - len(at)))


def mp_place():
    index = lax.axis_index("mp")
    return index >> 3, (index >> 1) & 3, index & 1


def pair_up(block):
    x_hi = mp_place()[0]
    other = lax.ppermute(block, "mp", FAR)
    pair = jnp.zeros((2, *block.shape), block.dtype)
    return put(put(pair, block[None], x_hi), other[None], 1 - x_hi)


def spread(pair):
    y = mp_place()[1]
    held = put(jnp.zeros((2, 4, *pair.shape[1:]), pair.dtype), pair[:, None], 0, y)
    for k in (1, 3, 2):
        held = put(held, lax.ppermute(pair, "mp", AROUND_Y[k])[:, None], 0, (y - k) & 3)
    held = held.reshape(8, *pair.shape[1:])
    return held, lax.ppermute(held, "mp", CORE)


def collect(mine, theirs):
    y = mp_place()[1]
    other = lax.ppermute(theirs, "mp", CORE)
    held = (mine.astype(F32) + other.astype(F32)).astype(BF16).reshape(2, 4, *mine.shape[1:])
    arrived = [lax.ppermute(pick(held, (y + k) & 3, 1), "mp", AROUND_Y[k]) for k in (1, 3, 2)]
    total = pick(held, y, 1).astype(F32)
    for piece in arrived:
        total = total + piece.astype(F32)
    return total


def sum_pair(total):
    rounded = total.astype(BF16)
    return rounded.astype(F32) + lax.ppermute(rounded, "mp", FAR).astype(F32)


def sum_own(total):
    x_hi = mp_place()[0]
    other = lax.ppermute(pick(total, 1 - x_hi, 0).astype(BF16), "mp", FAR)
    return pick(total, x_hi, 0) + other.astype(F32)


def scatter_dp(mine, theirs):
    z = lax.axis_index("dp") & 7
    other = lax.ppermute(theirs, "dp", FAR)
    held = (mine.astype(F32) + other.astype(F32)).astype(BF16)
    arrived = [
        lax.ppermute(pick(held, (z + k) & 7, 0), "dp", AROUND_Z[k]) for k in (4, 3, 5, 2, 6, 1, 7)
    ]
    total = pick(held, z, 0).astype(F32)
    for piece in arrived:
        total = total + piece.astype(F32)
    return total


def gather_dp(block):
    index = lax.axis_index("dp")
    x_lo, z = index >> 3, index & 7
    held = block[None]
    for bit in (2, 1, 0):
        other = lax.ppermute(held, "dp", TWICE_Z[bit])
        on = ((z >> bit) & 1) == 1
        held = jnp.stack([jnp.where(on, other, held), jnp.where(on, held, other)], axis=held.ndim - 2)
    other = lax.ppermute(held, "dp", FAR)
    on = x_lo == 1
    held = jnp.stack([jnp.where(on, other, held), jnp.where(on, held, other)])
    return held.reshape(16, *block.shape)


def rows(start, size):
    return pl.ds(pl.multiple_of(start, 16), size)


def place(core, i, own, size):
    return rows((2 * i + (core if own else 1 - core)) * size, size)


def call(kernel, outs, *args, scratch=()):
    spec = pl.BlockSpec(memory_space=pltpu.VMEM)
    return pl.pallas_call(
        kernel,
        out_shape=tuple(jax.ShapeDtypeStruct(shape, dtype) for shape, dtype in outs),
        in_specs=[pl.BlockSpec(memory_space=pltpu.SMEM)] + [spec] * (len(args) - 1),
        out_specs=(spec,) * len(outs),
        scratch_shapes=list(scratch),
        compiler_params=pltpu.CompilerParams(vmem_limit_bytes=VMEM_LIMIT),
    )(*args)


def send_out(core, full_ref, mine_ref, theirs_ref, size):
    for i in range(8):
        mine_ref[i] = full_ref[place(core, i, True, size)].astype(BF16)
        theirs_ref[i] = full_ref[place(core, i, False, size)].astype(BF16)


def take_in(core, held_ref, other_ref, full_ref, size):
    for i in range(8):
        full_ref[place(core, i, True, size)] = held_ref[i]
        full_ref[place(core, i, False, size)] = other_ref[i]


def block_kernel(core_ref, held_ref, other_ref, gain_ref, w_in_t_ref, w_out_t_ref,
                 z_ref, pre_ref, act_ref, stat_ref, mine_ref, theirs_ref, full_ref):
    core = core_ref[0]
    width = z_ref.shape[0]
    total = jnp.zeros((1, z_ref.shape[1]), F32)
    for i in range(8):
        for ref in (held_ref, other_ref):
            total = total + jnp.sum(ref[i, :BLOCK].astype(F32), axis=0, keepdims=True)
    mean = total / width
    total = jnp.zeros_like(mean)
    for i in range(8):
        for ref in (held_ref, other_ref):
            centred = ref[i, :BLOCK].astype(F32) - mean
            total = total + jnp.sum(centred * centred, axis=0, keepdims=True)
    inv_std = 1.0 / jnp.sqrt(total / width + 1e-06)
    stat_ref[...] = jnp.zeros_like(stat_ref)
    stat_ref[0:1] = mean
    stat_ref[1:2] = inv_std
    for i in range(8):
        for own, ref in ((True, held_ref), (False, other_ref)):
            at = place(core, i, own, BLOCK)
            normed = (ref[i, :BLOCK].astype(F32) - mean) * inv_std
            z_ref[at] = (normed * gain_ref[at]).astype(BF16)
    pre = dot(w_in_t_ref[...], z_ref[...])
    pre_ref[...] = pre
    act_ref[...] = gelu(pre).astype(BF16)
    full_ref[...] = dot(w_out_t_ref[...], act_ref[...])
    send_out(core, full_ref, mine_ref, theirs_ref, BLOCK)


def adaptor_kernel(core_ref, held_ref, other_ref, adapt_t_ref, heads_t_ref,
                   h_ref, pre_ref, q_ref, mine_ref, theirs_ref):
    core = core_ref[0]
    take_in(core, held_ref, other_ref, h_ref, BLOCK)
    pre = dot(adapt_t_ref[...], h_ref[...])
    pre_ref[...] = pre
    q_ref[...] = gelu(pre).astype(BF16)
    for i in range(8):
        mine_ref[i] = dot(heads_t_ref[place(core, i, True, TEACH)], q_ref[...]).astype(BF16)
        theirs_ref[i] = dot(heads_t_ref[place(core, i, False, TEACH)], q_ref[...]).astype(BF16)


def adaptor_back_kernel(core_ref, held_ref, other_ref, heads_ref, pre_ref, adapt_ref,
                        err_ref, back_ref, mine_ref, theirs_ref, full_ref):
    core = core_ref[0]
    take_in(core, held_ref, other_ref, err_ref, TEACH)
    lifted = dot(heads_ref[...], err_ref[...])
    back_ref[...] = (lifted * gelu_slope(pre_ref[...])).astype(BF16)
    full_ref[...] = dot(adapt_ref[...], back_ref[...])
    send_out(core, full_ref, mine_ref, theirs_ref, BLOCK)


def adaptor_grads_kernel(scale, widths, half_ref, err_ref, q_ref, h_ref, back_ref,
                         mine_ref, theirs_ref, ga_ref, go_ref):
    half = half_ref[0]
    hid3 = q_ref.shape[0]
    hid = hid3 // 3
    ga_ref[...] = dot(h_ref[...], back_ref[...], 1, 1) * scale
    go_ref[...] = dot(err_ref[...], q_ref[...], 1, 1) * scale
    w0, w1, w2 = widths
    for j in range(8):
        for side, ref in ((half, mine_ref), (1 - half, theirs_ref)):
            chunk = side * 8 + j
            at = rows(chunk * BLOCK, BLOCK)
            go = go_ref[rows(chunk * TEACH, TEACH)]
            ref[j, :BLOCK] = jnp.concatenate(
                [ga_ref[at], go[:BLOCK, :hid]], axis=1
            ).astype(BF16)
            second = go[w0 : w0 + w1, hid : 2 * hid]
            third = go[w0 + w1 : w0 + w1 + w2, 2 * hid :]
            second = jnp.concatenate([second, jnp.zeros((2 * LOW - w1, hid), F32)], axis=0)
            third = jnp.concatenate([third, jnp.zeros((2 * LOW - w2, hid), F32)], axis=0)
            ref[j, BLOCK:] = jnp.concatenate(
                [second[:LOW], third[:LOW], second[LOW:], third[LOW:]], axis=1
            ).astype(BF16)


def w_out_grad_kernel(scale, place_ref, held_ref, other_ref, act_ref,
                      ds_ref, mine_ref, theirs_ref, full_ref):
    take_in(place_ref[0], held_ref, other_ref, ds_ref, BLOCK)
    full_ref[...] = dot(ds_ref[...], act_ref[...], 1, 1) * scale
    halves(place_ref[1], full_ref, mine_ref, theirs_ref)


def halves(half, full_ref, mine_ref, theirs_ref):
    for j in range(8):
        mine_ref[j] = full_ref[rows((half * 8 + j) * BLOCK, BLOCK)].astype(BF16)
        theirs_ref[j] = full_ref[rows(((1 - half) * 8 + j) * BLOCK, BLOCK)].astype(BF16)


def w_in_grad_kernel(scale, place_ref, z_ref, dpre_ref, mine_ref, theirs_ref, full_ref):
    full_ref[...] = dot(z_ref[...], dpre_ref[...], 1, 1) * scale
    halves(place_ref[1], full_ref, mine_ref, theirs_ref)


def block_back_kernel(core_ref, ds_ref, w_out_ref, pre_ref, w_in_ref, gain_ref, held_ref, other_ref, stat_ref,
                      dpre_ref, mine_ref, theirs_ref, full_ref):
    core = core_ref[0]
    width = ds_ref.shape[0]
    dpre_ref[...] = (dot(w_out_ref[...], ds_ref[...]) * gelu_slope(pre_ref[...])).astype(BF16)
    full_ref[...] = dot(w_in_ref[...], dpre_ref[...])
    mean = stat_ref[0:1]
    inv_std = stat_ref[1:2]
    first = jnp.zeros_like(mean)
    second = jnp.zeros_like(mean)
    for i in range(8):
        for own, ref, out_ref in ((True, held_ref, mine_ref), (False, other_ref, theirs_ref)):
            at = place(core, i, own, BLOCK)
            dnorm = full_ref[at]
            out_ref[i, :BLOCK] = dnorm.astype(BF16)
            lifted = dnorm * gain_ref[at]
            normed = (ref[i, :BLOCK].astype(F32) - mean) * inv_std
            first = first + jnp.sum(lifted, axis=0, keepdims=True)
            second = second + jnp.sum(lifted * normed, axis=0, keepdims=True)
    sums = []
    for part in (first / width, second / width):
        high = part.astype(BF16).astype(F32)
        sums = sums + [high, part - high]
    sums = jnp.concatenate(sums + [jnp.zeros((SUMS - 4, mean.shape[1]), F32)], axis=0).astype(BF16)
    for i in range(8):
        mine_ref[i, BLOCK:] = sums
        theirs_ref[i, BLOCK:] = sums


def body(
    tokens,
    ln_gain,
    w_in,
    w_out,
    adapt_in,
    out_dino,
    out_siglip,
    out_sam,
    teach_dino,
    teach_siglip,
    teach_sam,
    src_dev,
    src_row,
):
    heads = (out_dino, out_siglip, out_sam)
    teachers = (teach_dino, teach_siglip, teach_sam)
    n_rows = tokens.shape[0]
    n_mp = lax.axis_size("mp")
    n_dp = lax.axis_size("dp")
    width = BLOCK * n_mp
    hidden = w_in.shape[1]
    hid = adapt_in.shape[2]
    share = n_rows // n_mp
    short = [head.shape[1] // n_mp for head in heads]
    spare = TEACH - sum(short)
    scale = 1.0 / math.sqrt(n_rows * n_dp)
    x_hi, y, core = mp_place()
    at = jnp.stack([core, lax.axis_index("dp") >> 3]).astype(jnp.int32)
    half = at[1:]

    with jax.named_scope("weights"):
        w_in_t = w_in.T
        w_out_t = w_out.T
        adapt = jnp.concatenate([adapt_in[0], adapt_in[1], adapt_in[2]], axis=1)
        adapt_t = adapt.T
        heads_t = [
            jnp.pad(heads[k].T.reshape(n_mp, short[k], hid), ((0, 0), (0, 0), (k * hid, (2 - k) * hid)))
            for k in range(3)
        ]
        heads_t = jnp.concatenate(heads_t + [jnp.zeros((n_mp, spare, 3 * hid), BF16)], axis=1)
        heads_t = heads_t.reshape(n_mp * TEACH, 3 * hid)
        heads_all = heads_t.T
        gain = ln_gain[:, None]

    with jax.named_scope("tokens"):
        sources = jnp.concatenate([src_dev, src_row], axis=1).T.astype(BF16)
        sources = jnp.pad(sources, ((0, EXTRA - 4), (0, n_rows - share)))
        token_pair = pair_up(jnp.concatenate([tokens.T, sources], axis=0))
        x_held, x_other = spread(token_pair)

    with jax.named_scope("block"):
        z, pre_mlp, act, stat, mine, theirs = call(
            block_kernel,
            [
                ((width, n_rows), BF16),
                ((hidden, n_rows), F32),
                ((hidden, n_rows), BF16),
                ((8, n_rows), F32),
                ((8, BLOCK, n_rows), BF16),
                ((8, BLOCK, n_rows), BF16),
            ],
            at, x_held, x_other, gain, w_in_t, w_out_t,
            scratch=[pltpu.VMEM((width, n_rows), F32)],
        )
        state = sum_pair(collect(mine, theirs)) + token_pair[:, :BLOCK].astype(F32)
        h_held, h_other = spread(state.astype(BF16))

    with jax.named_scope("targets"):
        slices = []
        for side in range(2):
            chunk = side * 8 + y * 2 + core
            parts = [
                lax.dynamic_index_in_dim(
                    teachers[k].reshape(-1, n_mp, short[k]), chunk, 1, keepdims=False
                )
                for k in range(3)
            ]
            slices.append(jnp.pad(jnp.concatenate(parts, axis=1), ((0, 0), (0, spare))))
        pool = gather_dp(jnp.concatenate(slices, axis=1)).reshape(-1, 2 * TEACH)
        mixed = [a[:, BLOCK : BLOCK + 4, :share] for a in (x_held, x_other)]
        mixed = jnp.stack(
            [jnp.where(core == 0, mixed[0], mixed[1]), jnp.where(core == 0, mixed[1], mixed[0])], axis=1
        )
        source = mixed.transpose(2, 0, 1, 3).reshape(4, n_rows).astype(jnp.int32)
        places = jnp.arange(pool.shape[0], dtype=jnp.int32)[:, None]
        spots = source[:1] * teach_dino.shape[0] + source[1:]
        target = []
        for side in range(2):
            offset = side * TEACH
            for k in range(3):
                chosen = (places == spots[k : k + 1]).astype(BF16)
                target.append(dot(pool[:, offset : offset + short[k]], chosen, 0, 0))
                offset = offset + short[k]
            target.append(jnp.zeros((spare, n_rows), F32))
        target = jnp.concatenate(target, axis=0).reshape(2, TEACH, n_rows).astype(BF16)

    with jax.named_scope("adaptors"):
        h, pre_adapt, q, mine, theirs = call(
            adaptor_kernel,
            [
                ((width, n_rows), BF16),
                ((3 * hid, n_rows), F32),
                ((3 * hid, n_rows), BF16),
                ((8, TEACH, n_rows), BF16),
                ((8, TEACH, n_rows), BF16),
            ],
            at, h_held, h_other, adapt_t, heads_t,
        )
        error = (sum_pair(collect(mine, theirs)) - target.astype(F32)).astype(BF16)
        e_held, e_other = spread(error)

    with jax.named_scope("adaptors_back"):
        err, back, mine, theirs = call(
            adaptor_back_kernel,
            [
                ((n_mp * TEACH, n_rows), BF16),
                ((3 * hid, n_rows), BF16),
                ((8, BLOCK, n_rows), BF16),
                ((8, BLOCK, n_rows), BF16),
            ],
            at, e_held, e_other, heads_all, pre_adapt, adapt,
            scratch=[pltpu.VMEM((width, n_rows), F32)],
        )
        dstate = sum_pair(collect(mine, theirs))
        d_held, d_other = spread(dstate.astype(BF16))

    with jax.named_scope("adaptor_grads"):
        mine, theirs = call(
            functools.partial(adaptor_grads_kernel, scale, short),
            [((8, BLOCK + LOW, 4 * hid), BF16)] * 2,
            half, err, q, h, back,
            scratch=[pltpu.VMEM((width, 3 * hid), F32), pltpu.VMEM((n_mp * TEACH, 3 * hid), F32)],
        )
        pack = scatter_dp(mine, theirs)

    with jax.named_scope("block_back"):
        ds, out_mine, out_theirs = call(
            functools.partial(w_out_grad_kernel, scale),
            [((width, n_rows), BF16)] + [((8, BLOCK, hidden), BF16)] * 2,
            at, d_held, d_other, act,
            scratch=[pltpu.VMEM((width, hidden), F32)],
        )
        dpre, mine, theirs = call(
            block_back_kernel,
            [((hidden, n_rows), BF16)] + [((8, BLOCK + SUMS, n_rows), BF16)] * 2,
            at, ds, w_out, pre_mlp, w_in, gain, x_held, x_other, stat,
            scratch=[pltpu.VMEM((width, n_rows), F32)],
        )
        summed = sum_own(collect(mine, theirs))
        gain_own = lax.dynamic_slice_in_dim(ln_gain, lax.axis_index("mp") * BLOCK, BLOCK, 0)
        normed = (tokens.T.astype(F32) - stat[0:1]) * stat[1:2]
        dnorm = summed[:BLOCK] * gain_own[:, None]
        first = summed[BLOCK : BLOCK + 1] + summed[BLOCK + 1 : BLOCK + 2]
        second = summed[BLOCK + 2 : BLOCK + 3] + summed[BLOCK + 3 : BLOCK + 4]
        grad_tokens = pick(dstate, x_hi, 0) + stat[1:2] * (dnorm - first - normed * second)

    with jax.named_scope("block_grads"):
        grad_w_out = scatter_dp(out_mine, out_theirs)
        in_mine, in_theirs = call(
            functools.partial(w_in_grad_kernel, scale),
            [((8, BLOCK, hidden), BF16)] * 2,
            at, z, dpre,
            scratch=[pltpu.VMEM((width, hidden), F32)],
        )
        grad_w_in = scatter_dp(in_mine, in_theirs)

    tail = pack[BLOCK:]
    second = jnp.concatenate([tail[:, :hid], tail[:, 2 * hid : 3 * hid]], axis=0)
    third = jnp.concatenate([tail[:, hid : 2 * hid], tail[:, 3 * hid :]], axis=0)
    return (
        grad_tokens.T,
        grad_w_in,
        grad_w_out.T,
        jnp.stack([pack[:BLOCK, k * hid : (k + 1) * hid] for k in range(3)]),
        pack[:BLOCK, 3 * hid :].T,
        second[: short[1]].T,
        third[: short[2]].T,
    )


def solution(mesh):
    placed = (
        P("dp", "mp"),
        P(),
        P(None, "mp"),
        P("mp", None),
        P(None, None, "mp"),
        P("mp", None),
        P("mp", None),
        P("mp", None),
        P("dp", None),
        P("dp", None),
        P("dp", None),
        P(("dp", "mp"), None),
        P(("dp", "mp"), None),
    )
    return jax.shard_map(
        body,
        mesh=mesh,
        in_specs=placed,
        out_specs=(
            P("dp", "mp"),
            P("dp", "mp"),
            P("mp", "dp"),
            P(None, "dp", "mp"),
            P("mp", "dp"),
            P("mp", "dp"),
            P("mp", "dp"),
        ),
        check_vma=False,
    )
```

```python
import functools
import math

import jax
import jax.numpy as jnp
from jax import lax
from jax.experimental import pallas as pl
from jax.experimental.pallas import tpu as pltpu
from jax.sharding import PartitionSpec as P

F32 = jnp.float32
BF16 = jnp.bfloat16
VMEM_LIMIT = 20 * 1024 * 1024
PACK_ORDER = (1, 2, 4, 8)
OUT_ORDER = (1, 8, 2, 4)
IN_ORDER = (8, 1, 2, 4)

CORE = [(i, i ^ 1) for i in range(16)]
FAR = [(i, i ^ 8) for i in range(16)]
AROUND_Y = [[(i, (i & 9) | ((((i >> 1 & 3) + k) & 3) << 1)) for i in range(16)] for k in range(4)]

BLOCK = 96
TEACH = 256
EXTRA = 8
SUMS = 16
LOW = 48


def gelu(value):
    return 0.5 * value * (1.0 + lax.erf(value * 0.7071067811865476))


def gelu_slope(value):
    return (
        0.5 * (1.0 + lax.erf(value * 0.7071067811865476))
        + value * jnp.exp(-0.5 * value * value) * 0.3989422804014327
    )


def dot(left, right, over_left=1, over_right=0):
    return lax.dot_general(
        left, right, (((over_left,), (over_right,)), ((), ())), preferred_element_type=F32
    )


def pick(array, index, axis):
    return lax.dynamic_index_in_dim(array, index, axis, keepdims=False)


def put(buffer, piece, *at):
    return lax.dynamic_update_slice(buffer, piece, at + (0,) * (buffer.ndim - len(at)))


def mp_place():
    index = lax.axis_index("mp")
    return index >> 3, (index >> 1) & 3, index & 1


def spread(pair):
    y = mp_place()[1]
    held = put(jnp.zeros((2, 4, *pair.shape[1:]), pair.dtype), pair[:, None], 0, y)
    for k in (1, 3, 2):
        held = put(held, lax.ppermute(pair, "mp", AROUND_Y[k])[:, None], 0, (y - k) & 3)
    held = held.reshape(8, *pair.shape[1:])
    return held, lax.ppermute(held, "mp", CORE)


def collect(mine, theirs, through=None):
    y = mp_place()[1]
    other = lax.ppermute(theirs, "mp", CORE)
    held = (mine.astype(F32) + other.astype(F32)).astype(BF16).reshape(2, 4, *mine.shape[1:])
    arrived = [lax.ppermute(pick(held, (y + k) & 3, 1), "mp", AROUND_Y[k]) for k in (1, 3, 2)]
    own = pick(held, y, 1)
    if through is not None:
        own = through(own)
    total = own.astype(F32)
    for piece in arrived:
        total = total + piece.astype(F32)
    return total


def sum_pair(total):
    rounded = total.astype(BF16)
    return rounded.astype(F32) + lax.ppermute(rounded, "mp", FAR).astype(F32)


def sum_own(total):
    x_hi = mp_place()[0]
    other = lax.ppermute(pick(total, 1 - x_hi, 0).astype(BF16), "mp", FAR)
    return pick(total, x_hi, 0) + other.astype(F32)


def dp_bit(weight):
    return (lax.axis_index("dp") // weight) & 1


def scatter_dp(order, mine, theirs):
    for step, weight in enumerate(order):
        if step:
            split = total.astype(BF16).reshape(2, -1, *total.shape[1:])
            on = dp_bit(weight)
            mine = pick(total.reshape(split.shape), on, 0)
            theirs = pick(split, 1 - on, 0)
        other = lax.ppermute(theirs, "dp", [(i, i ^ weight) for i in range(16)])
        total = mine.astype(F32) + other.astype(F32)
    return total[0]


def gather_dp(block):
    index = lax.axis_index("dp")
    x_lo, z = index >> 3, index & 7
    held = block[None]
    for bit in (2, 1, 0):
        other = lax.ppermute(held, "dp", [(i, i ^ (1 << bit)) for i in range(16)])
        on = ((z >> bit) & 1) == 1
        held = jnp.stack([jnp.where(on, other, held), jnp.where(on, held, other)], axis=held.ndim - 2)
    other = lax.ppermute(held, "dp", FAR)
    on = x_lo == 1
    held = jnp.stack([jnp.where(on, other, held), jnp.where(on, held, other)])
    return held.reshape(16, *block.shape)


def rows(start, size):
    return pl.ds(pl.multiple_of(start, 16), size)


def place(core, i, own, size):
    return rows((2 * i + (core if own else 1 - core)) * size, size)


def call(kernel, outs, *args, scratch=(), flops=0, after=()):
    spec = pl.BlockSpec(memory_space=pltpu.VMEM)
    specs = [pl.BlockSpec(memory_space=pltpu.SMEM)] + [spec] * (len(args) - 1)
    skip = len(after)
    if skip:
        inner = kernel
        kernel = lambda *refs: inner(*refs[skip:])
    size = sum(math.prod(a.shape) * a.dtype.itemsize for a in args)
    size += sum(math.prod(shape) * jnp.dtype(dtype).itemsize for shape, dtype in outs)
    return pl.pallas_call(
        kernel,
        out_shape=tuple(jax.ShapeDtypeStruct(shape, dtype) for shape, dtype in outs),
        in_specs=[pl.BlockSpec(memory_space=pl.ANY)] * skip + specs,
        out_specs=(spec,) * len(outs),
        scratch_shapes=list(scratch),
        compiler_params=pltpu.CompilerParams(vmem_limit_bytes=VMEM_LIMIT),
        cost_estimate=pl.CostEstimate(flops=flops, bytes_accessed=size, transcendentals=0),
    )(*after, *args)


def send_out(core, full_ref, mine_ref, theirs_ref, size):
    for i in range(8):
        mine_ref[i] = full_ref[place(core, i, True, size)].astype(BF16)
        theirs_ref[i] = full_ref[place(core, i, False, size)].astype(BF16)


def take_in(core, held_ref, other_ref, full_ref, size):
    for i in range(8):
        full_ref[place(core, i, True, size)] = held_ref[i]
        full_ref[place(core, i, False, size)] = other_ref[i]


def block_kernel(core_ref, held_ref, other_ref, gain_ref, w_in_t_ref, w_out_t_ref,
                 z_ref, pre_ref, act_ref, stat_ref, mine_ref, theirs_ref, full_ref):
    core = core_ref[0]
    width = z_ref.shape[0]
    total = jnp.zeros((1, z_ref.shape[1]), F32)
    for i in range(8):
        for ref in (held_ref, other_ref):
            total = total + jnp.sum(ref[i, :BLOCK].astype(F32), axis=0, keepdims=True)
    mean = total / width
    total = jnp.zeros_like(mean)
    for i in range(8):
        for ref in (held_ref, other_ref):
            centred = ref[i, :BLOCK].astype(F32) - mean
            total = total + jnp.sum(centred * centred, axis=0, keepdims=True)
    inv_std = 1.0 / jnp.sqrt(total / width + 1e-06)
    stat_ref[...] = jnp.zeros_like(stat_ref)
    stat_ref[0:1] = mean
    stat_ref[1:2] = inv_std
    for i in range(8):
        for own, ref in ((True, held_ref), (False, other_ref)):
            at = place(core, i, own, BLOCK)
            normed = (ref[i, :BLOCK].astype(F32) - mean) * inv_std
            z_ref[at] = (normed * gain_ref[at]).astype(BF16)
    pre = dot(w_in_t_ref[...], z_ref[...])
    pre_ref[...] = pre
    act_ref[...] = gelu(pre).astype(BF16)
    full_ref[...] = dot(w_out_t_ref[...], act_ref[...])
    send_out(core, full_ref, mine_ref, theirs_ref, BLOCK)


def adaptor_kernel(core_ref, held_ref, other_ref, adapt_t_ref, heads_t_ref,
                   h_ref, pre_ref, q_ref, mine_ref, theirs_ref):
    core = core_ref[0]
    take_in(core, held_ref, other_ref, h_ref, BLOCK)
    pre = dot(adapt_t_ref[...], h_ref[...])
    pre_ref[...] = pre
    q_ref[...] = gelu(pre).astype(BF16)
    for i in range(8):
        mine_ref[i] = dot(heads_t_ref[place(core, i, True, TEACH)], q_ref[...]).astype(BF16)
        theirs_ref[i] = dot(heads_t_ref[place(core, i, False, TEACH)], q_ref[...]).astype(BF16)


def adaptor_back_kernel(core_ref, held_ref, other_ref, heads_ref, pre_ref, adapt_ref,
                        err_ref, back_ref, mine_ref, theirs_ref, full_ref):
    core = core_ref[0]
    take_in(core, held_ref, other_ref, err_ref, TEACH)
    lifted = dot(heads_ref[...], err_ref[...])
    back_ref[...] = (lifted * gelu_slope(pre_ref[...])).astype(BF16)
    full_ref[...] = dot(adapt_ref[...], back_ref[...])
    send_out(core, full_ref, mine_ref, theirs_ref, BLOCK)


def adaptor_grads_kernel(scale, widths, on_ref, err_ref, q_ref, h_ref, back_ref,
                         mine_ref, theirs_ref, ga_ref, go_ref):
    hid3 = q_ref.shape[0]
    hid = hid3 // 3
    ga_ref[...] = dot(h_ref[...], back_ref[...], 1, 1) * scale
    go_ref[...] = dot(err_ref[...], q_ref[...], 1, 1) * scale
    w0, w1, w2 = widths
    for j in range(8):
        for chunk, ref in sides(PACK_ORDER, on_ref[0], j, mine_ref, theirs_ref):
            at = rows(chunk * BLOCK, BLOCK)
            go = go_ref[rows(chunk * TEACH, TEACH)]
            ref[j, :BLOCK] = jnp.concatenate(
                [ga_ref[at], go[:BLOCK, :hid]], axis=1
            ).astype(BF16)
            second = go[w0 : w0 + w1, hid : 2 * hid]
            third = go[w0 + w1 : w0 + w1 + w2, 2 * hid :]
            second = jnp.concatenate([second, jnp.zeros((2 * LOW - w1, hid), F32)], axis=0)
            third = jnp.concatenate([third, jnp.zeros((2 * LOW - w2, hid), F32)], axis=0)
            ref[j, BLOCK:] = jnp.concatenate(
                [second[:LOW], third[:LOW], second[LOW:], third[LOW:]], axis=1
            ).astype(BF16)


def w_out_grad_kernel(scale, place_ref, held_ref, other_ref, act_ref,
                      ds_ref, mine_ref, theirs_ref, full_ref):
    take_in(place_ref[0], held_ref, other_ref, ds_ref, BLOCK)
    full_ref[...] = dot(ds_ref[...], act_ref[...], 1, 1) * scale
    halves(OUT_ORDER, place_ref[1], full_ref, mine_ref, theirs_ref)


def sides(order, on, j, mine_ref, theirs_ref):
    first, rest = order[0], order[1:]
    chunk = sum(weight * ((j >> (2 - i)) & 1) for i, weight in enumerate(rest))
    return ((on * first + chunk, mine_ref), ((1 - on) * first + chunk, theirs_ref))


def halves(order, on, full_ref, mine_ref, theirs_ref):
    for j in range(8):
        for chunk, ref in sides(order, on, j, mine_ref, theirs_ref):
            ref[j] = full_ref[rows(chunk * BLOCK, BLOCK)].astype(BF16)


def w_in_grad_kernel(scale, place_ref, z_ref, dpre_ref, mine_ref, theirs_ref, full_ref):
    full_ref[...] = dot(z_ref[...], dpre_ref[...], 1, 1) * scale
    halves(IN_ORDER, place_ref[2], full_ref, mine_ref, theirs_ref)


def block_back_kernel(core_ref, ds_ref, w_out_ref, pre_ref, w_in_ref, gain_ref, held_ref, other_ref, stat_ref,
                      dpre_ref, mine_ref, theirs_ref, full_ref):
    core = core_ref[0]
    width = ds_ref.shape[0]
    dpre_ref[...] = (dot(w_out_ref[...], ds_ref[...]) * gelu_slope(pre_ref[...])).astype(BF16)
    full_ref[...] = dot(w_in_ref[...], dpre_ref[...])
    mean = stat_ref[0:1]
    inv_std = stat_ref[1:2]
    first = jnp.zeros_like(mean)
    second = jnp.zeros_like(mean)
    for i in range(8):
        for own, ref, out_ref in ((True, held_ref, mine_ref), (False, other_ref, theirs_ref)):
            at = place(core, i, own, BLOCK)
            dnorm = full_ref[at]
            out_ref[i, :BLOCK] = dnorm.astype(BF16)
            lifted = dnorm * gain_ref[at]
            normed = (ref[i, :BLOCK].astype(F32) - mean) * inv_std
            first = first + jnp.sum(lifted, axis=0, keepdims=True)
            second = second + jnp.sum(lifted * normed, axis=0, keepdims=True)
    sums = []
    for part in (first / width, second / width):
        high = part.astype(BF16).astype(F32)
        sums = sums + [high, part - high]
    sums = jnp.concatenate(sums + [jnp.zeros((SUMS - 4, mean.shape[1]), F32)], axis=0).astype(BF16)
    for i in range(8):
        mine_ref[i, BLOCK:] = sums
        theirs_ref[i, BLOCK:] = sums


def flip(block):
    return block.astype(F32).T.astype(BF16)


def first_weights_kernel(place_ref, tokens_ref, w_in_ref, w_out_ref, pair_ref, w_in_t_ref, w_out_t_ref):
    pair_ref[...] = jnp.zeros_like(pair_ref)
    pair_ref[place_ref[0], :BLOCK] = tokens_ref[...]
    depth, hidden = w_in_ref.shape
    for start in range(0, depth, hidden):
        w_in_t_ref[:, start : start + hidden] = flip(w_in_ref[start : start + hidden])
        w_out_t_ref[start : start + hidden] = flip(w_out_ref[:, start : start + hidden])


def more_weights_kernel(widths, _, own_ref, block_ref, adapt_ref, *refs):
    head_refs = refs[:3]
    own_out_ref, block_out_ref, all_ref, all_t_ref, heads_ref, heads_t_ref = refs[3:]
    own_out_ref[...] = own_ref[...]
    block_out_ref[...] = block_ref[...]
    depth = adapt_ref.shape[1]
    hid = adapt_ref.shape[2]
    for start in range(0, depth, 512):
        block = jnp.concatenate(
            [adapt_ref[k, start : start + 512].astype(F32) for k in range(3)], axis=1
        )
        all_ref[start : start + 512] = block.astype(BF16)
        all_t_ref[:, start : start + 512] = block.T.astype(BF16)
    heads_ref[...] = jnp.zeros_like(heads_ref)
    for m in range(16):
        offset = m * TEACH
        for k in range(3):
            wide = widths[k]
            heads_ref[k * hid : (k + 1) * hid, offset : offset + wide] = head_refs[k][:, m * wide : (m + 1) * wide]
            offset = offset + wide
        heads_t_ref[m * TEACH : (m + 1) * TEACH] = flip(heads_ref[:, m * TEACH : (m + 1) * TEACH])


def body(
    tokens,
    ln_gain,
    w_in,
    w_out,
    adapt_in,
    out_dino,
    out_siglip,
    out_sam,
    teach_dino,
    teach_siglip,
    teach_sam,
    src_dev,
    src_row,
):
    heads = (out_dino, out_siglip, out_sam)
    teachers = (teach_dino, teach_siglip, teach_sam)
    n_rows = tokens.shape[0]
    n_mp = lax.axis_size("mp")
    n_dp = lax.axis_size("dp")
    width = BLOCK * n_mp
    hidden = w_in.shape[1]
    hid = adapt_in.shape[2]
    share = n_rows // n_mp
    short = [head.shape[1] // n_mp for head in heads]
    spare = TEACH - sum(short)
    scale = 1.0 / math.sqrt(n_rows * n_dp)
    x_hi, y, core = mp_place()
    at = jnp.stack([core, dp_bit(OUT_ORDER[0]), dp_bit(IN_ORDER[0])]).astype(jnp.int32)
    gain = ln_gain[:, None]

    with jax.named_scope("tokens"):
        own_tokens = tokens.T
        far_tokens = lax.ppermute(own_tokens, "mp", FAR)
        token_pair, w_in_t, w_out_t = call(
            first_weights_kernel,
            [
                ((2, BLOCK + EXTRA, n_rows), BF16),
                ((hidden, width), BF16),
                ((width, hidden), BF16),
            ],
            x_hi[None].astype(jnp.int32), own_tokens, w_in, w_out,
        )
        sources = jnp.concatenate([src_dev, src_row], axis=1).T.astype(BF16)
        sources = jnp.pad(sources, ((0, EXTRA - 4), (0, n_rows - share)))
        token_pair = put(token_pair, far_tokens[None], 1 - x_hi)
        token_pair = put(token_pair, sources[None], x_hi, BLOCK)
        token_pair = put(token_pair, lax.ppermute(sources, "mp", FAR)[None], 1 - x_hi, BLOCK)
        x_held, x_other = spread(token_pair)

    with jax.named_scope("teachers"):
        slices = []
        for side in range(2):
            chunk = side * 8 + y * 2 + core
            parts = [
                lax.dynamic_index_in_dim(
                    teachers[k].reshape(-1, n_mp, short[k]), chunk, 1, keepdims=False
                )
                for k in range(3)
            ]
            slices.append(jnp.pad(jnp.concatenate(parts, axis=1), ((0, 0), (0, spare))))
        slices = jnp.concatenate(slices, axis=1)
    more = []

    def more_weights(own):
        own, *rest = call(
            functools.partial(more_weights_kernel, short),
            [
                (own.shape, BF16),
                (slices.shape, BF16),
                ((width, 3 * hid), BF16),
                ((3 * hid, width), BF16),
                ((3 * hid, n_mp * TEACH), BF16),
                ((n_mp * TEACH, 3 * hid), BF16),
            ],
            at, own, slices, adapt_in, *heads,
        )
        more.extend(rest)
        return own

    with jax.named_scope("block"):
        z, pre_mlp, act, stat, mine, theirs = call(
            block_kernel,
            [
                ((width, n_rows), BF16),
                ((hidden, n_rows), F32),
                ((hidden, n_rows), BF16),
                ((8, n_rows), F32),
                ((8, BLOCK, n_rows), BF16),
                ((8, BLOCK, n_rows), BF16),
            ],
            at, x_held, x_other, gain, w_in_t, w_out_t,
            scratch=[pltpu.VMEM((width, n_rows), F32)],
        )
        state = sum_pair(collect(mine, theirs, more_weights)) + token_pair[:, :BLOCK].astype(F32)
        h_held, h_other = spread(state.astype(BF16))

    with jax.named_scope("targets"):
        block, adapt, adapt_t, heads_all, heads_t = more
        pool = gather_dp(block).reshape(-1, 2 * TEACH)
        mixed = [a[:, BLOCK : BLOCK + 4, :share] for a in (x_held, x_other)]
        mixed = jnp.stack(
            [jnp.where(core == 0, mixed[0], mixed[1]), jnp.where(core == 0, mixed[1], mixed[0])], axis=1
        )
        source = mixed.transpose(2, 0, 1, 3).reshape(4, n_rows).astype(jnp.int32)
        places = jnp.arange(pool.shape[0], dtype=jnp.int32)[:, None]
        spots = source[:1] * teach_dino.shape[0] + source[1:]
        target = []
        for side in range(2):
            offset = side * TEACH
            for k in range(3):
                chosen = (places == spots[k : k + 1]).astype(BF16)
                target.append(dot(pool[:, offset : offset + short[k]], chosen, 0, 0))
                offset = offset + short[k]
            target.append(jnp.zeros((spare, n_rows), F32))
        target = jnp.concatenate(target, axis=0).reshape(2, TEACH, n_rows).astype(BF16)

    with jax.named_scope("adaptors"):
        h, pre_adapt, q, mine, theirs = call(
            adaptor_kernel,
            [
                ((width, n_rows), BF16),
                ((3 * hid, n_rows), F32),
                ((3 * hid, n_rows), BF16),
                ((8, TEACH, n_rows), BF16),
                ((8, TEACH, n_rows), BF16),
            ],
            at, h_held, h_other, adapt_t, heads_t,
        )
        error = (sum_pair(collect(mine, theirs)) - target.astype(F32)).astype(BF16)
        e_held, e_other = spread(error)

    with jax.named_scope("adaptors_back"):
        err, back, mine, theirs = call(
            adaptor_back_kernel,
            [
                ((n_mp * TEACH, n_rows), BF16),
                ((3 * hid, n_rows), BF16),
                ((8, BLOCK, n_rows), BF16),
                ((8, BLOCK, n_rows), BF16),
            ],
            at, e_held, e_other, heads_all, pre_adapt, adapt,
            scratch=[pltpu.VMEM((width, n_rows), F32)],
        )
        packs = []

        def adaptor_grads(own):
            packs.extend(
                call(
                    functools.partial(adaptor_grads_kernel, scale, short),
                    [((8, BLOCK + LOW, 4 * hid), BF16)] * 2,
                    dp_bit(PACK_ORDER[0])[None].astype(jnp.int32), err, q, h, back,
                    scratch=[
                        pltpu.VMEM((width, 3 * hid), F32),
                        pltpu.VMEM((n_mp * TEACH, 3 * hid), F32),
                    ],
                    after=(own,),
                )
            )
            return own

        dstate = sum_pair(collect(mine, theirs, adaptor_grads))
        d_held, d_other = spread(dstate.astype(BF16))

    with jax.named_scope("adaptor_grads"):
        pack = scatter_dp(PACK_ORDER, *packs)

    with jax.named_scope("block_back"):
        ds, out_mine, out_theirs = call(
            functools.partial(w_out_grad_kernel, scale),
            [((width, n_rows), BF16)] + [((8, BLOCK, hidden), BF16)] * 2,
            at, d_held, d_other, act,
            scratch=[pltpu.VMEM((width, hidden), F32)],
        )
        dpre, mine, theirs = call(
            block_back_kernel,
            [((hidden, n_rows), BF16)] + [((8, BLOCK + SUMS, n_rows), BF16)] * 2,
            at, ds, w_out, pre_mlp, w_in, gain, x_held, x_other, stat,
            scratch=[pltpu.VMEM((width, n_rows), F32)],
        )
        summed = sum_own(collect(mine, theirs))
        gain_own = lax.dynamic_slice_in_dim(ln_gain, lax.axis_index("mp") * BLOCK, BLOCK, 0)
        normed = (tokens.T.astype(F32) - stat[0:1]) * stat[1:2]
        dnorm = summed[:BLOCK] * gain_own[:, None]
        first = summed[BLOCK : BLOCK + 1] + summed[BLOCK + 1 : BLOCK + 2]
        second = summed[BLOCK + 2 : BLOCK + 3] + summed[BLOCK + 3 : BLOCK + 4]
        grad_tokens = pick(dstate, x_hi, 0) + stat[1:2] * (dnorm - first - normed * second)

    with jax.named_scope("block_grads"):
        grad_w_out = scatter_dp(OUT_ORDER, out_mine, out_theirs)
        in_mine, in_theirs = call(
            functools.partial(w_in_grad_kernel, scale),
            [((8, BLOCK, hidden), BF16)] * 2,
            at, z, dpre,
            scratch=[pltpu.VMEM((width, hidden), F32)],
        )
        grad_w_in = scatter_dp(IN_ORDER, in_mine, in_theirs)

    tail = pack[BLOCK:]
    second = jnp.concatenate([tail[:, :hid], tail[:, 2 * hid : 3 * hid]], axis=0)
    third = jnp.concatenate([tail[:, hid : 2 * hid], tail[:, 3 * hid :]], axis=0)
    return (
        grad_tokens.T,
        grad_w_in,
        grad_w_out.T,
        jnp.stack([pack[:BLOCK, k * hid : (k + 1) * hid] for k in range(3)]),
        pack[:BLOCK, 3 * hid :].T,
        second[: short[1]].T,
        third[: short[2]].T,
    )


def solution(mesh):
    placed = (
        P("dp", "mp"),
        P(),
        P(None, "mp"),
        P("mp", None),
        P(None, None, "mp"),
        P("mp", None),
        P("mp", None),
        P("mp", None),
        P("dp", None),
        P("dp", None),
        P("dp", None),
        P(("dp", "mp"), None),
        P(("dp", "mp"), None),
    )
    return jax.shard_map(
        body,
        mesh=mesh,
        in_specs=placed,
        out_specs=(
            P("dp", "mp"),
            P("dp", "mp"),
            P("mp", "dp"),
            P(None, "dp", "mp"),
            P("mp", "dp"),
            P("mp", "dp"),
            P("mp", "dp"),
        ),
        check_vma=False,
    )
```

```python
import functools
import math

import jax
import jax.numpy as jnp
from jax import lax
from jax.experimental import pallas as pl
from jax.experimental.pallas import tpu as pltpu
from jax.sharding import PartitionSpec as P

F32 = jnp.float32
BF16 = jnp.bfloat16
VMEM_LIMIT = 20 * 1024 * 1024
PACK_ORDER = (8, 1, 2, 4)
OUT_ORDER = (1, 8, 2, 4)
IN_ORDER = (8, 1, 2, 4)

CORE = [(i, i ^ 1) for i in range(16)]
FAR = [(i, i ^ 8) for i in range(16)]
AROUND_Y = [[(i, (i & 9) | ((((i >> 1 & 3) + k) & 3) << 1)) for i in range(16)] for k in range(4)]

BLOCK = 96
TEACH = 256
PART = 128
EXTRA = 8
SUMS = 16
LOW = 48


def gelu(value):
    return 0.5 * value * (1.0 + lax.erf(value * 0.7071067811865476))


def gelu_slope(value):
    return (
        0.5 * (1.0 + lax.erf(value * 0.7071067811865476))
        + value * jnp.exp(-0.5 * value * value) * 0.3989422804014327
    )


def dot(left, right, over_left=1, over_right=0):
    return lax.dot_general(
        left, right, (((over_left,), (over_right,)), ((), ())), preferred_element_type=F32
    )


def pick(array, index, axis):
    return lax.dynamic_index_in_dim(array, index, axis, keepdims=False)


def put(buffer, piece, *at):
    return lax.dynamic_update_slice(buffer, piece, at + (0,) * (buffer.ndim - len(at)))


def mp_place():
    index = lax.axis_index("mp")
    return index >> 3, (index >> 1) & 3, index & 1


def spread(pair, through=None):
    y = mp_place()[1]
    arrived = [(k, lax.ppermute(pair, "mp", AROUND_Y[k])) for k in (1, 3, 2)]
    if through is not None:
        pair = through(pair)
    held = put(jnp.zeros((2, 4, *pair.shape[1:]), pair.dtype), pair[:, None], 0, y)
    for k, piece in arrived:
        held = put(held, piece[:, None], 0, (y - k) & 3)
    held = held.reshape(8, *pair.shape[1:])
    return held, lax.ppermute(held, "mp", CORE)


def collect(mine, theirs, through=None):
    y = mp_place()[1]
    other = lax.ppermute(theirs, "mp", CORE)
    held = (mine.astype(F32) + other.astype(F32)).astype(BF16).reshape(2, 4, *mine.shape[1:])
    arrived = [lax.ppermute(pick(held, (y + k) & 3, 1), "mp", AROUND_Y[k]) for k in (1, 3, 2)]
    own = pick(held, y, 1)
    if through is not None:
        own = through(own)
    total = own.astype(F32)
    for piece in arrived:
        total = total + piece.astype(F32)
    return total


def sum_pair(total):
    rounded = total.astype(BF16)
    return rounded.astype(F32) + lax.ppermute(rounded, "mp", FAR).astype(F32)


def sum_own(total):
    x_hi = mp_place()[0]
    other = lax.ppermute(pick(total, 1 - x_hi, 0).astype(BF16), "mp", FAR)
    return pick(total, x_hi, 0) + other.astype(F32)


def dp_bit(weight):
    return (lax.axis_index("dp") // weight) & 1


def swap_dp(weight, array):
    return lax.ppermute(array, "dp", [(i, i ^ weight) for i in range(16)])


def scatter_dp(order, mine, theirs):
    total = mine.astype(F32) + swap_dp(order[0], theirs).astype(F32)
    for weight in order[1:]:
        total = scatter_step(weight, total)
    return total[0]


def scatter_step(weight, total):
    on = dp_bit(weight)
    total = total.reshape(2, -1, *total.shape[1:])
    return pick(total, on, 0) + swap_dp(weight, pick(total, 1 - on, 0).astype(BF16)).astype(F32)


def gather_dp(block):
    index = lax.axis_index("dp")
    x_lo, z = index >> 3, index & 7
    held = block[None]
    for bit in (2, 1, 0):
        other = lax.ppermute(held, "dp", [(i, i ^ (1 << bit)) for i in range(16)])
        on = ((z >> bit) & 1) == 1
        held = jnp.stack([jnp.where(on, other, held), jnp.where(on, held, other)], axis=held.ndim - 2)
    other = lax.ppermute(held, "dp", FAR)
    on = x_lo == 1
    held = jnp.stack([jnp.where(on, other, held), jnp.where(on, held, other)])
    return held.reshape(16, *block.shape)


def rows(start, size):
    return pl.ds(pl.multiple_of(start, 16), size)


def place(core, i, own, size):
    return rows((2 * i + (core if own else 1 - core)) * size, size)


def call(kernel, outs, *args, scratch=(), flops=0, after=(), far=0):
    spec = pl.BlockSpec(memory_space=pltpu.VMEM)
    specs = [pl.BlockSpec(memory_space=pltpu.SMEM)] + [spec] * (len(args) - 1)
    skip = len(after)
    if skip:
        inner = kernel
        kernel = lambda *refs: inner(*refs[skip:])
    size = sum(math.prod(a.shape) * a.dtype.itemsize for a in args)
    size += sum(math.prod(shape) * jnp.dtype(dtype).itemsize for shape, dtype in outs)
    return pl.pallas_call(
        kernel,
        out_shape=tuple(jax.ShapeDtypeStruct(shape, dtype) for shape, dtype in outs),
        in_specs=[pl.BlockSpec(memory_space=pl.ANY)] * skip + specs,
        out_specs=(pl.BlockSpec(memory_space=pltpu.HBM),) * far + (spec,) * (len(outs) - far),
        scratch_shapes=[pltpu.VMEM(shape, dtype) for shape, dtype in outs[:far]]
        + [pltpu.SemaphoreType.DMA((far,))] * (far > 0)
        + list(scratch),
        compiler_params=pltpu.CompilerParams(vmem_limit_bytes=VMEM_LIMIT),
        cost_estimate=pl.CostEstimate(flops=flops, bytes_accessed=size, transcendentals=0),
    )(*after, *args)


def copy_out(source_ref, target_ref, sems, i):
    copy = pltpu.make_async_copy(source_ref, target_ref, sems.at[i])
    copy.start()
    return copy


def send_out(core, full_ref, mine_ref, theirs_ref, size):
    for i in range(8):
        mine_ref[i] = full_ref[place(core, i, True, size)].astype(BF16)
        theirs_ref[i] = full_ref[place(core, i, False, size)].astype(BF16)


def take_in(core, held_ref, other_ref, full_ref, size):
    for i in range(8):
        full_ref[place(core, i, True, size)] = held_ref[i]
        full_ref[place(core, i, False, size)] = other_ref[i]


def block_kernel(core_ref, held_ref, other_ref, gain_ref, w_in_t_ref, w_out_t_ref,
                 z_out_ref, pre_out_ref, act_out_ref, stat_ref, mine_ref, theirs_ref,
                 z_ref, pre_ref, act_ref, sems, full_ref):
    core = core_ref[0]
    width = z_ref.shape[0]
    total = jnp.zeros((1, z_ref.shape[1]), F32)
    for i in range(8):
        for ref in (held_ref, other_ref):
            total = total + jnp.sum(ref[i, :BLOCK].astype(F32), axis=0, keepdims=True)
    mean = total / width
    total = jnp.zeros_like(mean)
    for i in range(8):
        for ref in (held_ref, other_ref):
            centred = ref[i, :BLOCK].astype(F32) - mean
            total = total + jnp.sum(centred * centred, axis=0, keepdims=True)
    inv_std = 1.0 / jnp.sqrt(total / width + 1e-06)
    stat_ref[...] = jnp.zeros_like(stat_ref)
    stat_ref[0:1] = mean
    stat_ref[1:2] = inv_std
    for i in range(8):
        for own, ref in ((True, held_ref), (False, other_ref)):
            at = place(core, i, own, BLOCK)
            normed = (ref[i, :BLOCK].astype(F32) - mean) * inv_std
            z_ref[at] = (normed * gain_ref[at]).astype(BF16)
    copies = [copy_out(z_ref, z_out_ref, sems, 0)]
    pre = dot(w_in_t_ref[...], z_ref[...])
    pre_ref[...] = pre
    copies.append(copy_out(pre_ref, pre_out_ref, sems, 1))
    act_ref[...] = gelu(pre).astype(BF16)
    copies.append(copy_out(act_ref, act_out_ref, sems, 2))
    full_ref[...] = dot(w_out_t_ref[...], act_ref[...])
    send_out(core, full_ref, mine_ref, theirs_ref, BLOCK)
    for copy in copies:
        copy.wait()


def adaptor_kernel(core_ref, held_ref, other_ref, adapt_t_ref, heads_t_ref,
                   h_out_ref, pre_out_ref, q_out_ref, mine_a_ref, theirs_a_ref, mine_b_ref, theirs_b_ref,
                   h_ref, pre_ref, q_ref, sems):
    core = core_ref[0]
    take_in(core, held_ref, other_ref, h_ref, BLOCK)
    copies = [copy_out(h_ref, h_out_ref, sems, 0)]
    pre = dot(adapt_t_ref[...], h_ref[...])
    pre_ref[...] = pre
    copies.append(copy_out(pre_ref, pre_out_ref, sems, 1))
    q_ref[...] = gelu(pre).astype(BF16)
    copies.append(copy_out(q_ref, q_out_ref, sems, 2))
    for i in range(8):
        for own, a_ref, b_ref in ((True, mine_a_ref, mine_b_ref), (False, theirs_a_ref, theirs_b_ref)):
            pred = dot(heads_t_ref[place(core, i, own, TEACH)], q_ref[...]).astype(BF16)
            a_ref[i] = pred[:PART]
            b_ref[i] = pred[PART:]
    for copy in copies:
        copy.wait()


def adaptor_back_kernel(core_ref, held_a_ref, other_a_ref, held_b_ref, other_b_ref, heads_ref, pre_ref, adapt_ref,
                        err_ref, back_ref, mine_ref, theirs_ref, full_ref):
    core = core_ref[0]
    for i in range(8):
        for own, refs in ((True, (held_a_ref, held_b_ref)), (False, (other_a_ref, other_b_ref))):
            start = (2 * i + (core if own else 1 - core)) * TEACH
            for part in range(2):
                err_ref[rows(start + part * PART, PART)] = refs[part][i]
    lifted = dot(heads_ref[...], err_ref[...])
    back_ref[...] = (lifted * gelu_slope(pre_ref[...])).astype(BF16)
    full_ref[...] = dot(adapt_ref[...], back_ref[...])
    send_out(core, full_ref, mine_ref, theirs_ref, BLOCK)


def adaptor_grads_kernel(scale, widths, on_ref, own_ref, err_ref, q_ref, h_ref, back_ref,
                         own_out_ref, mine_ref, theirs_ref, ga_ref, go_ref):
    own_out_ref[...] = own_ref[...]
    hid3 = q_ref.shape[0]
    hid = hid3 // 3
    ga_ref[...] = dot(h_ref[...], back_ref[...], 1, 1) * scale
    go_ref[...] = dot(err_ref[...], q_ref[...], 1, 1) * scale
    w0, w1, w2 = widths
    for j in range(8):
        for chunk, ref in sides(PACK_ORDER, on_ref[0], j, mine_ref, theirs_ref):
            at = rows(chunk * BLOCK, BLOCK)
            go = go_ref[rows(chunk * TEACH, TEACH)]
            ref[j, :BLOCK] = jnp.concatenate(
                [ga_ref[at], go[:BLOCK, :hid]], axis=1
            ).astype(BF16)
            second = go[w0 : w0 + w1, hid : 2 * hid]
            third = go[w0 + w1 : w0 + w1 + w2, 2 * hid :]
            second = jnp.concatenate([second, jnp.zeros((2 * LOW - w1, hid), F32)], axis=0)
            third = jnp.concatenate([third, jnp.zeros((2 * LOW - w2, hid), F32)], axis=0)
            ref[j, BLOCK:] = jnp.concatenate(
                [second[:LOW], third[:LOW], second[LOW:], third[LOW:]], axis=1
            ).astype(BF16)


def w_out_grad_kernel(scale, place_ref, held_ref, other_ref, act_ref,
                      ds_ref, mine_ref, theirs_ref, full_ref):
    take_in(place_ref[0], held_ref, other_ref, ds_ref, BLOCK)
    full_ref[...] = dot(ds_ref[...], act_ref[...], 1, 1) * scale
    halves(OUT_ORDER, place_ref[1], full_ref, mine_ref, theirs_ref)


def sides(order, on, j, mine_ref, theirs_ref):
    first, rest = order[0], order[1:]
    chunk = sum(weight * ((j >> (2 - i)) & 1) for i, weight in enumerate(rest))
    return ((on * first + chunk, mine_ref), ((1 - on) * first + chunk, theirs_ref))


def halves(order, on, full_ref, mine_ref, theirs_ref):
    for j in range(8):
        for chunk, ref in sides(order, on, j, mine_ref, theirs_ref):
            ref[j] = full_ref[rows(chunk * BLOCK, BLOCK)].astype(BF16)


def w_in_grad_kernel(scale, place_ref, z_ref, dpre_ref, mine_ref, theirs_ref, full_ref):
    full_ref[...] = dot(z_ref[...], dpre_ref[...], 1, 1) * scale
    halves(IN_ORDER, place_ref[2], full_ref, mine_ref, theirs_ref)


def block_back_kernel(core_ref, ds_ref, w_out_ref, pre_ref, w_in_ref, gain_ref, held_ref, other_ref, stat_ref,
                      dpre_ref, mine_ref, theirs_ref, full_ref):
    core = core_ref[0]
    width = ds_ref.shape[0]
    dpre_ref[...] = (dot(w_out_ref[...], ds_ref[...]) * gelu_slope(pre_ref[...])).astype(BF16)
    full_ref[...] = dot(w_in_ref[...], dpre_ref[...])
    mean = stat_ref[0:1]
    inv_std = stat_ref[1:2]
    first = jnp.zeros_like(mean)
    second = jnp.zeros_like(mean)
    for i in range(8):
        for own, ref, out_ref in ((True, held_ref, mine_ref), (False, other_ref, theirs_ref)):
            at = place(core, i, own, BLOCK)
            dnorm = full_ref[at]
            out_ref[i, :BLOCK] = dnorm.astype(BF16)
            lifted = dnorm * gain_ref[at]
            normed = (ref[i, :BLOCK].astype(F32) - mean) * inv_std
            first = first + jnp.sum(lifted, axis=0, keepdims=True)
            second = second + jnp.sum(lifted * normed, axis=0, keepdims=True)
    sums = []
    for part in (first / width, second / width):
        high = part.astype(BF16).astype(F32)
        sums = sums + [high, part - high]
    sums = jnp.concatenate(sums + [jnp.zeros((SUMS - 4, mean.shape[1]), F32)], axis=0).astype(BF16)
    for i in range(8):
        mine_ref[i, BLOCK:] = sums
        theirs_ref[i, BLOCK:] = sums


def flip(block):
    return block.astype(F32).T.astype(BF16)


def first_weights_kernel(place_ref, tokens_ref, w_in_ref, w_out_ref, pair_ref, w_in_t_ref, w_out_t_ref):
    pair_ref[...] = jnp.zeros_like(pair_ref)
    pair_ref[place_ref[0], :BLOCK] = tokens_ref[...]
    depth, hidden = w_in_ref.shape
    for start in range(0, depth, hidden):
        w_in_t_ref[:, start : start + hidden] = flip(w_in_ref[start : start + hidden])
        w_out_t_ref[start : start + hidden] = flip(w_out_ref[:, start : start + hidden])


def more_weights_kernel(widths, place_ref, own_ref, adapt_ref, *refs):
    head_refs, teach_refs = refs[:3], refs[3:6]
    own_out_ref, block_ref, all_ref, all_t_ref, heads_ref, heads_t_ref = refs[6:]
    own_out_ref[...] = own_ref[...]
    block_ref[...] = jnp.zeros_like(block_ref)
    for m in range(8):

        @pl.when(place_ref[3] == m)
        def _():
            for side in range(2):
                offset = side * TEACH
                for k in range(3):
                    wide = widths[k]
                    start = (side * 8 + m) * wide
                    block_ref[:, offset : offset + wide] = teach_refs[k][:, start : start + wide]
                    offset = offset + wide

    depth = adapt_ref.shape[1]
    hid = adapt_ref.shape[2]
    for start in range(0, depth, 512):
        block = jnp.concatenate(
            [adapt_ref[k, start : start + 512].astype(F32) for k in range(3)], axis=1
        )
        all_ref[start : start + 512] = block.astype(BF16)
        all_t_ref[:, start : start + 512] = block.T.astype(BF16)
    heads_ref[...] = jnp.zeros_like(heads_ref)
    for m in range(16):
        offset = m * TEACH
        for k in range(3):
            wide = widths[k]
            heads_ref[k * hid : (k + 1) * hid, offset : offset + wide] = head_refs[k][:, m * wide : (m + 1) * wide]
            offset = offset + wide
        heads_t_ref[m * TEACH : (m + 1) * TEACH] = flip(heads_ref[:, m * TEACH : (m + 1) * TEACH])


def pack_add_kernel(_, pair_ref, mine_ref, other_ref, pair_out_ref, total_ref):
    pair_out_ref[...] = pair_ref[...]
    total_ref[...] = mine_ref[...].astype(F32) + other_ref[...].astype(F32)


def body(
    tokens,
    ln_gain,
    w_in,
    w_out,
    adapt_in,
    out_dino,
    out_siglip,
    out_sam,
    teach_dino,
    teach_siglip,
    teach_sam,
    src_dev,
    src_row,
):
    heads = (out_dino, out_siglip, out_sam)
    teachers = (teach_dino, teach_siglip, teach_sam)
    n_rows = tokens.shape[0]
    n_mp = lax.axis_size("mp")
    n_dp = lax.axis_size("dp")
    width = BLOCK * n_mp
    hidden = w_in.shape[1]
    hid = adapt_in.shape[2]
    share = n_rows // n_mp
    short = [head.shape[1] // n_mp for head in heads]
    spare = TEACH - sum(short)
    scale = 1.0 / math.sqrt(n_rows * n_dp)
    x_hi, y, core = mp_place()
    at = jnp.stack([core, dp_bit(OUT_ORDER[0]), dp_bit(IN_ORDER[0]), y * 2 + core]).astype(jnp.int32)
    gain = ln_gain[:, None]

    with jax.named_scope("tokens"):
        own_tokens = tokens.T
        far_tokens = lax.ppermute(own_tokens, "mp", FAR)
        token_pair, w_in_t, w_out_t = call(
            first_weights_kernel,
            [
                ((2, BLOCK + EXTRA, n_rows), BF16),
                ((hidden, width), BF16),
                ((width, hidden), BF16),
            ],
            x_hi[None].astype(jnp.int32), own_tokens, w_in, w_out,
        )
        sources = jnp.concatenate([src_dev, src_row], axis=1).T.astype(BF16)
        sources = jnp.pad(sources, ((0, EXTRA - 4), (0, n_rows - share)))
        token_pair = put(token_pair, far_tokens[None], 1 - x_hi)
        token_pair = put(token_pair, sources[None], x_hi, BLOCK)
        token_pair = put(token_pair, lax.ppermute(sources, "mp", FAR)[None], 1 - x_hi, BLOCK)
        x_held, x_other = spread(token_pair)

    more = []

    def more_weights(own):
        own, *rest = call(
            functools.partial(more_weights_kernel, short),
            [
                (own.shape, BF16),
                ((teach_dino.shape[0], 2 * TEACH), BF16),
                ((width, 3 * hid), BF16),
                ((3 * hid, width), BF16),
                ((3 * hid, n_mp * TEACH), BF16),
                ((n_mp * TEACH, 3 * hid), BF16),
            ],
            at, own, adapt_in, *heads, *teachers,
        )
        more.extend(rest)
        return own

    with jax.named_scope("block"):
        z, pre_mlp, act, stat, mine, theirs = call(
            block_kernel,
            [
                ((width, n_rows), BF16),
                ((hidden, n_rows), F32),
                ((hidden, n_rows), BF16),
                ((8, n_rows), F32),
                ((8, BLOCK, n_rows), BF16),
                ((8, BLOCK, n_rows), BF16),
            ],
            at, x_held, x_other, gain, w_in_t, w_out_t, far=3,
            scratch=[pltpu.VMEM((width, n_rows), F32)],
        )
        state = sum_pair(collect(mine, theirs, more_weights)) + token_pair[:, :BLOCK].astype(F32)
        h_held, h_other = spread(state.astype(BF16))

    with jax.named_scope("targets"):
        block, adapt, adapt_t, heads_all, heads_t = more
        pool = gather_dp(block).reshape(-1, 2 * TEACH)
        mixed = [a[:, BLOCK : BLOCK + 4, :share] for a in (x_held, x_other)]
        mixed = jnp.stack(
            [jnp.where(core == 0, mixed[0], mixed[1]), jnp.where(core == 0, mixed[1], mixed[0])], axis=1
        )
        source = mixed.transpose(2, 0, 1, 3).reshape(4, n_rows).astype(jnp.int32)
        places = jnp.arange(pool.shape[0], dtype=jnp.int32)[:, None]
        spots = source[:1] * teach_dino.shape[0] + source[1:]
        target = []
        for side in range(2):
            offset = side * TEACH
            for k in range(3):
                chosen = (places == spots[k : k + 1]).astype(BF16)
                target.append(dot(pool[:, offset : offset + short[k]], chosen, 0, 0))
                offset = offset + short[k]
            target.append(jnp.zeros((spare, n_rows), F32))
        target = jnp.concatenate(target, axis=0).reshape(2, TEACH, n_rows).astype(BF16)

    with jax.named_scope("adaptors"):
        h, pre_adapt, q, *sent = call(
            adaptor_kernel,
            [
                ((width, n_rows), BF16),
                ((3 * hid, n_rows), F32),
                ((3 * hid, n_rows), BF16),
            ]
            + [((8, PART, n_rows), BF16)] * 4,
            at, h_held, h_other, adapt_t, heads_t, far=3,
        )
        errors = []
        for part in range(2):
            pred = sum_pair(collect(*sent[2 * part : 2 * part + 2]))
            error = pred - target[:, part * PART : (part + 1) * PART].astype(F32)
            errors.extend(spread(error.astype(BF16)))

    with jax.named_scope("adaptors_back"):
        err, back, mine, theirs = call(
            adaptor_back_kernel,
            [
                ((n_mp * TEACH, n_rows), BF16),
                ((3 * hid, n_rows), BF16),
                ((8, BLOCK, n_rows), BF16),
                ((8, BLOCK, n_rows), BF16),
            ],
            at, *errors, heads_all, pre_adapt, adapt,
            scratch=[pltpu.VMEM((width, n_rows), F32)],
        )
        packs = []

        def adaptor_grads(own):
            own, *halves = call(
                functools.partial(adaptor_grads_kernel, scale, short),
                [(own.shape, BF16)] + [((8, BLOCK + LOW, 4 * hid), BF16)] * 2,
                dp_bit(PACK_ORDER[0])[None].astype(jnp.int32), own, err, q, h, back,
                scratch=[
                    pltpu.VMEM((width, 3 * hid), F32),
                    pltpu.VMEM((n_mp * TEACH, 3 * hid), F32),
                ],
            )
            packs.extend((halves[0], swap_dp(PACK_ORDER[0], halves[1])))
            return own

        def add_packs(pair):
            pair, total = call(
                pack_add_kernel,
                [(pair.shape, BF16), ((8, BLOCK + LOW, 4 * hid), F32)],
                at, pair, *packs,
            )
            packs.append(scatter_step(PACK_ORDER[1], total))
            return pair

        dstate = sum_pair(collect(mine, theirs, adaptor_grads))
        d_held, d_other = spread(dstate.astype(BF16), add_packs)

    with jax.named_scope("adaptor_grads"):
        pack = packs[-1]
        for weight in PACK_ORDER[2:]:
            pack = scatter_step(weight, pack)
        pack = pack[0]

    with jax.named_scope("block_back"):
        ds, out_mine, out_theirs = call(
            functools.partial(w_out_grad_kernel, scale),
            [((width, n_rows), BF16)] + [((8, BLOCK, hidden), BF16)] * 2,
            at, d_held, d_other, act,
            scratch=[pltpu.VMEM((width, hidden), F32)],
        )
        dpre, mine, theirs = call(
            block_back_kernel,
            [((hidden, n_rows), BF16)] + [((8, BLOCK + SUMS, n_rows), BF16)] * 2,
            at, ds, w_out, pre_mlp, w_in, gain, x_held, x_other, stat,
            scratch=[pltpu.VMEM((width, n_rows), F32)],
        )
        ins = []

        def w_in_grad(own):
            ins.extend(
                call(
                    functools.partial(w_in_grad_kernel, scale),
                    [((8, BLOCK, hidden), BF16)] * 2,
                    at, z, dpre,
                    scratch=[pltpu.VMEM((width, hidden), F32)],
                    after=(own,),
                )
            )
            return own

        summed = sum_own(collect(mine, theirs, w_in_grad))
        gain_own = lax.dynamic_slice_in_dim(ln_gain, lax.axis_index("mp") * BLOCK, BLOCK, 0)
        normed = (tokens.T.astype(F32) - stat[0:1]) * stat[1:2]
        dnorm = summed[:BLOCK] * gain_own[:, None]
        first = summed[BLOCK : BLOCK + 1] + summed[BLOCK + 1 : BLOCK + 2]
        second = summed[BLOCK + 2 : BLOCK + 3] + summed[BLOCK + 3 : BLOCK + 4]
        grad_tokens = pick(dstate, x_hi, 0) + stat[1:2] * (dnorm - first - normed * second)

    with jax.named_scope("block_grads"):
        grad_w_out = scatter_dp(OUT_ORDER, out_mine, out_theirs)
        grad_w_in = scatter_dp(IN_ORDER, *ins)

    tail = pack[BLOCK:]
    second = jnp.concatenate([tail[:, :hid], tail[:, 2 * hid : 3 * hid]], axis=0)
    third = jnp.concatenate([tail[:, hid : 2 * hid], tail[:, 3 * hid :]], axis=0)
    return (
        grad_tokens.T,
        grad_w_in,
        grad_w_out.T,
        jnp.stack([pack[:BLOCK, k * hid : (k + 1) * hid] for k in range(3)]),
        pack[:BLOCK, 3 * hid :].T,
        second[: short[1]].T,
        third[: short[2]].T,
    )


def solution(mesh):
    placed = (
        P("dp", "mp"),
        P(),
        P(None, "mp"),
        P("mp", None),
        P(None, None, "mp"),
        P("mp", None),
        P("mp", None),
        P("mp", None),
        P("dp", None),
        P("dp", None),
        P("dp", None),
        P(("dp", "mp"), None),
        P(("dp", "mp"), None),
    )
    return jax.shard_map(
        body,
        mesh=mesh,
        in_specs=placed,
        out_specs=(
            P("dp", "mp"),
            P("dp", "mp"),
            P("mp", "dp"),
            P(None, "dp", "mp"),
            P("mp", "dp"),
            P("mp", "dp"),
            P("mp", "dp"),
        ),
        check_vma=False,
    )
```

```python
import functools
import math

import jax
import jax.numpy as jnp
from jax import lax
from jax.experimental import pallas as pl
from jax.experimental.pallas import tpu as pltpu
from jax.sharding import PartitionSpec as P

F32 = jnp.float32
BF16 = jnp.bfloat16
VMEM_LIMIT = 20 * 1024 * 1024
PACK_ORDER = (1, 8, 2, 4)
OUT_ORDER = (1, 8, 2, 4)
IN_ORDER = (8, 1, 2, 4)

CORE = [(i, i ^ 1) for i in range(16)]
FAR = [(i, i ^ 8) for i in range(16)]
AROUND_Y = [[(i, (i & 9) | ((((i >> 1 & 3) + k) & 3) << 1)) for i in range(16)] for k in range(4)]

BLOCK = 96
TEACH = 256
PART = 128
EXTRA = 8
SUMS = 16
LOW = 48


def gelu(value):
    return 0.5 * value * (1.0 + lax.erf(value * 0.7071067811865476))


def gelu_slope(value):
    return (
        0.5 * (1.0 + lax.erf(value * 0.7071067811865476))
        + value * jnp.exp(-0.5 * value * value) * 0.3989422804014327
    )


def dot(left, right, over_left=1, over_right=0):
    return lax.dot_general(
        left, right, (((over_left,), (over_right,)), ((), ())), preferred_element_type=F32
    )


def pick(array, index, axis):
    return lax.dynamic_index_in_dim(array, index, axis, keepdims=False)


def put(buffer, piece, *at):
    return lax.dynamic_update_slice(buffer, piece, at + (0,) * (buffer.ndim - len(at)))


def mp_place():
    index = lax.axis_index("mp")
    return index >> 3, (index >> 1) & 3, index & 1


def spread(pair, through=None):
    y = mp_place()[1]
    arrived = [(k, lax.ppermute(pair, "mp", AROUND_Y[k])) for k in (1, 3, 2)]
    if through is not None:
        pair = through(pair)
    held = put(jnp.zeros((2, 4, *pair.shape[1:]), pair.dtype), pair[:, None], 0, y)
    for k, piece in arrived:
        held = put(held, piece[:, None], 0, (y - k) & 3)
    held = held.reshape(8, *pair.shape[1:])
    return held, lax.ppermute(held, "mp", CORE)


def collect(mine, theirs, through=None):
    y = mp_place()[1]
    other = lax.ppermute(theirs, "mp", CORE)
    held = (mine.astype(F32) + other.astype(F32)).astype(BF16).reshape(2, 4, *mine.shape[1:])
    arrived = [lax.ppermute(pick(held, (y + k) & 3, 1), "mp", AROUND_Y[k]) for k in (1, 3, 2)]
    own = pick(held, y, 1)
    if through is not None:
        own = through(own)
    total = own.astype(F32)
    for piece in arrived:
        total = total + piece.astype(F32)
    return total


def sum_pair(total):
    rounded = total.astype(BF16)
    return rounded.astype(F32) + lax.ppermute(rounded, "mp", FAR).astype(F32)


def sum_own(total):
    x_hi = mp_place()[0]
    other = lax.ppermute(pick(total, 1 - x_hi, 0).astype(BF16), "mp", FAR)
    return pick(total, x_hi, 0) + other.astype(F32)


def dp_bit(weight):
    return (lax.axis_index("dp") // weight) & 1


def swap_dp(weight, array):
    return lax.ppermute(array, "dp", [(i, i ^ weight) for i in range(16)])


def scatter_dp(order, total):
    step, low, high = order[1:]
    on = dp_bit(step)
    total = total.reshape(2, 4, *total.shape[1:])
    total = pick(total, on, 0) + swap_dp(step, pick(total, 1 - on, 0).astype(BF16)).astype(F32)
    place = dp_bit(low) * 2 + dp_bit(high)
    rounded = total.astype(BF16)
    arrived = [
        swap_dp(weight, pick(rounded, place ^ flips, 0))
        for flips, weight in ((3, low | high), (2, low), (1, high))
    ]
    total = pick(total, place, 0)
    for piece in arrived:
        total = total + piece.astype(F32)
    return total


def gather_dp(block):
    index = lax.axis_index("dp")
    x_lo, z = index >> 3, index & 7
    held = block[None]
    for bit in (2, 1, 0):
        other = lax.ppermute(held, "dp", [(i, i ^ (1 << bit)) for i in range(16)])
        on = ((z >> bit) & 1) == 1
        held = jnp.stack([jnp.where(on, other, held), jnp.where(on, held, other)], axis=held.ndim - 2)
    other = lax.ppermute(held, "dp", FAR)
    on = x_lo == 1
    held = jnp.stack([jnp.where(on, other, held), jnp.where(on, held, other)])
    return held.reshape(16, *block.shape)


def rows(start, size):
    return pl.ds(pl.multiple_of(start, 16), size)


def place(core, i, own, size):
    return rows((2 * i + (core if own else 1 - core)) * size, size)


def call(kernel, outs, *args, scratch=(), after=()):
    spec = pl.BlockSpec(memory_space=pltpu.VMEM)
    specs = [pl.BlockSpec(memory_space=pltpu.SMEM)] + [spec] * (len(args) - 1)
    skip = len(after)
    if skip:
        inner = kernel
        kernel = lambda *refs: inner(*refs[skip:])
    size = sum(math.prod(a.shape) * a.dtype.itemsize for a in args)
    size += sum(math.prod(shape) * jnp.dtype(dtype).itemsize for shape, dtype in outs)
    return pl.pallas_call(
        kernel,
        out_shape=tuple(jax.ShapeDtypeStruct(shape, dtype) for shape, dtype in outs),
        in_specs=[pl.BlockSpec(memory_space=pl.ANY)] * skip + specs,
        out_specs=(spec,) * len(outs),
        scratch_shapes=list(scratch),
        compiler_params=pltpu.CompilerParams(vmem_limit_bytes=VMEM_LIMIT),
        cost_estimate=pl.CostEstimate(flops=0, bytes_accessed=size, transcendentals=0),
    )(*after, *args)


def flip(block):
    return block.astype(F32).T.astype(BF16)


def send_out(core, full_ref, mine_ref, theirs_ref, size):
    for i in range(8):
        mine_ref[i] = full_ref[place(core, i, True, size)].astype(BF16)
        theirs_ref[i] = full_ref[place(core, i, False, size)].astype(BF16)


def take_in(core, held_ref, other_ref, full_ref, size):
    for i in range(8):
        full_ref[place(core, i, True, size)] = held_ref[i]
        full_ref[place(core, i, False, size)] = other_ref[i]


def block_kernel(core_ref, held_ref, other_ref, gain_ref, w_in_ref, w_out_ref,
                 z_ref, pre_ref, act_ref, stat_ref, mine_ref, theirs_ref, full_ref):
    core = core_ref[0]
    width = z_ref.shape[0]
    total = jnp.zeros((1, z_ref.shape[1]), F32)
    for i in range(8):
        for ref in (held_ref, other_ref):
            total = total + jnp.sum(ref[i, :BLOCK].astype(F32), axis=0, keepdims=True)
    mean = total / width
    total = jnp.zeros_like(mean)
    for i in range(8):
        for ref in (held_ref, other_ref):
            centred = ref[i, :BLOCK].astype(F32) - mean
            total = total + jnp.sum(centred * centred, axis=0, keepdims=True)
    inv_std = 1.0 / jnp.sqrt(total / width + 1e-06)
    stat_ref[...] = jnp.zeros_like(stat_ref)
    stat_ref[0:1] = mean
    stat_ref[1:2] = inv_std
    for i in range(8):
        for own, ref in ((True, held_ref), (False, other_ref)):
            at = place(core, i, own, BLOCK)
            normed = (ref[i, :BLOCK].astype(F32) - mean) * inv_std
            z_ref[at] = (normed * gain_ref[at]).astype(BF16)
    hidden = pre_ref.shape[0]
    pre = jnp.zeros(pre_ref.shape, F32)
    for start in range(0, width, hidden):
        pre = pre + dot(flip(w_in_ref[start : start + hidden]), z_ref[start : start + hidden])
    pre_ref[...] = pre
    act_ref[...] = gelu(pre).astype(BF16)
    for start in range(0, width, hidden):
        full_ref[start : start + hidden] = dot(flip(w_out_ref[:, start : start + hidden]), act_ref[...])
    send_out(core, full_ref, mine_ref, theirs_ref, BLOCK)


def adaptor_kernel(core_ref, held_ref, other_ref, adapt_t_ref, heads_t_ref,
                   h_ref, pre_ref, q_ref, mine_a_ref, theirs_a_ref, mine_b_ref, theirs_b_ref):
    core = core_ref[0]
    take_in(core, held_ref, other_ref, h_ref, BLOCK)
    pre = dot(adapt_t_ref[...], h_ref[...])
    pre_ref[...] = pre
    q_ref[...] = gelu(pre).astype(BF16)
    for i in range(8):
        for own, a_ref, b_ref in ((True, mine_a_ref, mine_b_ref), (False, theirs_a_ref, theirs_b_ref)):
            pred = dot(heads_t_ref[place(core, i, own, TEACH)], q_ref[...]).astype(BF16)
            a_ref[i] = pred[:PART]
            b_ref[i] = pred[PART:]


def adaptor_back_kernel(core_ref, held_a_ref, other_a_ref, held_b_ref, other_b_ref, heads_ref, pre_ref, adapt_t_ref,
                        err_ref, back_ref, mine_ref, theirs_ref, full_ref):
    core = core_ref[0]
    for i in range(8):
        for own, refs in ((True, (held_a_ref, held_b_ref)), (False, (other_a_ref, other_b_ref))):
            start = (2 * i + (core if own else 1 - core)) * TEACH
            for part in range(2):
                err_ref[rows(start + part * PART, PART)] = refs[part][i]
    lifted = dot(heads_ref[...], err_ref[...])
    back_ref[...] = (lifted * gelu_slope(pre_ref[...])).astype(BF16)
    for start in range(0, full_ref.shape[0], 512):
        full_ref[start : start + 512] = dot(flip(adapt_t_ref[:, start : start + 512]), back_ref[...])
    send_out(core, full_ref, mine_ref, theirs_ref, BLOCK)


def adaptor_grads_kernel(scale, widths, on_ref, err_ref, q_ref, h_ref, back_ref,
                         mine_ref, theirs_ref, ga_ref, go_ref):
    hid3 = q_ref.shape[0]
    hid = hid3 // 3
    ga_ref[...] = dot(h_ref[...], back_ref[...], 1, 1) * scale
    go_ref[...] = dot(err_ref[...], q_ref[...], 1, 1) * scale
    w0, w1, w2 = widths
    for j in range(8):
        for chunk, ref in sides(PACK_ORDER, on_ref[0], j, mine_ref, theirs_ref):
            at = rows(chunk * BLOCK, BLOCK)
            go = go_ref[rows(chunk * TEACH, TEACH)]
            ref[j, :BLOCK] = jnp.concatenate(
                [ga_ref[at], go[:BLOCK, :hid]], axis=1
            ).astype(BF16)
            second = go[w0 : w0 + w1, hid : 2 * hid]
            third = go[w0 + w1 : w0 + w1 + w2, 2 * hid :]
            second = jnp.concatenate([second, jnp.zeros((2 * LOW - w1, hid), F32)], axis=0)
            third = jnp.concatenate([third, jnp.zeros((2 * LOW - w2, hid), F32)], axis=0)
            ref[j, BLOCK:] = jnp.concatenate(
                [second[:LOW], third[:LOW], second[LOW:], third[LOW:]], axis=1
            ).astype(BF16)


def w_out_grad_kernel(scale, place_ref, ds_ref, act_ref, mine_ref, theirs_ref, full_ref):
    full_ref[...] = dot(ds_ref[...], act_ref[...], 1, 1) * scale
    halves(OUT_ORDER, place_ref[1], full_ref, mine_ref, theirs_ref)


def sides(order, on, j, mine_ref, theirs_ref):
    first, rest = order[0], order[1:]
    chunk = sum(weight * ((j >> (2 - i)) & 1) for i, weight in enumerate(rest))
    return ((on * first + chunk, mine_ref), ((1 - on) * first + chunk, theirs_ref))


def halves(order, on, full_ref, mine_ref, theirs_ref):
    for j in range(8):
        for chunk, ref in sides(order, on, j, mine_ref, theirs_ref):
            ref[j] = full_ref[rows(chunk * BLOCK, BLOCK)].astype(BF16)


def w_in_grad_kernel(scale, place_ref, z_ref, dpre_ref, mine_ref, theirs_ref, full_ref):
    full_ref[...] = dot(z_ref[...], dpre_ref[...], 1, 1) * scale
    halves(IN_ORDER, place_ref[2], full_ref, mine_ref, theirs_ref)


def block_back_kernel(core_ref, ds_held_ref, ds_other_ref, w_out_ref, pre_ref, w_in_ref, gain_ref,
                      held_ref, other_ref, stat_ref,
                      ds_ref, dpre_ref, mine_ref, theirs_ref, full_ref):
    core = core_ref[0]
    take_in(core, ds_held_ref, ds_other_ref, ds_ref, BLOCK)
    width = ds_ref.shape[0]
    dpre_ref[...] = (dot(w_out_ref[...], ds_ref[...]) * gelu_slope(pre_ref[...])).astype(BF16)
    full_ref[...] = dot(w_in_ref[...], dpre_ref[...])
    mean = stat_ref[0:1]
    inv_std = stat_ref[1:2]
    first = jnp.zeros_like(mean)
    second = jnp.zeros_like(mean)
    for i in range(8):
        for own, ref, out_ref in ((True, held_ref, mine_ref), (False, other_ref, theirs_ref)):
            at = place(core, i, own, BLOCK)
            dnorm = full_ref[at]
            out_ref[i, :BLOCK] = dnorm.astype(BF16)
            lifted = dnorm * gain_ref[at]
            normed = (ref[i, :BLOCK].astype(F32) - mean) * inv_std
            first = first + jnp.sum(lifted, axis=0, keepdims=True)
            second = second + jnp.sum(lifted * normed, axis=0, keepdims=True)
    sums = []
    for part in (first / width, second / width):
        high = part.astype(BF16).astype(F32)
        sums = sums + [high, part - high]
    sums = jnp.concatenate(sums + [jnp.zeros((SUMS - 4, mean.shape[1]), F32)], axis=0).astype(BF16)
    for i in range(8):
        mine_ref[i, BLOCK:] = sums
        theirs_ref[i, BLOCK:] = sums


def start_kernel(place_ref, tokens_ref, *refs):
    teach_refs, (pair_ref, block_ref) = refs[:3], refs[3:]
    pair_ref[...] = jnp.zeros_like(pair_ref)
    pair_ref[place_ref[0], :BLOCK] = tokens_ref[...]
    block_ref[...] = jnp.zeros_like(block_ref)
    for m in range(8):

        @pl.when(place_ref[1] == m)
        def _():
            for side in range(2):
                offset = side * TEACH
                for ref in teach_refs:
                    wide = ref.shape[1] // 16
                    start = (side * 8 + m) * wide
                    block_ref[:, offset : offset + wide] = ref[:, start : start + wide]
                    offset = offset + wide


def heads_kernel(_, own_ref, *refs):
    head_refs, (own_out_ref, heads_ref, heads_t_ref) = refs[:3], refs[3:]
    own_out_ref[...] = own_ref[...]
    hid = heads_ref.shape[0] // 3
    heads_ref[...] = jnp.zeros_like(heads_ref)
    for m in range(16):
        offset = m * TEACH
        for k in range(3):
            wide = head_refs[k].shape[1] // 16
            heads_ref[k * hid : (k + 1) * hid, offset : offset + wide] = head_refs[k][:, m * wide : (m + 1) * wide]
            offset = offset + wide
        heads_t_ref[m * TEACH : (m + 1) * TEACH] = flip(heads_ref[:, m * TEACH : (m + 1) * TEACH])


def add_kernel(_, mine_ref, other_ref, total_ref):
    total_ref[...] = mine_ref[...].astype(F32) + other_ref[...].astype(F32)


def body(
    tokens,
    ln_gain,
    w_in,
    w_out,
    adapt_in,
    out_dino,
    out_siglip,
    out_sam,
    teach_dino,
    teach_siglip,
    teach_sam,
    src_dev,
    src_row,
):
    heads = (out_dino, out_siglip, out_sam)
    teachers = (teach_dino, teach_siglip, teach_sam)
    n_rows = tokens.shape[0]
    n_mp = lax.axis_size("mp")
    n_dp = lax.axis_size("dp")
    width = BLOCK * n_mp
    hidden = w_in.shape[1]
    hid = adapt_in.shape[2]
    share = n_rows // n_mp
    short = [head.shape[1] // n_mp for head in heads]
    spare = TEACH - sum(short)
    scale = 1.0 / math.sqrt(n_rows * n_dp)
    x_hi, y, core = mp_place()
    at = jnp.stack([core, dp_bit(OUT_ORDER[0]), dp_bit(IN_ORDER[0])]).astype(jnp.int32)
    gain = ln_gain[:, None]

    with jax.named_scope("tokens"):
        own_tokens = tokens.T
        far_tokens = lax.ppermute(own_tokens, "mp", FAR)
        token_pair, block = call(
            start_kernel,
            [((2, BLOCK + EXTRA, n_rows), BF16), ((teach_dino.shape[0], 2 * TEACH), BF16)],
            jnp.stack([x_hi, y * 2 + core]).astype(jnp.int32), own_tokens, *teachers,
        )
        sources = jnp.concatenate([src_dev, src_row], axis=1).T.astype(BF16)
        sources = jnp.pad(sources, ((0, EXTRA - 4), (0, n_rows - share)))
        token_pair = put(token_pair, far_tokens[None], 1 - x_hi)
        token_pair = put(token_pair, sources[None], x_hi, BLOCK)
        token_pair = put(token_pair, lax.ppermute(sources, "mp", FAR)[None], 1 - x_hi, BLOCK)
        x_held, x_other = spread(token_pair)

    more = []

    def more_weights(own):
        own, *rest = call(
            heads_kernel,
            [
                (own.shape, BF16),
                ((3 * hid, n_mp * TEACH), BF16),
                ((n_mp * TEACH, 3 * hid), BF16),
            ],
            at, own, *heads,
        )
        more.extend(rest)
        return own

    with jax.named_scope("block"):
        z, pre_mlp, act, stat, mine, theirs = call(
            block_kernel,
            [
                ((width, n_rows), BF16),
                ((hidden, n_rows), F32),
                ((hidden, n_rows), BF16),
                ((8, n_rows), F32),
                ((8, BLOCK, n_rows), BF16),
                ((8, BLOCK, n_rows), BF16),
            ],
            at, x_held, x_other, gain, w_in, w_out,
            scratch=[pltpu.VMEM((width, n_rows), F32)],
        )
        state = sum_pair(collect(mine, theirs, more_weights)) + token_pair[:, :BLOCK].astype(F32)
        h_held, h_other = spread(state.astype(BF16))

    with jax.named_scope("targets"):
        heads_all, heads_t = more
        adapt_t = adapt_in.transpose(0, 2, 1).reshape(3 * hid, width)
        pool = gather_dp(block).reshape(-1, 2 * TEACH)
        mixed = [a[:, BLOCK : BLOCK + 4, :share] for a in (x_held, x_other)]
        mixed = jnp.stack(
            [jnp.where(core == 0, mixed[0], mixed[1]), jnp.where(core == 0, mixed[1], mixed[0])], axis=1
        )
        source = mixed.transpose(2, 0, 1, 3).reshape(4, n_rows).astype(jnp.int32)
        places = jnp.arange(pool.shape[0], dtype=jnp.int32)[:, None]
        spots = source[:1] * teach_dino.shape[0] + source[1:]
        target = []
        for side in range(2):
            offset = side * TEACH
            for k in range(3):
                chosen = (places == spots[k : k + 1]).astype(BF16)
                target.append(dot(pool[:, offset : offset + short[k]], chosen, 0, 0))
                offset = offset + short[k]
            target.append(jnp.zeros((spare, n_rows), F32))
        target = jnp.concatenate(target, axis=0).reshape(2, TEACH, n_rows).astype(BF16)

    with jax.named_scope("adaptors"):
        h, pre_adapt, q, *sent = call(
            adaptor_kernel,
            [
                ((width, n_rows), BF16),
                ((3 * hid, n_rows), F32),
                ((3 * hid, n_rows), BF16),
            ]
            + [((8, PART, n_rows), BF16)] * 4,
            at, h_held, h_other, adapt_t, heads_t,
        )
        errors = []
        for part in range(2):
            pred = sum_pair(collect(*sent[2 * part : 2 * part + 2]))
            error = pred - target[:, part * PART : (part + 1) * PART].astype(F32)
            errors.extend(spread(error.astype(BF16)))

    with jax.named_scope("adaptors_back"):
        err, back, mine, theirs = call(
            adaptor_back_kernel,
            [
                ((n_mp * TEACH, n_rows), BF16),
                ((3 * hid, n_rows), BF16),
                ((8, BLOCK, n_rows), BF16),
                ((8, BLOCK, n_rows), BF16),
            ],
            at, *errors, heads_all, pre_adapt, adapt_t,
            scratch=[pltpu.VMEM((width, n_rows), F32)],
        )
        packs = []

        def adaptor_grads(own):
            packs.extend(
                call(
                    functools.partial(adaptor_grads_kernel, scale, short),
                    [((8, BLOCK + LOW, 4 * hid), BF16)] * 2,
                    dp_bit(PACK_ORDER[0])[None].astype(jnp.int32), err, q, h, back,
                    scratch=[
                        pltpu.VMEM((width, 3 * hid), F32),
                        pltpu.VMEM((n_mp * TEACH, 3 * hid), F32),
                    ],
                    after=(own,),
                )
            )
            return own

        dstate = sum_pair(collect(mine, theirs, adaptor_grads))
        d_held, d_other = spread(dstate.astype(BF16))

    with jax.named_scope("block_back"):
        ds, dpre, mine, theirs = call(
            block_back_kernel,
            [((width, n_rows), BF16), ((hidden, n_rows), BF16)]
            + [((8, BLOCK + SUMS, n_rows), BF16)] * 2,
            at, d_held, d_other, w_out, pre_mlp, w_in, gain, x_held, x_other, stat,
            scratch=[pltpu.VMEM((width, n_rows), F32)],
        )
        ins = call(
            functools.partial(w_in_grad_kernel, scale),
            [((8, BLOCK, hidden), BF16)] * 2,
            at, z, dpre,
            scratch=[pltpu.VMEM((width, hidden), F32)],
        )
        outs = call(
            functools.partial(w_out_grad_kernel, scale),
            [((8, BLOCK, hidden), BF16)] * 2,
            at, ds, act,
            scratch=[pltpu.VMEM((width, hidden), F32)],
            after=(ins[0],),
        )
        sums = []

        def first_sums(own):
            for order, (kept, sent) in ((PACK_ORDER, packs), (IN_ORDER, ins), (OUT_ORDER, outs)):
                sums.extend(
                    call(add_kernel, [(kept.shape, F32)], at, kept, swap_dp(order[0], sent), after=(own,))
                )
            return own

        summed = sum_own(collect(mine, theirs, first_sums))
        gain_own = lax.dynamic_slice_in_dim(ln_gain, lax.axis_index("mp") * BLOCK, BLOCK, 0)
        normed = (tokens.T.astype(F32) - stat[0:1]) * stat[1:2]
        dnorm = summed[:BLOCK] * gain_own[:, None]
        first = summed[BLOCK : BLOCK + 1] + summed[BLOCK + 1 : BLOCK + 2]
        second = summed[BLOCK + 2 : BLOCK + 3] + summed[BLOCK + 3 : BLOCK + 4]
        grad_tokens = pick(dstate, x_hi, 0) + stat[1:2] * (dnorm - first - normed * second)

    with jax.named_scope("weight_sums"):
        pack = scatter_dp(PACK_ORDER, sums[0])
        grad_w_in = scatter_dp(IN_ORDER, sums[1])
        grad_w_out = scatter_dp(OUT_ORDER, sums[2])

    tail = pack[BLOCK:]
    second = jnp.concatenate([tail[:, :hid], tail[:, 2 * hid : 3 * hid]], axis=0)
    third = jnp.concatenate([tail[:, hid : 2 * hid], tail[:, 3 * hid :]], axis=0)
    return (
        grad_tokens.T,
        grad_w_in,
        grad_w_out.T,
        jnp.stack([pack[:BLOCK, k * hid : (k + 1) * hid] for k in range(3)]),
        pack[:BLOCK, 3 * hid :].T,
        second[: short[1]].T,
        third[: short[2]].T,
    )


def solution(mesh):
    placed = (
        P("dp", "mp"),
        P(),
        P(None, "mp"),
        P("mp", None),
        P(None, None, "mp"),
        P("mp", None),
        P("mp", None),
        P("mp", None),
        P("dp", None),
        P("dp", None),
        P("dp", None),
        P(("dp", "mp"), None),
        P(("dp", "mp"), None),
    )
    return jax.shard_map(
        body,
        mesh=mesh,
        in_specs=placed,
        out_specs=(
            P("dp", "mp"),
            P("dp", "mp"),
            P("mp", "dp"),
            P(None, "dp", "mp"),
            P("mp", "dp"),
            P("mp", "dp"),
            P("mp", "dp"),
        ),
        check_vma=False,
    )
```

```python
import functools
import math

import jax
import jax.numpy as jnp
from jax import lax
from jax.experimental import pallas as pl
from jax.experimental.pallas import tpu as pltpu
from jax.sharding import PartitionSpec as P

F32 = jnp.float32
BF16 = jnp.bfloat16
VMEM_LIMIT = 20 * 1024 * 1024
PACK_ORDER = (1, 8, 2, 4)
OUT_ORDER = (1, 8, 2, 4)
IN_ORDER = (8, 1, 2, 4)

CORE = [(i, i ^ 1) for i in range(16)]
FAR = [(i, i ^ 8) for i in range(16)]
AROUND_Y = [[(i, (i & 9) | ((((i >> 1 & 3) + k) & 3) << 1)) for i in range(16)] for k in range(4)]

BLOCK = 96
TEACH = 256
PART = 128
EXTRA = 8
SUMS = 16
LOW = 48


def gelu(value):
    return 0.5 * value * (1.0 + lax.erf(value * 0.7071067811865476))


def gelu_slope(value):
    return (
        0.5 * (1.0 + lax.erf(value * 0.7071067811865476))
        + value * jnp.exp(-0.5 * value * value) * 0.3989422804014327
    )


def dot(left, right, over_left=1, over_right=0):
    return lax.dot_general(
        left, right, (((over_left,), (over_right,)), ((), ())), preferred_element_type=F32
    )


def pick(array, index, axis):
    return lax.dynamic_index_in_dim(array, index, axis, keepdims=False)


def put(buffer, piece, *at):
    return lax.dynamic_update_slice(buffer, piece, at + (0,) * (buffer.ndim - len(at)))


def mp_place():
    index = lax.axis_index("mp")
    return index >> 3, (index >> 1) & 3, index & 1


def spread(pair, through=None):
    y = mp_place()[1]
    arrived = [(k, lax.ppermute(pair, "mp", AROUND_Y[k])) for k in (1, 3, 2)]
    if through is not None:
        pair = through(pair)
    held = put(jnp.zeros((2, 4, *pair.shape[1:]), pair.dtype), pair[:, None], 0, y)
    for k, piece in arrived:
        held = put(held, piece[:, None], 0, (y - k) & 3)
    held = held.reshape(8, *pair.shape[1:])
    return held, lax.ppermute(held, "mp", CORE)


def collect(mine, theirs, through=None):
    y = mp_place()[1]
    other = lax.ppermute(theirs, "mp", CORE)
    held = (mine.astype(F32) + other.astype(F32)).astype(BF16).reshape(2, 4, *mine.shape[1:])
    arrived = [lax.ppermute(pick(held, (y + k) & 3, 1), "mp", AROUND_Y[k]) for k in (1, 3, 2)]
    own = pick(held, y, 1)
    if through is not None:
        own = through(own)
    total = own.astype(F32)
    for piece in arrived:
        total = total + piece.astype(F32)
    return total


def sum_pair(total):
    rounded = total.astype(BF16)
    return rounded.astype(F32) + lax.ppermute(rounded, "mp", FAR).astype(F32)


def sum_own(total):
    x_hi = mp_place()[0]
    other = lax.ppermute(pick(total, 1 - x_hi, 0).astype(BF16), "mp", FAR)
    return pick(total, x_hi, 0) + other.astype(F32)


def dp_bit(weight):
    return (lax.axis_index("dp") // weight) & 1


def swap_dp(weight, array):
    return lax.ppermute(array, "dp", [(i, i ^ weight) for i in range(16)])


def halve_dp(weight, total):
    on = dp_bit(weight)
    total = total.reshape(2, -1, *total.shape[1:])
    return pick(total, on, 0), swap_dp(weight, pick(total, 1 - on, 0).astype(BF16))


def finish_dp(order, total):
    low, high = order[2:]
    place = dp_bit(low) * 2 + dp_bit(high)
    rounded = total.astype(BF16)
    arrived = [
        swap_dp(weight, pick(rounded, place ^ flips, 0))
        for flips, weight in ((3, low | high), (2, low), (1, high))
    ]
    total = pick(total, place, 0)
    for piece in arrived:
        total = total + piece.astype(F32)
    return total


def scatter_dp(order, total):
    kept, other = halve_dp(order[1], total)
    return finish_dp(order, kept + other.astype(F32))


def gather_dp(block):
    index = lax.axis_index("dp")
    x_lo, z = index >> 3, index & 7
    held = block[None]
    for bit in (2, 1, 0):
        other = lax.ppermute(held, "dp", [(i, i ^ (1 << bit)) for i in range(16)])
        on = ((z >> bit) & 1) == 1
        held = jnp.stack([jnp.where(on, other, held), jnp.where(on, held, other)], axis=held.ndim - 2)
    other = lax.ppermute(held, "dp", FAR)
    on = x_lo == 1
    held = jnp.stack([jnp.where(on, other, held), jnp.where(on, held, other)])
    return held.reshape(16, *block.shape)


def rows(start, size):
    return pl.ds(pl.multiple_of(start, 16), size)


def place(core, i, own, size):
    return rows((2 * i + (core if own else 1 - core)) * size, size)


def call(kernel, outs, *args, scratch=(), after=()):
    spec = pl.BlockSpec(memory_space=pltpu.VMEM)
    specs = [pl.BlockSpec(memory_space=pltpu.SMEM)] + [spec] * (len(args) - 1)
    skip = len(after)
    if skip:
        inner = kernel
        kernel = lambda *refs: inner(*refs[skip:])
    size = sum(math.prod(a.shape) * a.dtype.itemsize for a in args)
    size += sum(math.prod(shape) * jnp.dtype(dtype).itemsize for shape, dtype in outs)
    return pl.pallas_call(
        kernel,
        out_shape=tuple(jax.ShapeDtypeStruct(shape, dtype) for shape, dtype in outs),
        in_specs=[pl.BlockSpec(memory_space=pl.ANY)] * skip + specs,
        out_specs=(spec,) * len(outs),
        scratch_shapes=list(scratch),
        compiler_params=pltpu.CompilerParams(vmem_limit_bytes=VMEM_LIMIT),
        cost_estimate=pl.CostEstimate(flops=0, bytes_accessed=size, transcendentals=0),
    )(*after, *args)


def flip(block):
    return block.astype(F32).T.astype(BF16)


def send_out(core, full_ref, mine_ref, theirs_ref, size):
    for i in range(8):
        mine_ref[i] = full_ref[place(core, i, True, size)].astype(BF16)
        theirs_ref[i] = full_ref[place(core, i, False, size)].astype(BF16)


def take_in(core, held_ref, other_ref, full_ref, size):
    for i in range(8):
        full_ref[place(core, i, True, size)] = held_ref[i]
        full_ref[place(core, i, False, size)] = other_ref[i]


def block_kernel(core_ref, held_ref, other_ref, gain_ref, w_in_ref, w_out_ref,
                 z_ref, pre_ref, act_ref, stat_ref, mine_ref, theirs_ref, full_ref):
    core = core_ref[0]
    width = z_ref.shape[0]
    total = jnp.zeros((1, z_ref.shape[1]), F32)
    for i in range(8):
        for ref in (held_ref, other_ref):
            total = total + jnp.sum(ref[i, :BLOCK].astype(F32), axis=0, keepdims=True)
    mean = total / width
    total = jnp.zeros_like(mean)
    for i in range(8):
        for ref in (held_ref, other_ref):
            centred = ref[i, :BLOCK].astype(F32) - mean
            total = total + jnp.sum(centred * centred, axis=0, keepdims=True)
    inv_std = 1.0 / jnp.sqrt(total / width + 1e-06)
    stat_ref[...] = jnp.zeros_like(stat_ref)
    stat_ref[0:1] = mean
    stat_ref[1:2] = inv_std
    for i in range(8):
        for own, ref in ((True, held_ref), (False, other_ref)):
            at = place(core, i, own, BLOCK)
            normed = (ref[i, :BLOCK].astype(F32) - mean) * inv_std
            z_ref[at] = (normed * gain_ref[at]).astype(BF16)
    hidden = pre_ref.shape[0]
    pre = jnp.zeros(pre_ref.shape, F32)
    for start in range(0, width, hidden):
        pre = pre + dot(flip(w_in_ref[start : start + hidden]), z_ref[start : start + hidden])
    pre_ref[...] = pre
    act_ref[...] = gelu(pre).astype(BF16)
    for start in range(0, width, hidden):
        full_ref[start : start + hidden] = dot(flip(w_out_ref[:, start : start + hidden]), act_ref[...])
    send_out(core, full_ref, mine_ref, theirs_ref, BLOCK)


def adaptor_kernel(core_ref, held_ref, other_ref, adapt_t_ref, heads_t_ref,
                   h_ref, pre_ref, q_ref, mine_a_ref, theirs_a_ref, mine_b_ref, theirs_b_ref):
    core = core_ref[0]
    take_in(core, held_ref, other_ref, h_ref, BLOCK)
    pre = dot(adapt_t_ref[...], h_ref[...])
    pre_ref[...] = pre
    q_ref[...] = gelu(pre).astype(BF16)
    for i in range(8):
        for own, a_ref, b_ref in ((True, mine_a_ref, mine_b_ref), (False, theirs_a_ref, theirs_b_ref)):
            pred = dot(heads_t_ref[place(core, i, own, TEACH)], q_ref[...]).astype(BF16)
            a_ref[i] = pred[:PART]
            b_ref[i] = pred[PART:]


def adaptor_back_kernel(core_ref, held_a_ref, other_a_ref, held_b_ref, other_b_ref, heads_ref, pre_ref, adapt_t_ref,
                        err_ref, back_ref, mine_ref, theirs_ref, full_ref):
    core = core_ref[0]
    for i in range(8):
        for own, refs in ((True, (held_a_ref, held_b_ref)), (False, (other_a_ref, other_b_ref))):
            start = (2 * i + (core if own else 1 - core)) * TEACH
            for part in range(2):
                err_ref[rows(start + part * PART, PART)] = refs[part][i]
    lifted = dot(heads_ref[...], err_ref[...])
    back_ref[...] = (lifted * gelu_slope(pre_ref[...])).astype(BF16)
    for start in range(0, full_ref.shape[0], 512):
        full_ref[start : start + 512] = dot(flip(adapt_t_ref[:, start : start + 512]), back_ref[...])
    send_out(core, full_ref, mine_ref, theirs_ref, BLOCK)


def adaptor_grads_kernel(scale, widths, on_ref, pair_ref, err_ref, q_ref, h_ref, back_ref,
                         pair_out_ref, mine_ref, theirs_ref, ga_ref, go_ref):
    pair_out_ref[...] = pair_ref[...]
    hid3 = q_ref.shape[0]
    hid = hid3 // 3
    ga_ref[...] = dot(h_ref[...], back_ref[...], 1, 1) * scale
    go_ref[...] = dot(err_ref[...], q_ref[...], 1, 1) * scale
    w0, w1, w2 = widths
    for j in range(8):
        for chunk, ref in sides(PACK_ORDER, on_ref[0], j, mine_ref, theirs_ref):
            at = rows(chunk * BLOCK, BLOCK)
            go = go_ref[rows(chunk * TEACH, TEACH)]
            ref[j, :BLOCK] = jnp.concatenate(
                [ga_ref[at], go[:BLOCK, :hid]], axis=1
            ).astype(BF16)
            second = go[w0 : w0 + w1, hid : 2 * hid]
            third = go[w0 + w1 : w0 + w1 + w2, 2 * hid :]
            second = jnp.concatenate([second, jnp.zeros((2 * LOW - w1, hid), F32)], axis=0)
            third = jnp.concatenate([third, jnp.zeros((2 * LOW - w2, hid), F32)], axis=0)
            ref[j, BLOCK:] = jnp.concatenate(
                [second[:LOW], third[:LOW], second[LOW:], third[LOW:]], axis=1
            ).astype(BF16)


def w_out_grad_kernel(scale, place_ref, ds_ref, act_ref, mine_ref, theirs_ref, full_ref):
    full_ref[...] = dot(ds_ref[...], act_ref[...], 1, 1) * scale
    halves(OUT_ORDER, place_ref[1], full_ref, mine_ref, theirs_ref)


def sides(order, on, j, mine_ref, theirs_ref):
    first, rest = order[0], order[1:]
    chunk = sum(weight * ((j >> (2 - i)) & 1) for i, weight in enumerate(rest))
    return ((on * first + chunk, mine_ref), ((1 - on) * first + chunk, theirs_ref))


def halves(order, on, full_ref, mine_ref, theirs_ref):
    for j in range(8):
        for chunk, ref in sides(order, on, j, mine_ref, theirs_ref):
            ref[j] = full_ref[rows(chunk * BLOCK, BLOCK)].astype(BF16)


def w_in_grad_kernel(scale, place_ref, z_ref, dpre_ref, kept_ref, other_ref,
                     mine_ref, theirs_ref, total_ref, full_ref):
    full_ref[...] = dot(z_ref[...], dpre_ref[...], 1, 1) * scale
    halves(IN_ORDER, place_ref[2], full_ref, mine_ref, theirs_ref)
    total_ref[...] = kept_ref[...].astype(F32) + other_ref[...].astype(F32)


def block_back_kernel(core_ref, ds_held_ref, ds_other_ref, w_out_ref, pre_ref, w_in_ref, gain_ref,
                      held_ref, other_ref, stat_ref,
                      ds_ref, dpre_ref, mine_ref, theirs_ref, full_ref):
    core = core_ref[0]
    take_in(core, ds_held_ref, ds_other_ref, ds_ref, BLOCK)
    width = ds_ref.shape[0]
    dpre_ref[...] = (dot(w_out_ref[...], ds_ref[...]) * gelu_slope(pre_ref[...])).astype(BF16)
    full_ref[...] = dot(w_in_ref[...], dpre_ref[...])
    mean = stat_ref[0:1]
    inv_std = stat_ref[1:2]
    first = jnp.zeros_like(mean)
    second = jnp.zeros_like(mean)
    for i in range(8):
        for own, ref, out_ref in ((True, held_ref, mine_ref), (False, other_ref, theirs_ref)):
            at = place(core, i, own, BLOCK)
            dnorm = full_ref[at]
            out_ref[i, :BLOCK] = dnorm.astype(BF16)
            lifted = dnorm * gain_ref[at]
            normed = (ref[i, :BLOCK].astype(F32) - mean) * inv_std
            first = first + jnp.sum(lifted, axis=0, keepdims=True)
            second = second + jnp.sum(lifted * normed, axis=0, keepdims=True)
    sums = []
    for part in (first / width, second / width):
        high = part.astype(BF16).astype(F32)
        sums = sums + [high, part - high]
    sums = jnp.concatenate(sums + [jnp.zeros((SUMS - 4, mean.shape[1]), F32)], axis=0).astype(BF16)
    for i in range(8):
        mine_ref[i, BLOCK:] = sums
        theirs_ref[i, BLOCK:] = sums


def start_kernel(place_ref, tokens_ref, *refs):
    teach_refs, (pair_ref, block_ref) = refs[:3], refs[3:]
    pair_ref[...] = jnp.zeros_like(pair_ref)
    pair_ref[place_ref[0], :BLOCK] = tokens_ref[...]
    block_ref[...] = jnp.zeros_like(block_ref)
    for m in range(8):

        @pl.when(place_ref[1] == m)
        def _():
            for side in range(2):
                offset = side * TEACH
                for ref in teach_refs:
                    wide = ref.shape[1] // 16
                    start = (side * 8 + m) * wide
                    block_ref[:, offset : offset + wide] = ref[:, start : start + wide]
                    offset = offset + wide


def heads_kernel(_, own_ref, block_ref, *refs):
    head_refs, (own_out_ref, block_out_ref, heads_ref, heads_t_ref) = refs[:3], refs[3:]
    own_out_ref[...] = own_ref[...]
    block_out_ref[...] = block_ref[...]
    hid = heads_ref.shape[0] // 3
    heads_ref[...] = jnp.zeros_like(heads_ref)
    for m in range(16):
        offset = m * TEACH
        for k in range(3):
            wide = head_refs[k].shape[1] // 16
            heads_ref[k * hid : (k + 1) * hid, offset : offset + wide] = head_refs[k][:, m * wide : (m + 1) * wide]
            offset = offset + wide
        heads_t_ref[m * TEACH : (m + 1) * TEACH] = flip(heads_ref[:, m * TEACH : (m + 1) * TEACH])


def add_kernel(_, mine_ref, other_ref, total_ref):
    total_ref[...] = mine_ref[...].astype(F32) + other_ref[...].astype(F32)


def body(
    tokens,
    ln_gain,
    w_in,
    w_out,
    adapt_in,
    out_dino,
    out_siglip,
    out_sam,
    teach_dino,
    teach_siglip,
    teach_sam,
    src_dev,
    src_row,
):
    heads = (out_dino, out_siglip, out_sam)
    teachers = (teach_dino, teach_siglip, teach_sam)
    n_rows = tokens.shape[0]
    n_mp = lax.axis_size("mp")
    n_dp = lax.axis_size("dp")
    width = BLOCK * n_mp
    hidden = w_in.shape[1]
    hid = adapt_in.shape[2]
    share = n_rows // n_mp
    short = [head.shape[1] // n_mp for head in heads]
    spare = TEACH - sum(short)
    scale = 1.0 / math.sqrt(n_rows * n_dp)
    x_hi, y, core = mp_place()
    at = jnp.stack([core, dp_bit(OUT_ORDER[0]), dp_bit(IN_ORDER[0])]).astype(jnp.int32)
    gain = ln_gain[:, None]

    with jax.named_scope("tokens"):
        own_tokens = tokens.T
        far_tokens = lax.ppermute(own_tokens, "mp", FAR)
        token_pair, block = call(
            start_kernel,
            [((2, BLOCK + EXTRA, n_rows), BF16), ((teach_dino.shape[0], 2 * TEACH), BF16)],
            jnp.stack([x_hi, y * 2 + core]).astype(jnp.int32), own_tokens, *teachers,
        )
        sources = jnp.concatenate([src_dev, src_row], axis=1).T.astype(BF16)
        sources = jnp.pad(sources, ((0, EXTRA - 4), (0, n_rows - share)))
        token_pair = put(token_pair, far_tokens[None], 1 - x_hi)
        token_pair = put(token_pair, sources[None], x_hi, BLOCK)
        token_pair = put(token_pair, lax.ppermute(sources, "mp", FAR)[None], 1 - x_hi, BLOCK)
        x_held, x_other = spread(token_pair)

    more = []

    def more_weights(own):
        own, *rest = call(
            heads_kernel,
            [
                (own.shape, BF16),
                (block.shape, BF16),
                ((3 * hid, n_mp * TEACH), BF16),
                ((n_mp * TEACH, 3 * hid), BF16),
            ],
            at, own, block, *heads,
        )
        more.extend(rest)
        return own

    with jax.named_scope("block"):
        z, pre_mlp, act, stat, mine, theirs = call(
            block_kernel,
            [
                ((width, n_rows), BF16),
                ((hidden, n_rows), F32),
                ((hidden, n_rows), BF16),
                ((8, n_rows), F32),
                ((8, BLOCK, n_rows), BF16),
                ((8, BLOCK, n_rows), BF16),
            ],
            at, x_held, x_other, gain, w_in, w_out,
            scratch=[pltpu.VMEM((width, n_rows), F32)],
        )
        state = sum_pair(collect(mine, theirs, more_weights)) + token_pair[:, :BLOCK].astype(F32)
        h_held, h_other = spread(state.astype(BF16))

    with jax.named_scope("targets"):
        block_later, heads_all, heads_t = more
        adapt_t = adapt_in.transpose(0, 2, 1).reshape(3 * hid, width)
        pool = gather_dp(block_later).reshape(-1, 2 * TEACH)
        mixed = [a[:, BLOCK : BLOCK + 4, :share] for a in (x_held, x_other)]
        mixed = jnp.stack(
            [jnp.where(core == 0, mixed[0], mixed[1]), jnp.where(core == 0, mixed[1], mixed[0])], axis=1
        )
        source = mixed.transpose(2, 0, 1, 3).reshape(4, n_rows).astype(jnp.int32)
        places = jnp.arange(pool.shape[0], dtype=jnp.int32)[:, None]
        spots = source[:1] * teach_dino.shape[0] + source[1:]
        target = []
        for side in range(2):
            offset = side * TEACH
            for k in range(3):
                chosen = (places == spots[k : k + 1]).astype(BF16)
                target.append(dot(pool[:, offset : offset + short[k]], chosen, 0, 0))
                offset = offset + short[k]
            target.append(jnp.zeros((spare, n_rows), F32))
        target = jnp.concatenate(target, axis=0).reshape(2, TEACH, n_rows).astype(BF16)

    with jax.named_scope("adaptors"):
        h, pre_adapt, q, *sent = call(
            adaptor_kernel,
            [
                ((width, n_rows), BF16),
                ((3 * hid, n_rows), F32),
                ((3 * hid, n_rows), BF16),
            ]
            + [((8, PART, n_rows), BF16)] * 4,
            at, h_held, h_other, adapt_t, heads_t,
        )
        errors = []
        for part in range(2):
            pred = sum_pair(collect(*sent[2 * part : 2 * part + 2]))
            error = pred - target[:, part * PART : (part + 1) * PART].astype(F32)
            errors.extend(spread(error.astype(BF16)))

    with jax.named_scope("adaptors_back"):
        err, back, mine, theirs = call(
            adaptor_back_kernel,
            [
                ((n_mp * TEACH, n_rows), BF16),
                ((3 * hid, n_rows), BF16),
                ((8, BLOCK, n_rows), BF16),
                ((8, BLOCK, n_rows), BF16),
            ],
            at, *errors, heads_all, pre_adapt, adapt_t,
            scratch=[pltpu.VMEM((width, n_rows), F32)],
        )
        packs = []

        def adaptor_grads(pair):
            pair, kept, sent = call(
                functools.partial(adaptor_grads_kernel, scale, short),
                [(pair.shape, BF16)] + [((8, BLOCK + LOW, 4 * hid), BF16)] * 2,
                dp_bit(PACK_ORDER[0])[None].astype(jnp.int32), pair, err, q, h, back,
                scratch=[
                    pltpu.VMEM((width, 3 * hid), F32),
                    pltpu.VMEM((n_mp * TEACH, 3 * hid), F32),
                ],
            )
            packs.extend((kept, swap_dp(PACK_ORDER[0], sent)))
            return pair

        dstate = sum_pair(collect(mine, theirs))
        d_held, d_other = spread(dstate.astype(BF16), adaptor_grads)

    with jax.named_scope("block_back"):
        ds, dpre, mine, theirs = call(
            block_back_kernel,
            [((width, n_rows), BF16), ((hidden, n_rows), BF16)]
            + [((8, BLOCK + SUMS, n_rows), BF16)] * 2,
            at, d_held, d_other, w_out, pre_mlp, w_in, gain, x_held, x_other, stat,
            scratch=[pltpu.VMEM((width, n_rows), F32)],
        )
        *ins, pack = call(
            functools.partial(w_in_grad_kernel, scale),
            [((8, BLOCK, hidden), BF16)] * 2 + [((8, BLOCK + LOW, 4 * hid), F32)],
            at, z, dpre, *packs,
            scratch=[pltpu.VMEM((width, hidden), F32)],
        )
        outs = call(
            functools.partial(w_out_grad_kernel, scale),
            [((8, BLOCK, hidden), BF16)] * 2,
            at, ds, act,
            scratch=[pltpu.VMEM((width, hidden), F32)],
            after=(ins[0],),
        )
        sums = []

        def first_sums(own):
            for order, (kept, sent) in ((IN_ORDER, ins), (OUT_ORDER, outs)):
                sums.extend(
                    call(add_kernel, [(kept.shape, F32)], at, kept, swap_dp(order[0], sent), after=(own, *sums))
                )
            return own

        pack_kept, pack_other = halve_dp(PACK_ORDER[1], pack)
        partial = collect(mine, theirs, first_sums)
        (pack,) = call(
            add_kernel, [(pack_kept.shape, F32)], at, pack_kept, pack_other, after=(partial, *sums)
        )
        summed = sum_own(partial)
        gain_own = lax.dynamic_slice_in_dim(ln_gain, lax.axis_index("mp") * BLOCK, BLOCK, 0)
        normed = (tokens.T.astype(F32) - stat[0:1]) * stat[1:2]
        dnorm = summed[:BLOCK] * gain_own[:, None]
        first = summed[BLOCK : BLOCK + 1] + summed[BLOCK + 1 : BLOCK + 2]
        second = summed[BLOCK + 2 : BLOCK + 3] + summed[BLOCK + 3 : BLOCK + 4]
        grad_tokens = pick(dstate, x_hi, 0) + stat[1:2] * (dnorm - first - normed * second)

    with jax.named_scope("weight_sums"):
        pack = finish_dp(PACK_ORDER, pack)
        grad_w_in = scatter_dp(IN_ORDER, sums[0])
        grad_w_out = scatter_dp(OUT_ORDER, sums[1])

    tail = pack[BLOCK:]
    second = jnp.concatenate([tail[:, :hid], tail[:, 2 * hid : 3 * hid]], axis=0)
    third = jnp.concatenate([tail[:, hid : 2 * hid], tail[:, 3 * hid :]], axis=0)
    return (
        grad_tokens.T,
        grad_w_in,
        grad_w_out.T,
        jnp.stack([pack[:BLOCK, k * hid : (k + 1) * hid] for k in range(3)]),
        pack[:BLOCK, 3 * hid :].T,
        second[: short[1]].T,
        third[: short[2]].T,
    )


def solution(mesh):
    placed = (
        P("dp", "mp"),
        P(),
        P(None, "mp"),
        P("mp", None),
        P(None, None, "mp"),
        P("mp", None),
        P("mp", None),
        P("mp", None),
        P("dp", None),
        P("dp", None),
        P("dp", None),
        P(("dp", "mp"), None),
        P(("dp", "mp"), None),
    )
    return jax.shard_map(
        body,
        mesh=mesh,
        in_specs=placed,
        out_specs=(
            P("dp", "mp"),
            P("dp", "mp"),
            P("mp", "dp"),
            P(None, "dp", "mp"),
            P("mp", "dp"),
            P("mp", "dp"),
            P("mp", "dp"),
        ),
        check_vma=False,
    )
```

```python
import functools
import math

import jax
import jax.numpy as jnp
from jax import lax
from jax.experimental import pallas as pl
from jax.experimental.pallas import tpu as pltpu
from jax.sharding import PartitionSpec as P

F32 = jnp.float32
BF16 = jnp.bfloat16
VMEM_LIMIT = 20 * 1024 * 1024
PACK_ORDER = (1, 8, 2, 4)
OUT_ORDER = (1, 8, 2, 4)
IN_ORDER = (8, 1, 2, 4)

CORE = [(i, i ^ 1) for i in range(16)]
FAR = [(i, i ^ 8) for i in range(16)]
AROUND_Y = [[(i, (i & 9) | ((((i >> 1 & 3) + k) & 3) << 1)) for i in range(16)] for k in range(4)]

BLOCK = 96
TEACH = 256
PART = 128
EXTRA = 8
SUMS = 16
LOW = 48


def gelu(value):
    return 0.5 * value * (1.0 + lax.erf(value * 0.7071067811865476))


def gelu_slope(value):
    return (
        0.5 * (1.0 + lax.erf(value * 0.7071067811865476))
        + value * jnp.exp(-0.5 * value * value) * 0.3989422804014327
    )


def dot(left, right, over_left=1, over_right=0):
    return lax.dot_general(
        left, right, (((over_left,), (over_right,)), ((), ())), preferred_element_type=F32
    )


def pick(array, index, axis):
    return lax.dynamic_index_in_dim(array, index, axis, keepdims=False)


def put(buffer, piece, *at):
    return lax.dynamic_update_slice(buffer, piece, at + (0,) * (buffer.ndim - len(at)))


def mp_place():
    index = lax.axis_index("mp")
    return index >> 3, (index >> 1) & 3, index & 1


def spread(pair, through=None):
    y = mp_place()[1]
    arrived = [(k, lax.ppermute(pair, "mp", AROUND_Y[k])) for k in (1, 3, 2)]
    if through is not None:
        pair = through(pair)
    held = put(jnp.zeros((2, 4, *pair.shape[1:]), pair.dtype), pair[:, None], 0, y)
    for k, piece in arrived:
        held = put(held, piece[:, None], 0, (y - k) & 3)
    held = held.reshape(8, *pair.shape[1:])
    return held, lax.ppermute(held, "mp", CORE)


def collect(mine, theirs, through=None):
    y = mp_place()[1]
    other = lax.ppermute(theirs, "mp", CORE)
    held = (mine.astype(F32) + other.astype(F32)).astype(BF16).reshape(2, 4, *mine.shape[1:])
    arrived = [lax.ppermute(pick(held, (y + k) & 3, 1), "mp", AROUND_Y[k]) for k in (1, 3, 2)]
    own = pick(held, y, 1)
    if through is not None:
        own = through(own)
    total = own.astype(F32)
    for piece in arrived:
        total = total + piece.astype(F32)
    return total


def sum_pair(total, through=None):
    rounded = total.astype(BF16)
    other = lax.ppermute(rounded, "mp", FAR)
    if through is not None:
        rounded = through(rounded)
    return rounded.astype(F32) + other.astype(F32)


def sum_own(total):
    x_hi = mp_place()[0]
    other = lax.ppermute(pick(total, 1 - x_hi, 0).astype(BF16), "mp", FAR)
    return pick(total, x_hi, 0) + other.astype(F32)


def dp_bit(weight):
    return (lax.axis_index("dp") // weight) & 1


def swap_dp(weight, array):
    return lax.ppermute(array, "dp", [(i, i ^ weight) for i in range(16)])


def halve_dp(weight, total):
    on = dp_bit(weight)
    total = total.reshape(2, -1, *total.shape[1:])
    return pick(total, on, 0), swap_dp(weight, pick(total, 1 - on, 0).astype(BF16))


def finish_dp(order, total):
    low, high = order[2:]
    place = dp_bit(low) * 2 + dp_bit(high)
    rounded = total.astype(BF16)
    arrived = [
        swap_dp(weight, pick(rounded, place ^ flips, 0))
        for flips, weight in ((3, low | high), (2, low), (1, high))
    ]
    total = pick(total, place, 0)
    for piece in arrived:
        total = total + piece.astype(F32)
    return total


def scatter_dp(order, total):
    kept, other = halve_dp(order[1], total)
    return finish_dp(order, kept + other.astype(F32))


def gather_dp(block):
    index = lax.axis_index("dp")
    x_lo, z = index >> 3, index & 7
    held = block[None]
    for bit in (2, 1, 0):
        other = lax.ppermute(held, "dp", [(i, i ^ (1 << bit)) for i in range(16)])
        on = ((z >> bit) & 1) == 1
        held = jnp.stack([jnp.where(on, other, held), jnp.where(on, held, other)], axis=held.ndim - 2)
    other = lax.ppermute(held, "dp", FAR)
    on = x_lo == 1
    held = jnp.stack([jnp.where(on, other, held), jnp.where(on, held, other)])
    return held.reshape(16, *block.shape)


def rows(start, size):
    return pl.ds(pl.multiple_of(start, 16), size)


def place(core, i, own, size):
    return rows((2 * i + (core if own else 1 - core)) * size, size)


def call(kernel, outs, *args, scratch=(), after=()):
    spec = pl.BlockSpec(memory_space=pltpu.VMEM)
    specs = [pl.BlockSpec(memory_space=pltpu.SMEM)] + [spec] * (len(args) - 1)
    skip = len(after)
    if skip:
        inner = kernel
        kernel = lambda *refs: inner(*refs[skip:])
    size = sum(math.prod(a.shape) * a.dtype.itemsize for a in args)
    size += sum(math.prod(shape) * jnp.dtype(dtype).itemsize for shape, dtype in outs)
    return pl.pallas_call(
        kernel,
        out_shape=tuple(jax.ShapeDtypeStruct(shape, dtype) for shape, dtype in outs),
        in_specs=[pl.BlockSpec(memory_space=pl.ANY)] * skip + specs,
        out_specs=(spec,) * len(outs),
        scratch_shapes=list(scratch),
        compiler_params=pltpu.CompilerParams(vmem_limit_bytes=VMEM_LIMIT),
        cost_estimate=pl.CostEstimate(flops=0, bytes_accessed=size, transcendentals=0),
    )(*after, *args)


def flip(block):
    return block.astype(F32).T.astype(BF16)


def send_out(core, full_ref, mine_ref, theirs_ref, size):
    for i in range(8):
        mine_ref[i] = full_ref[place(core, i, True, size)].astype(BF16)
        theirs_ref[i] = full_ref[place(core, i, False, size)].astype(BF16)


def take_in(core, held_ref, other_ref, full_ref, size):
    for i in range(8):
        full_ref[place(core, i, True, size)] = held_ref[i]
        full_ref[place(core, i, False, size)] = other_ref[i]


def block_kernel(core_ref, held_ref, other_ref, gain_ref, w_in_ref, w_out_ref,
                 pre_ref, stat_ref, mine_ref, theirs_ref, z_ref, act_ref, full_ref):
    core = core_ref[0]
    width = z_ref.shape[0]
    total = jnp.zeros((1, z_ref.shape[1]), F32)
    for i in range(8):
        for ref in (held_ref, other_ref):
            total = total + jnp.sum(ref[i, :BLOCK].astype(F32), axis=0, keepdims=True)
    mean = total / width
    total = jnp.zeros_like(mean)
    for i in range(8):
        for ref in (held_ref, other_ref):
            centred = ref[i, :BLOCK].astype(F32) - mean
            total = total + jnp.sum(centred * centred, axis=0, keepdims=True)
    inv_std = 1.0 / jnp.sqrt(total / width + 1e-06)
    stat_ref[...] = jnp.zeros_like(stat_ref)
    stat_ref[0:1] = mean
    stat_ref[1:2] = inv_std
    for i in range(8):
        for own, ref in ((True, held_ref), (False, other_ref)):
            at = place(core, i, own, BLOCK)
            normed = (ref[i, :BLOCK].astype(F32) - mean) * inv_std
            z_ref[at] = (normed * gain_ref[at]).astype(BF16)
    hidden = pre_ref.shape[0]
    pre = jnp.zeros(pre_ref.shape, F32)
    for start in range(0, width, hidden):
        pre = pre + dot(flip(w_in_ref[start : start + hidden]), z_ref[start : start + hidden])
    pre_ref[...] = pre
    act_ref[...] = gelu(pre).astype(BF16)
    for start in range(0, width, hidden):
        full_ref[start : start + hidden] = dot(flip(w_out_ref[:, start : start + hidden]), act_ref[...])
    send_out(core, full_ref, mine_ref, theirs_ref, BLOCK)


def adaptor_kernel(core_ref, held_ref, other_ref, adapt_t_ref, heads_t_ref,
                   h_ref, pre_ref, q_ref, mine_a_ref, theirs_a_ref, mine_b_ref, theirs_b_ref):
    core = core_ref[0]
    take_in(core, held_ref, other_ref, h_ref, BLOCK)
    pre = dot(adapt_t_ref[...], h_ref[...])
    pre_ref[...] = pre
    q_ref[...] = gelu(pre).astype(BF16)
    for i in range(8):
        for own, a_ref, b_ref in ((True, mine_a_ref, mine_b_ref), (False, theirs_a_ref, theirs_b_ref)):
            pred = dot(heads_t_ref[place(core, i, own, TEACH)], q_ref[...]).astype(BF16)
            a_ref[i] = pred[:PART]
            b_ref[i] = pred[PART:]


def adaptor_back_kernel(core_ref, held_a_ref, other_a_ref, held_b_ref, other_b_ref, heads_ref, pre_ref, adapt_t_ref,
                        err_ref, back_ref, mine_ref, theirs_ref, full_ref):
    core = core_ref[0]
    for i in range(8):
        for own, refs in ((True, (held_a_ref, held_b_ref)), (False, (other_a_ref, other_b_ref))):
            start = (2 * i + (core if own else 1 - core)) * TEACH
            for part in range(2):
                err_ref[rows(start + part * PART, PART)] = refs[part][i]
    lifted = dot(heads_ref[...], err_ref[...])
    back_ref[...] = (lifted * gelu_slope(pre_ref[...])).astype(BF16)
    for start in range(0, full_ref.shape[0], 512):
        full_ref[start : start + 512] = dot(flip(adapt_t_ref[:, start : start + 512]), back_ref[...])
    send_out(core, full_ref, mine_ref, theirs_ref, BLOCK)


def adaptor_grads_kernel(scale, widths, on_ref, pair_ref, err_ref, q_ref, h_ref, back_ref,
                         pair_out_ref, mine_ref, theirs_ref, ga_ref, go_ref):
    pair_out_ref[...] = pair_ref[...]
    hid3 = q_ref.shape[0]
    hid = hid3 // 3
    ga_ref[...] = dot(h_ref[...], back_ref[...], 1, 1) * scale
    go_ref[...] = dot(err_ref[...], q_ref[...], 1, 1) * scale
    w0, w1, w2 = widths
    for j in range(8):
        for chunk, ref in sides(PACK_ORDER, on_ref[0], j, mine_ref, theirs_ref):
            at = rows(chunk * BLOCK, BLOCK)
            go = go_ref[rows(chunk * TEACH, TEACH)]
            ref[j, :BLOCK] = jnp.concatenate(
                [ga_ref[at], go[:BLOCK, :hid]], axis=1
            ).astype(BF16)
            second = go[w0 : w0 + w1, hid : 2 * hid]
            third = go[w0 + w1 : w0 + w1 + w2, 2 * hid :]
            second = jnp.concatenate([second, jnp.zeros((2 * LOW - w1, hid), F32)], axis=0)
            third = jnp.concatenate([third, jnp.zeros((2 * LOW - w2, hid), F32)], axis=0)
            ref[j, BLOCK:] = jnp.concatenate(
                [second[:LOW], third[:LOW], second[LOW:], third[LOW:]], axis=1
            ).astype(BF16)


def w_out_grad_kernel(scale, place_ref, ds_ref, act_ref, mine_ref, theirs_ref, full_ref):
    full_ref[...] = dot(ds_ref[...], act_ref[...], 1, 1) * scale
    halves(OUT_ORDER, place_ref[1], full_ref, mine_ref, theirs_ref)


def sides(order, on, j, mine_ref, theirs_ref):
    first, rest = order[0], order[1:]
    chunk = sum(weight * ((j >> (2 - i)) & 1) for i, weight in enumerate(rest))
    return ((on * first + chunk, mine_ref), ((1 - on) * first + chunk, theirs_ref))


def halves(order, on, full_ref, mine_ref, theirs_ref):
    for j in range(8):
        for chunk, ref in sides(order, on, j, mine_ref, theirs_ref):
            ref[j] = full_ref[rows(chunk * BLOCK, BLOCK)].astype(BF16)


def w_in_grad_kernel(scale, place_ref, z_ref, dpre_ref, mine_ref, theirs_ref, full_ref):
    full_ref[...] = dot(z_ref[...], dpre_ref[...], 1, 1) * scale
    halves(IN_ORDER, place_ref[2], full_ref, mine_ref, theirs_ref)


def block_back_kernel(core_ref, ds_held_ref, ds_other_ref, w_out_ref, pre_ref, w_in_ref, gain_ref,
                      held_ref, other_ref, stat_ref,
                      ds_ref, dpre_ref, z_ref, act_ref, mine_ref, theirs_ref, full_ref):
    core = core_ref[0]
    take_in(core, ds_held_ref, ds_other_ref, ds_ref, BLOCK)
    width = ds_ref.shape[0]
    act_ref[...] = gelu(pre_ref[...]).astype(BF16)
    dpre_ref[...] = (dot(w_out_ref[...], ds_ref[...]) * gelu_slope(pre_ref[...])).astype(BF16)
    full_ref[...] = dot(w_in_ref[...], dpre_ref[...])
    mean = stat_ref[0:1]
    inv_std = stat_ref[1:2]
    first = jnp.zeros_like(mean)
    second = jnp.zeros_like(mean)
    for i in range(8):
        for own, ref, out_ref in ((True, held_ref, mine_ref), (False, other_ref, theirs_ref)):
            at = place(core, i, own, BLOCK)
            dnorm = full_ref[at]
            out_ref[i, :BLOCK] = dnorm.astype(BF16)
            lifted = dnorm * gain_ref[at]
            normed = (ref[i, :BLOCK].astype(F32) - mean) * inv_std
            z_ref[at] = (normed * gain_ref[at]).astype(BF16)
            first = first + jnp.sum(lifted, axis=0, keepdims=True)
            second = second + jnp.sum(lifted * normed, axis=0, keepdims=True)
    sums = []
    for part in (first / width, second / width):
        high = part.astype(BF16).astype(F32)
        sums = sums + [high, part - high]
    sums = jnp.concatenate(sums + [jnp.zeros((SUMS - 4, mean.shape[1]), F32)], axis=0).astype(BF16)
    for i in range(8):
        mine_ref[i, BLOCK:] = sums
        theirs_ref[i, BLOCK:] = sums


def start_kernel(place_ref, tokens_ref, *refs):
    teach_refs, (pair_ref, block_ref) = refs[:3], refs[3:]
    pair_ref[...] = jnp.zeros_like(pair_ref)
    pair_ref[place_ref[0], :BLOCK] = tokens_ref[...]
    block_ref[...] = jnp.zeros_like(block_ref)
    for m in range(8):

        @pl.when(place_ref[1] == m)
        def _():
            for side in range(2):
                offset = side * TEACH
                for ref in teach_refs:
                    wide = ref.shape[1] // 16
                    start = (side * 8 + m) * wide
                    block_ref[:, offset : offset + wide] = ref[:, start : start + wide]
                    offset = offset + wide


def heads_kernel(_, own_ref, block_ref, *refs):
    head_refs, (own_out_ref, block_out_ref, heads_ref, heads_t_ref) = refs[:3], refs[3:]
    own_out_ref[...] = own_ref[...]
    block_out_ref[...] = block_ref[...]
    hid = heads_ref.shape[0] // 3
    heads_ref[...] = jnp.zeros_like(heads_ref)
    for m in range(16):
        offset = m * TEACH
        for k in range(3):
            wide = head_refs[k].shape[1] // 16
            heads_ref[k * hid : (k + 1) * hid, offset : offset + wide] = head_refs[k][:, m * wide : (m + 1) * wide]
            offset = offset + wide
        heads_t_ref[m * TEACH : (m + 1) * TEACH] = flip(heads_ref[:, m * TEACH : (m + 1) * TEACH])


def add_kernel(_, mine_ref, other_ref, total_ref):
    total_ref[...] = mine_ref[...].astype(F32) + other_ref[...].astype(F32)


def body(
    tokens,
    ln_gain,
    w_in,
    w_out,
    adapt_in,
    out_dino,
    out_siglip,
    out_sam,
    teach_dino,
    teach_siglip,
    teach_sam,
    src_dev,
    src_row,
):
    heads = (out_dino, out_siglip, out_sam)
    teachers = (teach_dino, teach_siglip, teach_sam)
    n_rows = tokens.shape[0]
    n_mp = lax.axis_size("mp")
    n_dp = lax.axis_size("dp")
    width = BLOCK * n_mp
    hidden = w_in.shape[1]
    hid = adapt_in.shape[2]
    share = n_rows // n_mp
    short = [head.shape[1] // n_mp for head in heads]
    spare = TEACH - sum(short)
    scale = 1.0 / math.sqrt(n_rows * n_dp)
    x_hi, y, core = mp_place()
    at = jnp.stack([core, dp_bit(OUT_ORDER[0]), dp_bit(IN_ORDER[0])]).astype(jnp.int32)
    gain = ln_gain[:, None]

    with jax.named_scope("tokens"):
        own_tokens = tokens.T
        far_tokens = lax.ppermute(own_tokens, "mp", FAR)
        token_pair, block = call(
            start_kernel,
            [((2, BLOCK + EXTRA, n_rows), BF16), ((teach_dino.shape[0], 2 * TEACH), BF16)],
            jnp.stack([x_hi, y * 2 + core]).astype(jnp.int32), own_tokens, *teachers,
        )
        sources = jnp.concatenate([src_dev, src_row], axis=1).T.astype(BF16)
        sources = jnp.pad(sources, ((0, EXTRA - 4), (0, n_rows - share)))
        token_pair = put(token_pair, far_tokens[None], 1 - x_hi)
        token_pair = put(token_pair, sources[None], x_hi, BLOCK)
        token_pair = put(token_pair, lax.ppermute(sources, "mp", FAR)[None], 1 - x_hi, BLOCK)
        x_held, x_other = spread(token_pair)

    more = []

    def more_weights(own):
        own, *rest = call(
            heads_kernel,
            [
                (own.shape, BF16),
                (block.shape, BF16),
                ((3 * hid, n_mp * TEACH), BF16),
                ((n_mp * TEACH, 3 * hid), BF16),
            ],
            at, own, block, *heads,
        )
        more.extend(rest)
        return own

    with jax.named_scope("block"):
        pre_mlp, stat, mine, theirs = call(
            block_kernel,
            [
                ((hidden, n_rows), F32),
                ((8, n_rows), F32),
                ((8, BLOCK, n_rows), BF16),
                ((8, BLOCK, n_rows), BF16),
            ],
            at, x_held, x_other, gain, w_in, w_out,
            scratch=[
                pltpu.VMEM((width, n_rows), BF16),
                pltpu.VMEM((hidden, n_rows), BF16),
                pltpu.VMEM((width, n_rows), F32),
            ],
        )
        state = sum_pair(collect(mine, theirs, more_weights)) + token_pair[:, :BLOCK].astype(F32)
        h_held, h_other = spread(state.astype(BF16))

    with jax.named_scope("targets"):
        block_later, heads_all, heads_t = more
        adapt_t = adapt_in.transpose(0, 2, 1).reshape(3 * hid, width)
        pool = gather_dp(block_later).reshape(-1, 2 * TEACH)
        mixed = [a[:, BLOCK : BLOCK + 4, :share] for a in (x_held, x_other)]
        mixed = jnp.stack(
            [jnp.where(core == 0, mixed[0], mixed[1]), jnp.where(core == 0, mixed[1], mixed[0])], axis=1
        )
        source = mixed.transpose(2, 0, 1, 3).reshape(4, n_rows).astype(jnp.int32)
        places = jnp.arange(pool.shape[0], dtype=jnp.int32)[:, None]
        spots = source[:1] * teach_dino.shape[0] + source[1:]
        target = []
        for side in range(2):
            offset = side * TEACH
            for k in range(3):
                chosen = (places == spots[k : k + 1]).astype(BF16)
                target.append(dot(pool[:, offset : offset + short[k]], chosen, 0, 0))
                offset = offset + short[k]
            target.append(jnp.zeros((spare, n_rows), F32))
        target = jnp.concatenate(target, axis=0).reshape(2, TEACH, n_rows).astype(BF16)

    with jax.named_scope("adaptors"):
        h, pre_adapt, q, *sent = call(
            adaptor_kernel,
            [
                ((width, n_rows), BF16),
                ((3 * hid, n_rows), F32),
                ((3 * hid, n_rows), BF16),
            ]
            + [((8, PART, n_rows), BF16)] * 4,
            at, h_held, h_other, adapt_t, heads_t,
        )
        errors = []
        for part in range(2):
            pred = sum_pair(collect(*sent[2 * part : 2 * part + 2]))
            error = pred - target[:, part * PART : (part + 1) * PART].astype(F32)
            errors.extend(spread(error.astype(BF16)))

    with jax.named_scope("adaptors_back"):
        err, back, mine, theirs = call(
            adaptor_back_kernel,
            [
                ((n_mp * TEACH, n_rows), BF16),
                ((3 * hid, n_rows), BF16),
                ((8, BLOCK, n_rows), BF16),
                ((8, BLOCK, n_rows), BF16),
            ],
            at, *errors, heads_all, pre_adapt, adapt_t,
            scratch=[pltpu.VMEM((width, n_rows), F32)],
        )
        packs = []

        def adaptor_grads(pair):
            pair, kept, sent = call(
                functools.partial(adaptor_grads_kernel, scale, short),
                [(pair.shape, BF16)] + [((8, BLOCK + LOW, 4 * hid), BF16)] * 2,
                dp_bit(PACK_ORDER[0])[None].astype(jnp.int32), pair, err, q, h, back,
                scratch=[
                    pltpu.VMEM((width, 3 * hid), F32),
                    pltpu.VMEM((n_mp * TEACH, 3 * hid), F32),
                ],
            )
            packs.extend((kept, swap_dp(PACK_ORDER[0], sent)))
            return pair

        dstate = sum_pair(collect(mine, theirs), adaptor_grads)
        d_held, d_other = spread(dstate.astype(BF16))

    with jax.named_scope("block_back"):
        ds, dpre, z, act, mine, theirs = call(
            block_back_kernel,
            [((width, n_rows), BF16), ((hidden, n_rows), BF16)] * 2
            + [((8, BLOCK + SUMS, n_rows), BF16)] * 2,
            at, d_held, d_other, w_out, pre_mlp, w_in, gain, x_held, x_other, stat,
            scratch=[pltpu.VMEM((width, n_rows), F32)],
        )
        ins = call(
            functools.partial(w_in_grad_kernel, scale),
            [((8, BLOCK, hidden), BF16)] * 2,
            at, z, dpre,
            scratch=[pltpu.VMEM((width, hidden), F32)],
        )
        outs = call(
            functools.partial(w_out_grad_kernel, scale),
            [((8, BLOCK, hidden), BF16)] * 2,
            at, ds, act,
            scratch=[pltpu.VMEM((width, hidden), F32)],
            after=(ins[0],),
        )
        sums = []

        def first_sums(own):
            total = call(add_kernel, [(packs[0].shape, F32)], at, *packs, after=(own,))
            for order, (kept, sent) in ((IN_ORDER, ins), (OUT_ORDER, outs)):
                sums.extend(
                    call(add_kernel, [(kept.shape, F32)], at, kept, swap_dp(order[0], sent), after=(own, *total, *sums))
                )
            sums.extend(total)
            return own

        partial = collect(mine, theirs, first_sums)
        summed = sum_own(partial)
        gain_own = lax.dynamic_slice_in_dim(ln_gain, lax.axis_index("mp") * BLOCK, BLOCK, 0)
        normed = (tokens.T.astype(F32) - stat[0:1]) * stat[1:2]
        dnorm = summed[:BLOCK] * gain_own[:, None]
        first = summed[BLOCK : BLOCK + 1] + summed[BLOCK + 1 : BLOCK + 2]
        second = summed[BLOCK + 2 : BLOCK + 3] + summed[BLOCK + 3 : BLOCK + 4]
        grad_tokens = pick(dstate, x_hi, 0) + stat[1:2] * (dnorm - first - normed * second)

    with jax.named_scope("weight_sums"):
        pack = scatter_dp(PACK_ORDER, sums[2])
        grad_w_in = scatter_dp(IN_ORDER, sums[0])
        grad_w_out = scatter_dp(OUT_ORDER, sums[1])

    tail = pack[BLOCK:]
    second = jnp.concatenate([tail[:, :hid], tail[:, 2 * hid : 3 * hid]], axis=0)
    third = jnp.concatenate([tail[:, hid : 2 * hid], tail[:, 3 * hid :]], axis=0)
    return (
        grad_tokens.T,
        grad_w_in,
        grad_w_out.T,
        jnp.stack([pack[:BLOCK, k * hid : (k + 1) * hid] for k in range(3)]),
        pack[:BLOCK, 3 * hid :].T,
        second[: short[1]].T,
        third[: short[2]].T,
    )


def solution(mesh):
    placed = (
        P("dp", "mp"),
        P(),
        P(None, "mp"),
        P("mp", None),
        P(None, None, "mp"),
        P("mp", None),
        P("mp", None),
        P("mp", None),
        P("dp", None),
        P("dp", None),
        P("dp", None),
        P(("dp", "mp"), None),
        P(("dp", "mp"), None),
    )
    return jax.shard_map(
        body,
        mesh=mesh,
        in_specs=placed,
        out_specs=(
            P("dp", "mp"),
            P("dp", "mp"),
            P("mp", "dp"),
            P(None, "dp", "mp"),
            P("mp", "dp"),
            P("mp", "dp"),
            P("mp", "dp"),
        ),
        check_vma=False,
    )
```

```python
import functools
import math

import jax
import jax.numpy as jnp
from jax import lax
from jax.experimental import pallas as pl
from jax.experimental.pallas import tpu as pltpu
from jax.sharding import PartitionSpec as P

F32 = jnp.float32
BF16 = jnp.bfloat16
VMEM_LIMIT = 20 * 1024 * 1024
PARTNER = {1: 1, 2: 2, 4: 6, 8: 8}
PACK_ORDER = (1, 8, 2, 4)
OUT_ORDER = (1, 8, 2, 4)
IN_ORDER = (8, 1, 2, 4)

CORE = [(i, i ^ 1) for i in range(16)]
FAR = [(i, i ^ 8) for i in range(16)]
AROUND_Y = [[(i, (i & 9) | ((((i >> 1 & 3) + k) & 3) << 1)) for i in range(16)] for k in range(4)]

BLOCK = 96
TEACH = 256
PART = 128
EXTRA = 8
SUMS = 16
LOW = 48


def gelu(value):
    return 0.5 * value * (1.0 + lax.erf(value * 0.7071067811865476))


def gelu_slope(value):
    return (
        0.5 * (1.0 + lax.erf(value * 0.7071067811865476))
        + value * jnp.exp(-0.5 * value * value) * 0.3989422804014327
    )


def dot(left, right, over_left=1, over_right=0):
    return lax.dot_general(
        left, right, (((over_left,), (over_right,)), ((), ())), preferred_element_type=F32
    )


def pick(array, index, axis):
    return lax.dynamic_index_in_dim(array, index, axis, keepdims=False)


def put(buffer, piece, *at):
    return lax.dynamic_update_slice(buffer, piece, at + (0,) * (buffer.ndim - len(at)))


def mp_place():
    index = lax.axis_index("mp")
    return index >> 3, (index >> 1) & 3, index & 1


def spread(pair, through=None):
    y = mp_place()[1]
    arrived = [(k, lax.ppermute(pair, "mp", AROUND_Y[k])) for k in (1, 3, 2)]
    if through is not None:
        pair = through(pair)
    held = put(jnp.zeros((2, 4, *pair.shape[1:]), pair.dtype), pair[:, None], 0, y)
    for k, piece in arrived:
        held = put(held, piece[:, None], 0, (y - k) & 3)
    held = held.reshape(8, *pair.shape[1:])
    return held, lax.ppermute(held, "mp", CORE)


def collect(mine, theirs, through=None):
    y = mp_place()[1]
    other = lax.ppermute(theirs, "mp", CORE)
    held = (mine.astype(F32) + other.astype(F32)).astype(BF16).reshape(2, 4, *mine.shape[1:])
    arrived = [lax.ppermute(pick(held, (y + k) & 3, 1), "mp", AROUND_Y[k]) for k in (1, 3, 2)]
    own = pick(held, y, 1)
    if through is not None:
        own = through(own)
    total = own.astype(F32)
    for piece in arrived:
        total = total + piece.astype(F32)
    return total


def sum_pair(total, through=None):
    rounded = total.astype(BF16)
    other = lax.ppermute(rounded, "mp", FAR)
    if through is not None:
        rounded = through(rounded)
    return rounded.astype(F32) + other.astype(F32)


def sum_own(total):
    x_hi = mp_place()[0]
    other = lax.ppermute(pick(total, 1 - x_hi, 0).astype(BF16), "mp", FAR)
    return pick(total, x_hi, 0) + other.astype(F32)


def unlabel(label):
    return label ^ ((label >> 1) & 2)


def dp_bit(weight):
    return (unlabel(lax.axis_index("dp")) // weight) & 1


def swap_dp(weight, array):
    return lax.ppermute(array, "dp", [(i, i ^ PARTNER[weight]) for i in range(16)])


def halve_dp(weight, total):
    on = dp_bit(weight)
    total = total.reshape(2, -1, *total.shape[1:])
    return pick(total, on, 0), swap_dp(weight, pick(total, 1 - on, 0).astype(BF16))


def scatter_dp(order, total):
    for weight in order[1:]:
        kept, other = halve_dp(weight, total)
        total = kept + other.astype(F32)
    return total[0]


def gather_dp(block):
    held = block[None]
    for weight in (4, 2, 1):
        other = swap_dp(weight, held)
        on = dp_bit(weight) == 1
        held = jnp.stack([jnp.where(on, other, held), jnp.where(on, held, other)], axis=held.ndim - 2)
    other = swap_dp(8, held)
    on = dp_bit(8) == 1
    held = jnp.stack([jnp.where(on, other, held), jnp.where(on, held, other)])
    return held.reshape(16, *block.shape)


def rows(start, size):
    return pl.ds(pl.multiple_of(start, 16), size)


def place(core, i, own, size):
    return rows((2 * i + (core if own else 1 - core)) * size, size)


def call(kernel, outs, *args, scratch=(), after=()):
    spec = pl.BlockSpec(memory_space=pltpu.VMEM)
    specs = [pl.BlockSpec(memory_space=pltpu.SMEM)] + [spec] * (len(args) - 1)
    skip = len(after)
    if skip:
        inner = kernel
        kernel = lambda *refs: inner(*refs[skip:])
    size = sum(math.prod(a.shape) * a.dtype.itemsize for a in args)
    size += sum(math.prod(shape) * jnp.dtype(dtype).itemsize for shape, dtype in outs)
    return pl.pallas_call(
        kernel,
        out_shape=tuple(jax.ShapeDtypeStruct(shape, dtype) for shape, dtype in outs),
        in_specs=[pl.BlockSpec(memory_space=pl.ANY)] * skip + specs,
        out_specs=(spec,) * len(outs),
        scratch_shapes=list(scratch),
        compiler_params=pltpu.CompilerParams(vmem_limit_bytes=VMEM_LIMIT),
        cost_estimate=pl.CostEstimate(flops=0, bytes_accessed=size, transcendentals=0),
    )(*after, *args)


def flip(block):
    return block.astype(F32).T.astype(BF16)


def send_out(core, full_ref, mine_ref, theirs_ref, size):
    for i in range(8):
        mine_ref[i] = full_ref[place(core, i, True, size)].astype(BF16)
        theirs_ref[i] = full_ref[place(core, i, False, size)].astype(BF16)


def take_in(core, held_ref, other_ref, full_ref, size):
    for i in range(8):
        full_ref[place(core, i, True, size)] = held_ref[i]
        full_ref[place(core, i, False, size)] = other_ref[i]


def block_kernel(core_ref, held_ref, other_ref, gain_ref, w_in_ref, w_out_ref,
                 pre_ref, stat_ref, mine_ref, theirs_ref, z_ref, act_ref, full_ref):
    core = core_ref[0]
    width = z_ref.shape[0]
    total = jnp.zeros((1, z_ref.shape[1]), F32)
    for i in range(8):
        for ref in (held_ref, other_ref):
            total = total + jnp.sum(ref[i, :BLOCK].astype(F32), axis=0, keepdims=True)
    mean = total / width
    total = jnp.zeros_like(mean)
    for i in range(8):
        for ref in (held_ref, other_ref):
            centred = ref[i, :BLOCK].astype(F32) - mean
            total = total + jnp.sum(centred * centred, axis=0, keepdims=True)
    inv_std = 1.0 / jnp.sqrt(total / width + 1e-06)
    stat_ref[...] = jnp.zeros_like(stat_ref)
    stat_ref[0:1] = mean
    stat_ref[1:2] = inv_std
    for i in range(8):
        for own, ref in ((True, held_ref), (False, other_ref)):
            at = place(core, i, own, BLOCK)
            normed = (ref[i, :BLOCK].astype(F32) - mean) * inv_std
            z_ref[at] = (normed * gain_ref[at]).astype(BF16)
    hidden = pre_ref.shape[0]
    pre = jnp.zeros(pre_ref.shape, F32)
    for start in range(0, width, hidden):
        pre = pre + dot(flip(w_in_ref[start : start + hidden]), z_ref[start : start + hidden])
    pre_ref[...] = pre
    act_ref[...] = gelu(pre).astype(BF16)
    for start in range(0, width, hidden):
        full_ref[start : start + hidden] = dot(flip(w_out_ref[:, start : start + hidden]), act_ref[...])
    send_out(core, full_ref, mine_ref, theirs_ref, BLOCK)


def adaptor_kernel(core_ref, held_ref, other_ref, adapt_t_ref, heads_t_ref,
                   h_ref, pre_ref, q_ref, mine_a_ref, theirs_a_ref, mine_b_ref, theirs_b_ref):
    core = core_ref[0]
    take_in(core, held_ref, other_ref, h_ref, BLOCK)
    pre = dot(adapt_t_ref[...], h_ref[...])
    pre_ref[...] = pre
    q_ref[...] = gelu(pre).astype(BF16)
    for i in range(8):
        for own, a_ref, b_ref in ((True, mine_a_ref, mine_b_ref), (False, theirs_a_ref, theirs_b_ref)):
            pred = dot(heads_t_ref[place(core, i, own, TEACH)], q_ref[...]).astype(BF16)
            a_ref[i] = pred[:PART]
            b_ref[i] = pred[PART:]


def adaptor_back_kernel(core_ref, held_a_ref, other_a_ref, held_b_ref, other_b_ref, heads_ref, pre_ref, adapt_t_ref,
                        err_ref, back_ref, mine_ref, theirs_ref, full_ref):
    core = core_ref[0]
    for i in range(8):
        for own, refs in ((True, (held_a_ref, held_b_ref)), (False, (other_a_ref, other_b_ref))):
            start = (2 * i + (core if own else 1 - core)) * TEACH
            for part in range(2):
                err_ref[rows(start + part * PART, PART)] = refs[part][i]
    lifted = dot(heads_ref[...], err_ref[...])
    back_ref[...] = (lifted * gelu_slope(pre_ref[...])).astype(BF16)
    for start in range(0, full_ref.shape[0], 512):
        full_ref[start : start + 512] = dot(flip(adapt_t_ref[:, start : start + 512]), back_ref[...])
    send_out(core, full_ref, mine_ref, theirs_ref, BLOCK)


def adaptor_grads_kernel(scale, widths, on_ref, pair_ref, err_ref, q_ref, h_ref, back_ref,
                         pair_out_ref, mine_ref, theirs_ref, ga_ref, go_ref):
    pair_out_ref[...] = pair_ref[...]
    hid3 = q_ref.shape[0]
    hid = hid3 // 3
    ga_ref[...] = dot(h_ref[...], back_ref[...], 1, 1) * scale
    go_ref[...] = dot(err_ref[...], q_ref[...], 1, 1) * scale
    w0, w1, w2 = widths
    for j in range(8):
        for chunk, ref in sides(PACK_ORDER, on_ref[0], j, mine_ref, theirs_ref):
            at = rows(chunk * BLOCK, BLOCK)
            go = go_ref[rows(chunk * TEACH, TEACH)]
            ref[j, :BLOCK] = jnp.concatenate(
                [ga_ref[at], go[:BLOCK, :hid]], axis=1
            ).astype(BF16)
            second = go[w0 : w0 + w1, hid : 2 * hid]
            third = go[w0 + w1 : w0 + w1 + w2, 2 * hid :]
            second = jnp.concatenate([second, jnp.zeros((2 * LOW - w1, hid), F32)], axis=0)
            third = jnp.concatenate([third, jnp.zeros((2 * LOW - w2, hid), F32)], axis=0)
            ref[j, BLOCK:] = jnp.concatenate(
                [second[:LOW], third[:LOW], second[LOW:], third[LOW:]], axis=1
            ).astype(BF16)


def w_out_grad_kernel(scale, place_ref, ds_ref, act_ref, mine_ref, theirs_ref, full_ref):
    full_ref[...] = dot(ds_ref[...], act_ref[...], 1, 1) * scale
    halves(OUT_ORDER, place_ref[1], full_ref, mine_ref, theirs_ref)


def sides(order, on, j, mine_ref, theirs_ref):
    first, rest = order[0], order[1:]
    chunk = sum(weight * ((j >> (2 - i)) & 1) for i, weight in enumerate(rest))
    return ((unlabel(on * first + chunk), mine_ref), (unlabel((1 - on) * first + chunk), theirs_ref))


def halves(order, on, full_ref, mine_ref, theirs_ref):
    for j in range(8):
        for chunk, ref in sides(order, on, j, mine_ref, theirs_ref):
            ref[j] = full_ref[rows(chunk * BLOCK, BLOCK)].astype(BF16)


def w_in_grad_kernel(scale, place_ref, z_ref, dpre_ref, mine_ref, theirs_ref, full_ref):
    full_ref[...] = dot(z_ref[...], dpre_ref[...], 1, 1) * scale
    halves(IN_ORDER, place_ref[2], full_ref, mine_ref, theirs_ref)


def block_back_kernel(core_ref, ds_held_ref, ds_other_ref, w_out_ref, pre_ref, w_in_ref, gain_ref,
                      held_ref, other_ref, stat_ref,
                      ds_ref, dpre_ref, z_ref, act_ref, mine_ref, theirs_ref, full_ref):
    core = core_ref[0]
    take_in(core, ds_held_ref, ds_other_ref, ds_ref, BLOCK)
    width = ds_ref.shape[0]
    act_ref[...] = gelu(pre_ref[...]).astype(BF16)
    dpre_ref[...] = (dot(w_out_ref[...], ds_ref[...]) * gelu_slope(pre_ref[...])).astype(BF16)
    full_ref[...] = dot(w_in_ref[...], dpre_ref[...])
    mean = stat_ref[0:1]
    inv_std = stat_ref[1:2]
    first = jnp.zeros_like(mean)
    second = jnp.zeros_like(mean)
    for i in range(8):
        for own, ref, out_ref in ((True, held_ref, mine_ref), (False, other_ref, theirs_ref)):
            at = place(core, i, own, BLOCK)
            dnorm = full_ref[at]
            out_ref[i, :BLOCK] = dnorm.astype(BF16)
            lifted = dnorm * gain_ref[at]
            normed = (ref[i, :BLOCK].astype(F32) - mean) * inv_std
            z_ref[at] = (normed * gain_ref[at]).astype(BF16)
            first = first + jnp.sum(lifted, axis=0, keepdims=True)
            second = second + jnp.sum(lifted * normed, axis=0, keepdims=True)
    sums = []
    for part in (first / width, second / width):
        high = part.astype(BF16).astype(F32)
        sums = sums + [high, part - high]
    sums = jnp.concatenate(sums + [jnp.zeros((SUMS - 4, mean.shape[1]), F32)], axis=0).astype(BF16)
    for i in range(8):
        mine_ref[i, BLOCK:] = sums
        theirs_ref[i, BLOCK:] = sums


def start_kernel(place_ref, tokens_ref, *refs):
    teach_refs, (pair_ref, block_ref) = refs[:3], refs[3:]
    pair_ref[...] = jnp.zeros_like(pair_ref)
    pair_ref[place_ref[0], :BLOCK] = tokens_ref[...]
    block_ref[...] = jnp.zeros_like(block_ref)
    for m in range(8):

        @pl.when(place_ref[1] == m)
        def _():
            for side in range(2):
                offset = side * TEACH
                for ref in teach_refs:
                    wide = ref.shape[1] // 16
                    start = (side * 8 + m) * wide
                    block_ref[:, offset : offset + wide] = ref[:, start : start + wide]
                    offset = offset + wide


def pass_kernel(_, first_ref, second_ref, first_out_ref, second_out_ref):
    first_out_ref[...] = first_ref[...]
    second_out_ref[...] = second_ref[...]


def heads_kernel(_, own_ref, *refs):
    head_refs, (own_out_ref, heads_ref, heads_t_ref) = refs[:3], refs[3:]
    own_out_ref[...] = own_ref[...]
    hid = heads_ref.shape[0] // 3
    heads_ref[...] = jnp.zeros_like(heads_ref)
    for m in range(16):
        offset = m * TEACH
        for k in range(3):
            wide = head_refs[k].shape[1] // 16
            heads_ref[k * hid : (k + 1) * hid, offset : offset + wide] = head_refs[k][:, m * wide : (m + 1) * wide]
            offset = offset + wide
        heads_t_ref[m * TEACH : (m + 1) * TEACH] = flip(heads_ref[:, m * TEACH : (m + 1) * TEACH])


def add_kernel(_, mine_ref, other_ref, total_ref):
    total_ref[...] = mine_ref[...].astype(F32) + other_ref[...].astype(F32)


def body(
    tokens,
    ln_gain,
    w_in,
    w_out,
    adapt_in,
    out_dino,
    out_siglip,
    out_sam,
    teach_dino,
    teach_siglip,
    teach_sam,
    src_dev,
    src_row,
):
    heads = (out_dino, out_siglip, out_sam)
    teachers = (teach_dino, teach_siglip, teach_sam)
    n_rows = tokens.shape[0]
    n_mp = lax.axis_size("mp")
    n_dp = lax.axis_size("dp")
    width = BLOCK * n_mp
    hidden = w_in.shape[1]
    hid = adapt_in.shape[2]
    share = n_rows // n_mp
    short = [head.shape[1] // n_mp for head in heads]
    spare = TEACH - sum(short)
    scale = 1.0 / math.sqrt(n_rows * n_dp)
    x_hi, y, core = mp_place()
    at = jnp.stack([core, dp_bit(OUT_ORDER[0]), dp_bit(IN_ORDER[0])]).astype(jnp.int32)
    gain = ln_gain[:, None]

    with jax.named_scope("tokens"):
        own_tokens = tokens.T
        far_tokens = lax.ppermute(own_tokens, "mp", FAR)
        token_pair, block = call(
            start_kernel,
            [((2, BLOCK + EXTRA, n_rows), BF16), ((teach_dino.shape[0], 2 * TEACH), BF16)],
            jnp.stack([x_hi, y * 2 + core]).astype(jnp.int32), own_tokens, *teachers,
        )
        sources = jnp.concatenate([src_dev, src_row], axis=1).T.astype(BF16)
        sources = jnp.pad(sources, ((0, EXTRA - 4), (0, n_rows - share)))
        token_pair = put(token_pair, far_tokens[None], 1 - x_hi)
        token_pair = put(token_pair, sources[None], x_hi, BLOCK)
        token_pair = put(token_pair, lax.ppermute(sources, "mp", FAR)[None], 1 - x_hi, BLOCK)
        x_held, x_other = spread(token_pair)

    more = []

    def more_weights(own):
        own, later = call(pass_kernel, [(own.shape, BF16), (block.shape, BF16)], at, own, block)
        own, *rest = call(
            heads_kernel,
            [
                (own.shape, BF16),
                ((3 * hid, n_mp * TEACH), BF16),
                ((n_mp * TEACH, 3 * hid), BF16),
            ],
            at, own, *heads,
        )
        more.extend((*rest, later))
        return own

    with jax.named_scope("block"):
        pre_mlp, stat, mine, theirs = call(
            block_kernel,
            [
                ((hidden, n_rows), F32),
                ((8, n_rows), F32),
                ((8, BLOCK, n_rows), BF16),
                ((8, BLOCK, n_rows), BF16),
            ],
            at, x_held, x_other, gain, w_in, w_out,
            scratch=[
                pltpu.VMEM((width, n_rows), BF16),
                pltpu.VMEM((hidden, n_rows), BF16),
                pltpu.VMEM((width, n_rows), F32),
            ],
        )
        state = sum_pair(collect(mine, theirs, more_weights)) + token_pair[:, :BLOCK].astype(F32)
        h_held, h_other = spread(state.astype(BF16))

    with jax.named_scope("targets"):
        heads_all, heads_t, block_later = more
        adapt_t = adapt_in.transpose(0, 2, 1).reshape(3 * hid, width)
        pool = gather_dp(block_later).reshape(-1, 2 * TEACH)
        mixed = [a[:, BLOCK : BLOCK + 4, :share] for a in (x_held, x_other)]
        mixed = jnp.stack(
            [jnp.where(core == 0, mixed[0], mixed[1]), jnp.where(core == 0, mixed[1], mixed[0])], axis=1
        )
        source = mixed.transpose(2, 0, 1, 3).reshape(4, n_rows).astype(jnp.int32)
        places = jnp.arange(pool.shape[0], dtype=jnp.int32)[:, None]
        deep = teach_dino.shape[0]
        places = unlabel(places // deep) * deep + places % deep
        spots = source[:1] * teach_dino.shape[0] + source[1:]
        target = []
        for side in range(2):
            offset = side * TEACH
            for k in range(3):
                chosen = (places == spots[k : k + 1]).astype(BF16)
                target.append(dot(pool[:, offset : offset + short[k]], chosen, 0, 0))
                offset = offset + short[k]
            target.append(jnp.zeros((spare, n_rows), F32))
        target = jnp.concatenate(target, axis=0).reshape(2, TEACH, n_rows).astype(BF16)

    with jax.named_scope("adaptors"):
        h, pre_adapt, q, *sent = call(
            adaptor_kernel,
            [
                ((width, n_rows), BF16),
                ((3 * hid, n_rows), F32),
                ((3 * hid, n_rows), BF16),
            ]
            + [((8, PART, n_rows), BF16)] * 4,
            at, h_held, h_other, adapt_t, heads_t,
        )
        errors = []
        for part in range(2):
            pred = sum_pair(collect(*sent[2 * part : 2 * part + 2]))
            error = pred - target[:, part * PART : (part + 1) * PART].astype(F32)
            errors.extend(spread(error.astype(BF16)))

    with jax.named_scope("adaptors_back"):
        err, back, mine, theirs = call(
            adaptor_back_kernel,
            [
                ((n_mp * TEACH, n_rows), BF16),
                ((3 * hid, n_rows), BF16),
                ((8, BLOCK, n_rows), BF16),
                ((8, BLOCK, n_rows), BF16),
            ],
            at, *errors, heads_all, pre_adapt, adapt_t,
            scratch=[pltpu.VMEM((width, n_rows), F32)],
        )
        packs = []

        def adaptor_grads(pair):
            pair, kept, sent = call(
                functools.partial(adaptor_grads_kernel, scale, short),
                [(pair.shape, BF16)] + [((8, BLOCK + LOW, 4 * hid), BF16)] * 2,
                dp_bit(PACK_ORDER[0])[None].astype(jnp.int32), pair, err, q, h, back,
                scratch=[
                    pltpu.VMEM((width, 3 * hid), F32),
                    pltpu.VMEM((n_mp * TEACH, 3 * hid), F32),
                ],
            )
            packs.extend((kept, swap_dp(PACK_ORDER[0], sent)))
            return pair

        dstate = sum_pair(collect(mine, theirs), adaptor_grads)
        d_held, d_other = spread(dstate.astype(BF16))

    with jax.named_scope("block_back"):
        ds, dpre, z, act, mine, theirs = call(
            block_back_kernel,
            [((width, n_rows), BF16), ((hidden, n_rows), BF16)] * 2
            + [((8, BLOCK + SUMS, n_rows), BF16)] * 2,
            at, d_held, d_other, w_out, pre_mlp, w_in, gain, x_held, x_other, stat,
            scratch=[pltpu.VMEM((width, n_rows), F32)],
        )
        ins = call(
            functools.partial(w_in_grad_kernel, scale),
            [((8, BLOCK, hidden), BF16)] * 2,
            at, z, dpre,
            scratch=[pltpu.VMEM((width, hidden), F32)],
        )
        outs = call(
            functools.partial(w_out_grad_kernel, scale),
            [((8, BLOCK, hidden), BF16)] * 2,
            at, ds, act,
            scratch=[pltpu.VMEM((width, hidden), F32)],
            after=(ins[0],),
        )
        sums = []

        def first_sums(own):
            total = call(add_kernel, [(packs[0].shape, F32)], at, *packs, after=(own,))
            for order, (kept, sent) in ((IN_ORDER, ins), (OUT_ORDER, outs)):
                sums.extend(
                    call(add_kernel, [(kept.shape, F32)], at, kept, swap_dp(order[0], sent), after=(own, *total, *sums))
                )
            sums.extend(total)
            return own

        partial = collect(mine, theirs, first_sums)
        summed = sum_own(partial)
        gain_own = lax.dynamic_slice_in_dim(ln_gain, lax.axis_index("mp") * BLOCK, BLOCK, 0)
        normed = (tokens.T.astype(F32) - stat[0:1]) * stat[1:2]
        dnorm = summed[:BLOCK] * gain_own[:, None]
        first = summed[BLOCK : BLOCK + 1] + summed[BLOCK + 1 : BLOCK + 2]
        second = summed[BLOCK + 2 : BLOCK + 3] + summed[BLOCK + 3 : BLOCK + 4]
        grad_tokens = pick(dstate, x_hi, 0) + stat[1:2] * (dnorm - first - normed * second)

    with jax.named_scope("weight_sums"):
        pack = scatter_dp(PACK_ORDER, sums[2])
        grad_w_in = scatter_dp(IN_ORDER, sums[0])
        grad_w_out = scatter_dp(OUT_ORDER, sums[1])

    tail = pack[BLOCK:]
    second = jnp.concatenate([tail[:, :hid], tail[:, 2 * hid : 3 * hid]], axis=0)
    third = jnp.concatenate([tail[:, hid : 2 * hid], tail[:, 3 * hid :]], axis=0)
    return (
        grad_tokens.T,
        grad_w_in,
        grad_w_out.T,
        jnp.stack([pack[:BLOCK, k * hid : (k + 1) * hid] for k in range(3)]),
        pack[:BLOCK, 3 * hid :].T,
        second[: short[1]].T,
        third[: short[2]].T,
    )


def solution(mesh):
    placed = (
        P("dp", "mp"),
        P(),
        P(None, "mp"),
        P("mp", None),
        P(None, None, "mp"),
        P("mp", None),
        P("mp", None),
        P("mp", None),
        P("dp", None),
        P("dp", None),
        P("dp", None),
        P(("dp", "mp"), None),
        P(("dp", "mp"), None),
    )
    return jax.shard_map(
        body,
        mesh=mesh,
        in_specs=placed,
        out_specs=(
            P("dp", "mp"),
            P("dp", "mp"),
            P("mp", "dp"),
            P(None, "dp", "mp"),
            P("mp", "dp"),
            P("mp", "dp"),
            P("mp", "dp"),
        ),
        check_vma=False,
    )
```

```python
import functools
import math

import jax
import jax.numpy as jnp
from jax import lax
from jax.experimental import pallas as pl
from jax.experimental.pallas import tpu as pltpu
from jax.sharding import PartitionSpec as P

F32 = jnp.float32
BF16 = jnp.bfloat16
VMEM_LIMIT = 20 * 1024 * 1024
PACK_ORDER = (1, 8, 2, 4)
OUT_ORDER = (1, 8, 2, 4)
IN_ORDER = (8, 1, 2, 4)

CORE = [(i, i ^ 1) for i in range(16)]
FAR = [(i, i ^ 8) for i in range(16)]
AROUND_Y = [[(i, (i & 9) | ((((i >> 1 & 3) + k) & 3) << 1)) for i in range(16)] for k in range(4)]

BLOCK = 96
TEACH = 256
PART = 128
EXTRA = 8
SUMS = 16
LOW = 48


def gelu(value):
    return 0.5 * value * (1.0 + lax.erf(value * 0.7071067811865476))


def gelu_slope(value):
    return (
        0.5 * (1.0 + lax.erf(value * 0.7071067811865476))
        + value * jnp.exp(-0.5 * value * value) * 0.3989422804014327
    )


def dot(left, right, over_left=1, over_right=0):
    return lax.dot_general(
        left, right, (((over_left,), (over_right,)), ((), ())), preferred_element_type=F32
    )


def pick(array, index, axis):
    return lax.dynamic_index_in_dim(array, index, axis, keepdims=False)


def put(buffer, piece, *at):
    return lax.dynamic_update_slice(buffer, piece, at + (0,) * (buffer.ndim - len(at)))


def mp_place():
    index = lax.axis_index("mp")
    return index >> 3, (index >> 1) & 3, index & 1


def spread(pair, through=None):
    y = mp_place()[1]
    arrived = [(k, lax.ppermute(pair, "mp", AROUND_Y[k])) for k in (1, 3, 2)]
    if through is not None:
        pair = through(pair)
    held = put(jnp.zeros((2, 4, *pair.shape[1:]), pair.dtype), pair[:, None], 0, y)
    for k, piece in arrived:
        held = put(held, piece[:, None], 0, (y - k) & 3)
    held = held.reshape(8, *pair.shape[1:])
    return held, lax.ppermute(held, "mp", CORE)


def collect(mine, theirs, through=None):
    y = mp_place()[1]
    other = lax.ppermute(theirs, "mp", CORE)
    held = (mine.astype(F32) + other.astype(F32)).astype(BF16).reshape(2, 4, *mine.shape[1:])
    arrived = [lax.ppermute(pick(held, (y + k) & 3, 1), "mp", AROUND_Y[k]) for k in (1, 3, 2)]
    own = pick(held, y, 1)
    if through is not None:
        own = through(own)
    total = own.astype(F32)
    for piece in arrived:
        total = total + piece.astype(F32)
    return total


def sum_pair(total, through=None):
    rounded = total.astype(BF16)
    other = lax.ppermute(rounded, "mp", FAR)
    if through is not None:
        rounded = through(rounded)
    return rounded.astype(F32) + other.astype(F32)


def sum_own(total):
    x_hi = mp_place()[0]
    other = lax.ppermute(pick(total, 1 - x_hi, 0).astype(BF16), "mp", FAR)
    return pick(total, x_hi, 0) + other.astype(F32)


def dp_bit(weight):
    return (lax.axis_index("dp") // weight) & 1


def swap_dp(weight, array):
    return lax.ppermute(array, "dp", [(i, i ^ weight) for i in range(16)])


def halve_dp(weight, total):
    on = dp_bit(weight)
    total = total.reshape(2, -1, *total.shape[1:])
    return pick(total, on, 0), swap_dp(weight, pick(total, 1 - on, 0).astype(BF16))


def finish_dp(order, total):
    low, high = order[2:]
    place = dp_bit(low) * 2 + dp_bit(high)
    rounded = total.astype(BF16)
    arrived = [
        swap_dp(weight, pick(rounded, place ^ flips, 0))
        for flips, weight in ((3, low | high), (2, low), (1, high))
    ]
    total = pick(total, place, 0)
    for piece in arrived:
        total = total + piece.astype(F32)
    return total


def scatter_dp(order, total):
    kept, other = halve_dp(order[1], total)
    return finish_dp(order, kept + other.astype(F32))


def gather_dp(block):
    index = lax.axis_index("dp")
    x_lo, z = index >> 3, index & 7
    held = block[None]
    for bit in (2, 1, 0):
        other = lax.ppermute(held, "dp", [(i, i ^ (1 << bit)) for i in range(16)])
        on = ((z >> bit) & 1) == 1
        held = jnp.stack([jnp.where(on, other, held), jnp.where(on, held, other)], axis=held.ndim - 2)
    other = lax.ppermute(held, "dp", FAR)
    on = x_lo == 1
    held = jnp.stack([jnp.where(on, other, held), jnp.where(on, held, other)])
    return held.reshape(16, *block.shape)


def rows(start, size):
    return pl.ds(pl.multiple_of(start, 16), size)


def place(core, i, own, size):
    return rows((2 * i + (core if own else 1 - core)) * size, size)


def call(kernel, outs, *args, scratch=(), after=()):
    spec = pl.BlockSpec(memory_space=pltpu.VMEM)
    specs = [pl.BlockSpec(memory_space=pltpu.SMEM)] + [spec] * (len(args) - 1)
    skip = len(after)
    if skip:
        inner = kernel
        kernel = lambda *refs: inner(*refs[skip:])
    size = sum(math.prod(a.shape) * a.dtype.itemsize for a in args)
    size += sum(math.prod(shape) * jnp.dtype(dtype).itemsize for shape, dtype in outs)
    return pl.pallas_call(
        kernel,
        out_shape=tuple(jax.ShapeDtypeStruct(shape, dtype) for shape, dtype in outs),
        in_specs=[pl.BlockSpec(memory_space=pl.ANY)] * skip + specs,
        out_specs=(spec,) * len(outs),
        scratch_shapes=list(scratch),
        compiler_params=pltpu.CompilerParams(vmem_limit_bytes=VMEM_LIMIT),
        cost_estimate=pl.CostEstimate(flops=0, bytes_accessed=size, transcendentals=0),
    )(*after, *args)


def flip(block):
    return block.astype(F32).T.astype(BF16)


def send_out(core, full_ref, mine_ref, theirs_ref, size):
    for i in range(8):
        mine_ref[i] = full_ref[place(core, i, True, size)].astype(BF16)
        theirs_ref[i] = full_ref[place(core, i, False, size)].astype(BF16)


def take_in(core, held_ref, other_ref, full_ref, size):
    for i in range(8):
        full_ref[place(core, i, True, size)] = held_ref[i]
        full_ref[place(core, i, False, size)] = other_ref[i]


def block_kernel(core_ref, held_ref, other_ref, gain_ref, w_in_ref, w_out_ref,
                 pre_ref, stat_ref, mine_ref, theirs_ref, z_ref, act_ref, full_ref):
    core = core_ref[0]
    width = z_ref.shape[0]
    total = jnp.zeros((1, z_ref.shape[1]), F32)
    for i in range(8):
        for ref in (held_ref, other_ref):
            total = total + jnp.sum(ref[i, :BLOCK].astype(F32), axis=0, keepdims=True)
    mean = total / width
    total = jnp.zeros_like(mean)
    for i in range(8):
        for ref in (held_ref, other_ref):
            centred = ref[i, :BLOCK].astype(F32) - mean
            total = total + jnp.sum(centred * centred, axis=0, keepdims=True)
    inv_std = 1.0 / jnp.sqrt(total / width + 1e-06)
    stat_ref[...] = jnp.zeros_like(stat_ref)
    stat_ref[0:1] = mean
    stat_ref[1:2] = inv_std
    for i in range(8):
        for own, ref in ((True, held_ref), (False, other_ref)):
            at = place(core, i, own, BLOCK)
            normed = (ref[i, :BLOCK].astype(F32) - mean) * inv_std
            z_ref[at] = (normed * gain_ref[at]).astype(BF16)
    hidden = pre_ref.shape[0]
    pre = jnp.zeros(pre_ref.shape, F32)
    for start in range(0, width, hidden):
        pre = pre + dot(flip(w_in_ref[start : start + hidden]), z_ref[start : start + hidden])
    pre_ref[...] = pre
    act_ref[...] = gelu(pre).astype(BF16)
    for start in range(0, width, hidden):
        full_ref[start : start + hidden] = dot(flip(w_out_ref[:, start : start + hidden]), act_ref[...])
    send_out(core, full_ref, mine_ref, theirs_ref, BLOCK)


def adaptor_kernel(core_ref, held_ref, other_ref, adapt_t_ref, heads_t_ref,
                   h_ref, pre_ref, q_ref, mine_a_ref, theirs_a_ref, mine_b_ref, theirs_b_ref):
    core = core_ref[0]
    take_in(core, held_ref, other_ref, h_ref, BLOCK)
    pre = dot(adapt_t_ref[...], h_ref[...])
    pre_ref[...] = pre
    q_ref[...] = gelu(pre).astype(BF16)
    for i in range(8):
        for own, a_ref, b_ref in ((True, mine_a_ref, mine_b_ref), (False, theirs_a_ref, theirs_b_ref)):
            pred = dot(heads_t_ref[place(core, i, own, TEACH)], q_ref[...]).astype(BF16)
            a_ref[i] = pred[:PART]
            b_ref[i] = pred[PART:]


def adaptor_back_kernel(core_ref, held_a_ref, other_a_ref, held_b_ref, other_b_ref, heads_ref, pre_ref, adapt_t_ref,
                        err_ref, back_ref, mine_ref, theirs_ref, full_ref):
    core = core_ref[0]
    for i in range(8):
        for own, refs in ((True, (held_a_ref, held_b_ref)), (False, (other_a_ref, other_b_ref))):
            start = (2 * i + (core if own else 1 - core)) * TEACH
            for part in range(2):
                err_ref[rows(start + part * PART, PART)] = refs[part][i]
    lifted = dot(heads_ref[...], err_ref[...])
    back_ref[...] = (lifted * gelu_slope(pre_ref[...])).astype(BF16)
    for start in range(0, full_ref.shape[0], 512):
        full_ref[start : start + 512] = dot(flip(adapt_t_ref[:, start : start + 512]), back_ref[...])
    send_out(core, full_ref, mine_ref, theirs_ref, BLOCK)


def adaptor_grads_kernel(scale, widths, on_ref, pair_ref, err_ref, q_ref, h_ref, back_ref,
                         pair_out_ref, mine_ref, theirs_ref, ga_ref, go_ref):
    pair_out_ref[...] = pair_ref[...]
    hid3 = q_ref.shape[0]
    hid = hid3 // 3
    ga_ref[...] = dot(h_ref[...], back_ref[...], 1, 1) * scale
    go_ref[...] = dot(err_ref[...], q_ref[...], 1, 1) * scale
    w0, w1, w2 = widths
    for j in range(8):
        for chunk, ref in sides(PACK_ORDER, on_ref[0], j, mine_ref, theirs_ref):
            at = rows(chunk * BLOCK, BLOCK)
            go = go_ref[rows(chunk * TEACH, TEACH)]
            ref[j, :BLOCK] = jnp.concatenate(
                [ga_ref[at], go[:BLOCK, :hid]], axis=1
            ).astype(BF16)
            second = go[w0 : w0 + w1, hid : 2 * hid]
            third = go[w0 + w1 : w0 + w1 + w2, 2 * hid :]
            second = jnp.concatenate([second, jnp.zeros((2 * LOW - w1, hid), F32)], axis=0)
            third = jnp.concatenate([third, jnp.zeros((2 * LOW - w2, hid), F32)], axis=0)
            ref[j, BLOCK:] = jnp.concatenate(
                [second[:LOW], third[:LOW], second[LOW:], third[LOW:]], axis=1
            ).astype(BF16)


def w_out_grad_kernel(scale, place_ref, ds_ref, act_ref, mine_ref, theirs_ref, full_ref):
    full_ref[...] = dot(ds_ref[...], act_ref[...], 1, 1) * scale
    halves(OUT_ORDER, place_ref[1], full_ref, mine_ref, theirs_ref)


def sides(order, on, j, mine_ref, theirs_ref):
    first, rest = order[0], order[1:]
    chunk = sum(weight * ((j >> (2 - i)) & 1) for i, weight in enumerate(rest))
    return ((on * first + chunk, mine_ref), ((1 - on) * first + chunk, theirs_ref))


def halves(order, on, full_ref, mine_ref, theirs_ref):
    for j in range(8):
        for chunk, ref in sides(order, on, j, mine_ref, theirs_ref):
            ref[j] = full_ref[rows(chunk * BLOCK, BLOCK)].astype(BF16)


def w_in_grad_kernel(scale, place_ref, z_ref, dpre_ref, mine_ref, theirs_ref, full_ref):
    full_ref[...] = dot(z_ref[...], dpre_ref[...], 1, 1) * scale
    halves(IN_ORDER, place_ref[2], full_ref, mine_ref, theirs_ref)


def block_back_kernel(core_ref, ds_held_ref, ds_other_ref, w_out_ref, pre_ref, w_in_ref, gain_ref,
                      held_ref, other_ref, stat_ref,
                      ds_ref, dpre_ref, z_ref, act_ref, mine_ref, theirs_ref, full_ref):
    core = core_ref[0]
    take_in(core, ds_held_ref, ds_other_ref, ds_ref, BLOCK)
    width = ds_ref.shape[0]
    act_ref[...] = gelu(pre_ref[...]).astype(BF16)
    dpre_ref[...] = (dot(w_out_ref[...], ds_ref[...]) * gelu_slope(pre_ref[...])).astype(BF16)
    full_ref[...] = dot(w_in_ref[...], dpre_ref[...])
    mean = stat_ref[0:1]
    inv_std = stat_ref[1:2]
    first = jnp.zeros_like(mean)
    second = jnp.zeros_like(mean)
    for i in range(8):
        for own, ref, out_ref in ((True, held_ref, mine_ref), (False, other_ref, theirs_ref)):
            at = place(core, i, own, BLOCK)
            dnorm = full_ref[at]
            out_ref[i, :BLOCK] = dnorm.astype(BF16)
            lifted = dnorm * gain_ref[at]
            normed = (ref[i, :BLOCK].astype(F32) - mean) * inv_std
            z_ref[at] = (normed * gain_ref[at]).astype(BF16)
            first = first + jnp.sum(lifted, axis=0, keepdims=True)
            second = second + jnp.sum(lifted * normed, axis=0, keepdims=True)
    sums = []
    for part in (first / width, second / width):
        high = part.astype(BF16).astype(F32)
        sums = sums + [high, part - high]
    sums = jnp.concatenate(sums + [jnp.zeros((SUMS - 4, mean.shape[1]), F32)], axis=0).astype(BF16)
    for i in range(8):
        mine_ref[i, BLOCK:] = sums
        theirs_ref[i, BLOCK:] = sums


def start_kernel(place_ref, tokens_ref, *refs):
    teach_refs, (pair_ref, block_ref) = refs[:3], refs[3:]
    pair_ref[...] = jnp.zeros_like(pair_ref)
    pair_ref[place_ref[0], :BLOCK] = tokens_ref[...]
    block_ref[...] = jnp.zeros_like(block_ref)
    for m in range(8):

        @pl.when(place_ref[1] == m)
        def _():
            for side in range(2):
                offset = side * TEACH
                for ref in teach_refs:
                    wide = ref.shape[1] // 16
                    start = (side * 8 + m) * wide
                    block_ref[:, offset : offset + wide] = ref[:, start : start + wide]
                    offset = offset + wide


def pass_kernel(_, first_ref, second_ref, first_out_ref, second_out_ref):
    first_out_ref[...] = first_ref[...]
    second_out_ref[...] = second_ref[...]


def heads_kernel(_, own_ref, *refs):
    head_refs, (own_out_ref, heads_ref, heads_t_ref) = refs[:3], refs[3:]
    own_out_ref[...] = own_ref[...]
    hid = heads_ref.shape[0] // 3
    heads_ref[...] = jnp.zeros_like(heads_ref)
    for m in range(16):
        offset = m * TEACH
        for k in range(3):
            wide = head_refs[k].shape[1] // 16
            heads_ref[k * hid : (k + 1) * hid, offset : offset + wide] = head_refs[k][:, m * wide : (m + 1) * wide]
            offset = offset + wide
        heads_t_ref[m * TEACH : (m + 1) * TEACH] = flip(heads_ref[:, m * TEACH : (m + 1) * TEACH])


def add_kernel(_, mine_ref, other_ref, total_ref):
    total_ref[...] = mine_ref[...].astype(F32) + other_ref[...].astype(F32)


def body(
    tokens,
    ln_gain,
    w_in,
    w_out,
    adapt_in,
    out_dino,
    out_siglip,
    out_sam,
    teach_dino,
    teach_siglip,
    teach_sam,
    src_dev,
    src_row,
):
    heads = (out_dino, out_siglip, out_sam)
    teachers = (teach_dino, teach_siglip, teach_sam)
    n_rows = tokens.shape[0]
    n_mp = lax.axis_size("mp")
    n_dp = lax.axis_size("dp")
    width = BLOCK * n_mp
    hidden = w_in.shape[1]
    hid = adapt_in.shape[2]
    share = n_rows // n_mp
    short = [head.shape[1] // n_mp for head in heads]
    spare = TEACH - sum(short)
    scale = 1.0 / math.sqrt(n_rows * n_dp)
    x_hi, y, core = mp_place()
    at = jnp.stack([core, dp_bit(OUT_ORDER[0]), dp_bit(IN_ORDER[0])]).astype(jnp.int32)
    gain = ln_gain[:, None]

    with jax.named_scope("tokens"):
        own_tokens = tokens.T
        far_tokens = lax.ppermute(own_tokens, "mp", FAR)
        token_pair, block = call(
            start_kernel,
            [((2, BLOCK + EXTRA, n_rows), BF16), ((teach_dino.shape[0], 2 * TEACH), BF16)],
            jnp.stack([x_hi, y * 2 + core]).astype(jnp.int32), own_tokens, *teachers,
        )
        sources = jnp.concatenate([src_dev, src_row], axis=1).T.astype(BF16)
        sources = jnp.pad(sources, ((0, EXTRA - 4), (0, n_rows - share)))
        token_pair = put(token_pair, far_tokens[None], 1 - x_hi)
        token_pair = put(token_pair, sources[None], x_hi, BLOCK)
        token_pair = put(token_pair, lax.ppermute(sources, "mp", FAR)[None], 1 - x_hi, BLOCK)
        x_held, x_other = spread(token_pair)

    more = []

    def more_weights(own):
        own, later = call(pass_kernel, [(own.shape, BF16), (block.shape, BF16)], at, own, block)
        own, *rest = call(
            heads_kernel,
            [
                (own.shape, BF16),
                ((3 * hid, n_mp * TEACH), BF16),
                ((n_mp * TEACH, 3 * hid), BF16),
            ],
            at, own, *heads,
        )
        more.extend((*rest, later))
        return own

    with jax.named_scope("block"):
        pre_mlp, stat, mine, theirs = call(
            block_kernel,
            [
                ((hidden, n_rows), F32),
                ((8, n_rows), F32),
                ((8, BLOCK, n_rows), BF16),
                ((8, BLOCK, n_rows), BF16),
            ],
            at, x_held, x_other, gain, w_in, w_out,
            scratch=[
                pltpu.VMEM((width, n_rows), BF16),
                pltpu.VMEM((hidden, n_rows), BF16),
                pltpu.VMEM((width, n_rows), F32),
            ],
        )
        state = sum_pair(collect(mine, theirs, more_weights)) + token_pair[:, :BLOCK].astype(F32)
        h_held, h_other = spread(state.astype(BF16))

    with jax.named_scope("targets"):
        heads_all, heads_t, block_later = more
        adapt_t = adapt_in.transpose(0, 2, 1).reshape(3 * hid, width)
        pool = gather_dp(block_later).reshape(-1, 2 * TEACH)
        mixed = [a[:, BLOCK : BLOCK + 4, :share] for a in (x_held, x_other)]
        mixed = jnp.stack(
            [jnp.where(core == 0, mixed[0], mixed[1]), jnp.where(core == 0, mixed[1], mixed[0])], axis=1
        )
        source = mixed.transpose(2, 0, 1, 3).reshape(4, n_rows).astype(jnp.int32)
        places = jnp.arange(pool.shape[0], dtype=jnp.int32)[:, None]
        spots = source[:1] * teach_dino.shape[0] + source[1:]
        target = []
        for side in range(2):
            offset = side * TEACH
            for k in range(3):
                chosen = (places == spots[k : k + 1]).astype(BF16)
                target.append(dot(pool[:, offset : offset + short[k]], chosen, 0, 0))
                offset = offset + short[k]
            target.append(jnp.zeros((spare, n_rows), F32))
        target = jnp.concatenate(target, axis=0).reshape(2, TEACH, n_rows).astype(BF16)

    with jax.named_scope("adaptors"):
        h, pre_adapt, q, *sent = call(
            adaptor_kernel,
            [
                ((width, n_rows), BF16),
                ((3 * hid, n_rows), F32),
                ((3 * hid, n_rows), BF16),
            ]
            + [((8, PART, n_rows), BF16)] * 4,
            at, h_held, h_other, adapt_t, heads_t,
        )
        errors = []
        for part in range(2):
            pred = sum_pair(collect(*sent[2 * part : 2 * part + 2]))
            error = pred - target[:, part * PART : (part + 1) * PART].astype(F32)
            errors.extend(spread(error.astype(BF16)))

    with jax.named_scope("adaptors_back"):
        err, back, mine, theirs = call(
            adaptor_back_kernel,
            [
                ((n_mp * TEACH, n_rows), BF16),
                ((3 * hid, n_rows), BF16),
                ((8, BLOCK, n_rows), BF16),
                ((8, BLOCK, n_rows), BF16),
            ],
            at, *errors, heads_all, pre_adapt, adapt_t,
            scratch=[pltpu.VMEM((width, n_rows), F32)],
        )
        packs = []

        def adaptor_grads(pair):
            pair, kept, sent = call(
                functools.partial(adaptor_grads_kernel, scale, short),
                [(pair.shape, BF16)] + [((8, BLOCK + LOW, 4 * hid), BF16)] * 2,
                dp_bit(PACK_ORDER[0])[None].astype(jnp.int32), pair, err, q, h, back,
                scratch=[
                    pltpu.VMEM((width, 3 * hid), F32),
                    pltpu.VMEM((n_mp * TEACH, 3 * hid), F32),
                ],
            )
            packs.extend((kept, swap_dp(PACK_ORDER[0], sent)))
            return pair

        dstate = sum_pair(collect(mine, theirs), adaptor_grads)
        d_held, d_other = spread(dstate.astype(BF16))

    with jax.named_scope("block_back"):
        ds, dpre, z, act, mine, theirs = call(
            block_back_kernel,
            [((width, n_rows), BF16), ((hidden, n_rows), BF16)] * 2
            + [((8, BLOCK + SUMS, n_rows), BF16)] * 2,
            at, d_held, d_other, w_out, pre_mlp, w_in, gain, x_held, x_other, stat,
            scratch=[pltpu.VMEM((width, n_rows), F32)],
        )
        ins = call(
            functools.partial(w_in_grad_kernel, scale),
            [((8, BLOCK, hidden), BF16)] * 2,
            at, z, dpre,
            scratch=[pltpu.VMEM((width, hidden), F32)],
        )
        outs = call(
            functools.partial(w_out_grad_kernel, scale),
            [((8, BLOCK, hidden), BF16)] * 2,
            at, ds, act,
            scratch=[pltpu.VMEM((width, hidden), F32)],
            after=(ins[0],),
        )
        def add(array, other, *after):
            return call(add_kernel, [(array.shape, F32)], at, array, other, after=after)[0]

        sums = []

        def first_sums(own):
            pack = add(*packs, own)
            sums.extend((pack, add(ins[0], swap_dp(IN_ORDER[0], ins[1]), own, pack)))
            return own

        partial = collect(mine, theirs, first_sums)
        in_quarter = add(*halve_dp(IN_ORDER[1], sums[1]))
        pack = finish_dp(PACK_ORDER, add(*halve_dp(PACK_ORDER[1], sums[0]), sums[1]))
        out_half = add(outs[0], swap_dp(OUT_ORDER[0], outs[1]), in_quarter)
        out_quarter = add(*halve_dp(OUT_ORDER[1], out_half), pack)
        summed = sum_own(partial)
        gain_own = lax.dynamic_slice_in_dim(ln_gain, lax.axis_index("mp") * BLOCK, BLOCK, 0)
        normed = (tokens.T.astype(F32) - stat[0:1]) * stat[1:2]
        dnorm = summed[:BLOCK] * gain_own[:, None]
        first = summed[BLOCK : BLOCK + 1] + summed[BLOCK + 1 : BLOCK + 2]
        second = summed[BLOCK + 2 : BLOCK + 3] + summed[BLOCK + 3 : BLOCK + 4]
        grad_tokens = pick(dstate, x_hi, 0) + stat[1:2] * (dnorm - first - normed * second)

    with jax.named_scope("weight_sums"):
        grad_w_in = finish_dp(IN_ORDER, in_quarter)
        grad_w_out = finish_dp(OUT_ORDER, out_quarter)

    tail = pack[BLOCK:]
    second = jnp.concatenate([tail[:, :hid], tail[:, 2 * hid : 3 * hid]], axis=0)
    third = jnp.concatenate([tail[:, hid : 2 * hid], tail[:, 3 * hid :]], axis=0)
    return (
        grad_tokens.T,
        grad_w_in,
        grad_w_out.T,
        jnp.stack([pack[:BLOCK, k * hid : (k + 1) * hid] for k in range(3)]),
        pack[:BLOCK, 3 * hid :].T,
        second[: short[1]].T,
        third[: short[2]].T,
    )


def solution(mesh):
    placed = (
        P("dp", "mp"),
        P(),
        P(None, "mp"),
        P("mp", None),
        P(None, None, "mp"),
        P("mp", None),
        P("mp", None),
        P("mp", None),
        P("dp", None),
        P("dp", None),
        P("dp", None),
        P(("dp", "mp"), None),
        P(("dp", "mp"), None),
    )
    return jax.shard_map(
        body,
        mesh=mesh,
        in_specs=placed,
        out_specs=(
            P("dp", "mp"),
            P("dp", "mp"),
            P("mp", "dp"),
            P(None, "dp", "mp"),
            P("mp", "dp"),
            P("mp", "dp"),
            P("mp", "dp"),
        ),
        check_vma=False,
    )
```
